128 devices in a mesh: fsdp: 32 (over x, y, z_hi), tp: 4 (over z_lo, core).
Axes of the slice: x: 4, y: 4, z: 4 (z_hi: 2, z_lo: 2; z = z_hi * 2 + z_lo), core: 2. Of those that a mesh axis runs over, the one named last changes fastest.
Arguments:
- tokens: bfloat16 [32, 1024, 1024], P('fsdp', 'tp'), may hold values from -6 to 6
- attention_gain: bfloat16 [1024], P('fsdp'), may hold values from 0.25 to 1.75
- query_weight: bfloat16 [1024, 2048], P('fsdp', 'tp'), may hold values from -0.1875 to 0.1875
- key_weight: bfloat16 [1024, 1024], P('fsdp', 'tp'), may hold values from -0.1875 to 0.1875
- value_weight: bfloat16 [1024, 1024], P('fsdp', 'tp'), may hold values from -0.1875 to 0.1875
- query_gain: bfloat16 [128], P('fsdp'), may hold values from 0.25 to 1.75
- key_gain: bfloat16 [128], P('fsdp'), may hold values from 0.25 to 1.75
- output_weight: bfloat16 [1024, 2048], P('fsdp', 'tp'), may hold values from -0.375 to 0.375
- feed_gain: bfloat16 [1024], P('fsdp'), may hold values from 0.25 to 1.75
- gate_weight: bfloat16 [1024, 3072], P('fsdp', 'tp'), may hold values from -0.1875 to 0.1875
- up_weight: bfloat16 [1024, 3072], P('fsdp', 'tp'), may hold values from -0.1875 to 0.1875
- down_weight: bfloat16 [1024, 3072], P('fsdp', 'tp'), may hold values from -0.109375 to 0.109375
- cotangent: bfloat16 [32, 1024, 1024], P('fsdp', 'tp'), may hold values from -6 to 6
Outputs:
- layer_output: bfloat16 [32, 1024, 1024], P('fsdp', 'tp')
- tokens_grad: float32 [32, 1024, 1024], P('fsdp', 'tp')
- attention_gain_grad: float32 [1024], P('fsdp')
- query_weight_grad: float32 [1024, 2048], P('fsdp', 'tp')
- key_weight_grad: float32 [1024, 1024], P('fsdp', 'tp')
- value_weight_grad: float32 [1024, 1024], P('fsdp', 'tp')
- query_gain_grad: float32 [128], P('fsdp')
- key_gain_grad: float32 [128], P('fsdp')
- output_weight_grad: float32 [1024, 2048], P('fsdp', 'tp')
- feed_gain_grad: float32 [1024], P('fsdp')
- gate_weight_grad: float32 [1024, 3072], P('fsdp', 'tp')
- up_weight_grad: float32 [1024, 3072], P('fsdp', 'tp')
- down_weight_grad: float32 [1024, 3072], P('fsdp', 'tp')
The draws below stay inside these ranges and needn't reach their ends.
All inputs are finite; a program needn't handle non-finite values.
Results may differ from the reference program's by a relative error of at most 0.017.
Values may be sent and summed in bfloat16 or wider, within the bound.
No kernel may reach another device: no remote copies, remote signals or barrier semaphores. Data moves between devices by JAX's collectives and lax.ppermute only.
A program may use at most 192 MiB of HBM per device.

```python
import math
import jax
import jax.numpy as jnp
from jax import lax

D = 1024
HQ = 16
HK = 8
HD = 128
FF = 3072
LEN = 1024
QBLOCK = 512
BATCH = 32


def block_scale(key, dims, shards, low, largest):
    gain = 1.0
    for position, parts in shards:
        steps = jax.random.uniform(jax.random.fold_in(jax.random.fold_in(key, 6), position), (parts,), jnp.float32, low / len(shards), largest / len(shards))
        gain = gain * jnp.repeat(jnp.exp(steps), dims[position] // parts).reshape((-1,) + (1,) * (len(dims) - 1 - position))
    return gain


def normal_values(rng, shape, width, limit, pieces=(), held_as=jnp.bfloat16):
    loudness = block_scale(rng, shape, pieces, -0.22, 0.18) if pieces else 1.0
    values = jax.random.normal(rng, shape, jnp.float32) * width * loudness
    return jnp.minimum(jnp.maximum(values, -limit), limit).astype(held_as)


def setup_inputs(seed: int = 0) -> dict:
    splits = jax.random.split(jax.random.key(seed), 14)
    return {
        "tokens": normal_values(splits[0], (BATCH, LEN, D), 1.0, 6.0, ((0, 32), (1, 4))),
        "attention_gain": jnp.clip(1.0 + 0.15 * jax.random.normal(splits[1], (D,), jnp.float32), 0.25, 1.75).astype(jnp.bfloat16),
        "query_weight": normal_values(splits[2], (D, HQ * HD), D ** -0.5, 0.1875, ((0, 32), (1, 4))),
        "key_weight": normal_values(splits[3], (D, HK * HD), D ** -0.5, 0.1875, ((0, 32), (1, 4))),
        "value_weight": normal_values(splits[4], (D, HK * HD), D ** -0.5, 0.1875, ((0, 32), (1, 4))),
        "query_gain": jnp.clip(1.0 + 0.15 * jax.random.normal(splits[5], (HD,), jnp.float32), 0.25, 1.75).astype(jnp.bfloat16),
        "key_gain": jnp.clip(1.0 + 0.15 * jax.random.normal(splits[6], (HD,), jnp.float32), 0.25, 1.75).astype(jnp.bfloat16),
        "output_weight": normal_values(splits[7], (D, HQ * HD), (HQ * HD // 8) ** -0.5, 0.375, ((0, 32), (1, 4))),
        "feed_gain": jnp.clip(1.0 + 0.15 * jax.random.normal(splits[8], (D,), jnp.float32), 0.25, 1.75).astype(jnp.bfloat16),
        "gate_weight": normal_values(splits[9], (D, FF), D ** -0.5, 0.1875, ((0, 32), (1, 4))),
        "up_weight": normal_values(splits[10], (D, FF), D ** -0.5, 0.1875, ((0, 32), (1, 4))),
        "down_weight": normal_values(splits[11], (D, FF), FF ** -0.5, 0.109375, ((0, 32), (1, 4))),
        "cotangent": normal_values(splits[12], (BATCH, LEN, D), 1.0, 6.0, ((0, 32), (1, 4))),
    }


epsilon = 1e-06
rope_base = 1000000.0
masked_score = -1e+30
precise = lax.Precision.HIGHEST

@jax.custom_vjp
def low(v):
    return lax.optimization_barrier(v.astype(jnp.bfloat16)).astype(jnp.float32)

@jax.custom_vjp
def low_back(v):
    return v

def low_keep(v):
    return (low(v), None)

def low_pass(kept, grad):
    return (grad,)

def back_keep(v):
    return (v, None)

def back_low(kept, grad):
    return (low(grad),)
low.defvjp(low_keep, low_pass)
low_back.defvjp(back_keep, back_low)

def rms_scale(values, gain_vector):
    inverse = lax.rsqrt(lax.optimization_barrier(jnp.mean(values * values, axis=-1, keepdims=True)) + epsilon)
    return values * inverse * gain_vector

def rotary_tables(length, head_size):
    midway = head_size // 2
    frequency = 1.0 / rope_base ** (jnp.arange(midway, dtype=jnp.float32) * 2.0 / head_size)
    angles = jnp.arange(length, dtype=jnp.float32)[:, None] * frequency[None, :]
    cosine_table = jnp.concatenate([jnp.cos(angles), jnp.cos(angles)], axis=1)[:, None, :]
    sine_table = jnp.concatenate([jnp.sin(angles), jnp.sin(angles)], axis=1)[:, None, :]
    return (cosine_table, sine_table)

def rotate(values, cosine_table, sine_table):
    midway = values.shape[-1] // 2
    turned = jnp.concatenate([-values[..., midway:], values[..., :midway]], axis=-1)
    return values * cosine_table + turned * sine_table

def attend_block(query_block, key_rows, value_rows, offset):
    score_scale = 1.0 / math.sqrt(HD)
    scores = low_back(jnp.einsum('qhd,khd->hqk', query_block, key_rows, precision=precise) * score_scale)
    query_positions = offset + jnp.arange(QBLOCK)
    allowed = jnp.arange(LEN)[None, :] <= query_positions[:, None]
    scores = jnp.where(allowed, scores, masked_score)
    log_total = jax.nn.logsumexp(scores, axis=-1, keepdims=True)
    weights_low = low(jnp.exp(scores - log_total))
    return jnp.einsum('hqk,khd->qhd', weights_low, value_rows, precision=precise)

def layer(stream, attention_gain, query_weight, key_weight, value_weight, query_gain, key_gain, output_weight, feed_gain, gate_weight, up_weight, down_weight):
    first_low = low(rms_scale(stream, attention_gain))
    queries_raw = low_back(jnp.dot(first_low, query_weight, precision=precise)).reshape(LEN, HQ, HD)
    keys_raw = low_back(jnp.dot(first_low, key_weight, precision=precise)).reshape(LEN, HK, HD)
    values_low = low(low_back(jnp.dot(first_low, value_weight, precision=precise))).reshape(LEN, HK, HD)
    cosine_table, sine_table = rotary_tables(LEN, HD)
    queries_low = low(rotate(rms_scale(queries_raw, query_gain), cosine_table, sine_table))
    keys_low = low(rotate(rms_scale(keys_raw, key_gain), cosine_table, sine_table))
    key_rows = jnp.repeat(keys_low, HQ // HK, axis=1)
    value_rows = jnp.repeat(values_low, HQ // HK, axis=1)
    query_blocks = queries_low.reshape(LEN // QBLOCK, QBLOCK, HQ, HD)
    offsets = jnp.arange(LEN // QBLOCK) * QBLOCK
    attended = lax.map(jax.checkpoint(lambda element: attend_block(element[0], key_rows, value_rows, element[1])), (query_blocks, offsets))
    attended_low = low(low_back(attended.reshape(LEN, HQ * HD)))
    middle = stream + low_back(jnp.dot(attended_low, output_weight.T, precision=precise))
    second_low = low(rms_scale(middle, feed_gain))
    gate_values = low_back(jnp.dot(second_low, gate_weight, precision=precise))
    up_values = low_back(jnp.dot(second_low, up_weight, precision=precise))
    hidden_low = low(jax.nn.silu(gate_values) * up_values)
    return middle + jnp.dot(hidden_low, down_weight.T, precision=precise)

def reference(tokens, attention_gain, query_weight, key_weight, value_weight, query_gain, key_gain, output_weight, feed_gain, gate_weight, up_weight, down_weight, cotangent):
    weights = (attention_gain.astype(jnp.float32), query_weight.astype(jnp.float32), key_weight.astype(jnp.float32), value_weight.astype(jnp.float32), query_gain.astype(jnp.float32), key_gain.astype(jnp.float32), output_weight.astype(jnp.float32), feed_gain.astype(jnp.float32), gate_weight.astype(jnp.float32), up_weight.astype(jnp.float32), down_weight.astype(jnp.float32))

    def one_sequence(running, element):
        outputs, pull = jax.vjp(layer, element[0].astype(jnp.float32), *weights)
        grads = pull(element[1].astype(jnp.float32))
        running = tuple((before + addition for before, addition in zip(running, grads[1:])))
        return (running, (outputs.astype(jnp.bfloat16), grads[0]))
    initial = tuple((jnp.zeros(weight.shape, jnp.float32) for weight in weights))
    totals, (layer_output, tokens_grad) = lax.scan(one_sequence, initial, (tokens, cotangent))
    return (layer_output, tokens_grad, totals[0], totals[1], totals[2], totals[3], totals[4], totals[5], totals[6], totals[7], totals[8], totals[9], totals[10])
```

```python
import math

import jax
import jax.numpy as jnp
from jax import lax
from jax.experimental import pallas as pl
from jax.experimental.pallas import tpu as pltpu
from jax.sharding import Mesh, PartitionSpec as P

HD = 128
ROWS = 256
GROUP = 2
epsilon = 1e-06
rope_base = 1000000.0
score_scale = 1.0 / math.sqrt(HD)
log2_scale = score_scale / math.log(2.0)
FSDP = ("x", "y", "zh")
EVERY = ("x", "y", "zh", "zl", "core")
f32 = jnp.float32
bf16 = jnp.bfloat16


def matmul(a, b):
    return lax.dot_general(a, b, (((1,), (0,)), ((), ())), preferred_element_type=f32)


def matmul_t(a, b):
    return lax.dot_general(a, b, (((1,), (1,)), ((), ())), preferred_element_type=f32)


def t_matmul(a, b):
    return lax.dot_general(a, b, (((0,), (0,)), ((), ())), preferred_element_type=f32)


def inverse_rms(values):
    return lax.rsqrt(jnp.mean(values * values, axis=-1, keepdims=True) + epsilon)


def norm_back(values, gain, upstream):
    inverse = inverse_rms(values)
    scaled = gain * upstream
    moment = jnp.mean(scaled * values, axis=-1, keepdims=True)
    grad = inverse * scaled - values * (inverse * inverse * inverse) * moment
    return grad, jnp.sum(upstream * values * inverse, axis=0, keepdims=True)


def params(**kw):
    return pltpu.CompilerParams(vmem_limit_bytes=56 * 1024 * 1024, **kw)


def cost(flops, nbytes, trans=0):
    return pl.CostEstimate(flops=int(flops), bytes_accessed=int(nbytes), transcendentals=int(trans))


def whole(shape, index=None):
    index = index or (0,) * len(shape)
    return pl.BlockSpec(shape, lambda i, *_: index)


def pick(which, pieces, target):
    for k, piece in enumerate(pieces):

        @pl.when(which == k)
        def _(piece=piece):
            target[...] = piece[...]


def forward_attention_kernel(place, *refs):
    tokens = refs[:4]
    gain, qgain, kgain, wqkv, wo, cos, sin = refs[4:11]
    first, qraw, kraw, low, att, totals, part = refs[11:18]
    rows, keys, values, acc = refs[18:]
    i = pl.program_id(0)
    pick(place[i], tokens, rows)
    x = rows[...].astype(f32)
    normed = (x * inverse_rms(x) * gain[...]).astype(bf16)
    first[...] = normed
    qkv = matmul(normed, wqkv[...])
    nq = qraw.shape[1]
    nk = kraw.shape[1]
    qraw[...] = qkv[:, :nq]
    kraw[...] = qkv[:, nq : nq + nk]
    here = pl.ds(i * ROWS, ROWS)
    c, s = cos[...], sin[...]

    def turned(v, g):
        n = v * inverse_rms(v) * g
        return (n * c + pltpu.roll(n, HD // 2, 1) * s).astype(bf16)

    for h in range(nk // HD):
        k_low = turned(qkv[:, nq + h * HD : nq + (h + 1) * HD], kgain[...])
        v_low = qkv[:, nq + nk + h * HD : nq + nk + (h + 1) * HD].astype(bf16)
        low[:, nq + h * HD : nq + (h + 1) * HD] = k_low
        low[:, nq + nk + h * HD : nq + nk + (h + 1) * HD] = v_low
        keys[h, here, :] = k_low
        values[h, here, :HD] = v_low
        values[h, here, HD:] = jnp.ones((ROWS, HD), bf16)
    mask_q = lax.broadcasted_iota(jnp.int32, (GROUP * ROWS, ROWS), 0) % ROWS
    mask_k = lax.broadcasted_iota(jnp.int32, (GROUP * ROWS, ROWS), 1)
    outs = []
    sums = []
    for h in range(nk // HD):
        qs = []
        for a in range(GROUP):
            col = (h * GROUP + a) * HD
            q_low = turned(qkv[:, col : col + HD], qgain[...])
            low[:, col : col + HD] = q_low
            qs.append(q_low)
        q2 = jnp.concatenate(qs, axis=0)
        scores = matmul_t(q2, keys[h, here, :])
        weights = jnp.where(mask_k <= mask_q, jnp.exp2(scores * log2_scale), 0.0)
        acc[...] = matmul(weights.astype(bf16), values[h, here, :])

        def step(j, _, h=h, q2=q2):
            there = pl.ds(pl.multiple_of(j * ROWS, ROWS), ROWS)
            scores = matmul_t(q2, keys[h, there, :])
            weights = jnp.exp2(scores * log2_scale).astype(bf16)
            acc[...] += matmul(weights, values[h, there, :])
            return 0

        lax.fori_loop(0, i, step, 0)
        total = acc[:, HD:]
        o = (acc[:, :HD] / total).astype(bf16)
        outs += [o[a * ROWS : (a + 1) * ROWS] for a in range(GROUP)]
        sums.append(jnp.log2(total).T[:1, :])
    totals[0] = jnp.concatenate(sums + [jnp.zeros((8 - len(sums), GROUP * ROWS), f32)], axis=0)
    together = jnp.concatenate(outs, axis=1)
    att[...] = together
    part[0] = matmul_t(together, wo[...]).astype(bf16)


def forward_attention(place, tokens, gain, qgain, kgain, weights, nq, nk, cos, sin):
    n, width = 4, tokens[0].shape[1]
    length = n * ROWS
    nqkv = nq + 2 * nk
    row = lambda cols: pl.BlockSpec((ROWS, cols), lambda i, p: (i, 0))
    out = [
        ((length, width), bf16, row(width)),
        ((length, nq), f32, row(nq)),
        ((length, nk), f32, row(nk)),
        ((length, nqkv), bf16, row(nqkv)),
        ((length, nq), bf16, row(nq)),
        ((n, 8, GROUP * ROWS), f32, pl.BlockSpec((1, 8, GROUP * ROWS), lambda i, p: (i, 0, 0))),
        ((n, ROWS, width), bf16, pl.BlockSpec((1, ROWS, width), lambda i, p: (p[i], 0, 0))),
    ]
    return pl.pallas_call(
        forward_attention_kernel,
        grid_spec=pltpu.PrefetchScalarGridSpec(
            num_scalar_prefetch=1,
            grid=(n,),
            in_specs=[
                *[whole((ROWS, width))] * 4,
                whole((1, width)),
                whole((1, HD)),
                whole((1, HD)),
                whole((width, nqkv)),
                whole((width, nq), (0, nqkv // nq)),
                row(HD),
                row(HD),
            ],
            out_specs=[o[2] for o in out],
            scratch_shapes=[
                pltpu.VMEM((ROWS, width), bf16),
                pltpu.VMEM((nk // HD, length, HD), bf16),
                pltpu.VMEM((nk // HD, length, 2 * HD), bf16),
                pltpu.VMEM((GROUP * ROWS, 2 * HD), f32),
            ],
        ),
        out_shape=[jax.ShapeDtypeStruct(o[0], o[1]) for o in out],
        compiler_params=params(),
        cost_estimate=cost(7e9, 16e6, 3e6),
        name="forward_attention",
    )(place, *tokens, gain, qgain, kgain, weights, weights, cos, sin)


def middle_kernel(tokens, mine, from_core, from_z, gain, middle, second):
    total = mine[...].astype(f32) + from_core[...].astype(f32) + from_z[...].astype(f32)
    v = tokens[...].astype(f32) + total
    middle[...] = v
    second[...] = (v * inverse_rms(v) * gain[...]).astype(bf16)


def middle_step(tokens, part, from_core, from_z, gain):
    width = tokens.shape[1]
    half = ROWS // 2
    row = pl.BlockSpec((half, width), lambda i: (i, 0))
    first = pl.BlockSpec((None, None, half, width), lambda i: (0, 0, i, 0))
    return pl.pallas_call(
        middle_kernel,
        grid=(2,),
        in_specs=[row, first, pl.BlockSpec((None, half, width), lambda i: (0, i, 0)), row, whole((1, width))],
        out_specs=[row, row],
        out_shape=[jax.ShapeDtypeStruct((ROWS, width), f32), jax.ShapeDtypeStruct((ROWS, width), bf16)],
        compiler_params=params(),
        cost_estimate=cost(2e6, 4e6),
        name="middle_step",
    )(tokens, part, from_core, from_z, gain)


def feed_kernel(*refs):
    second, grads = refs[:4], refs[4:8]
    wg, wu, wd = refs[8:11]
    hidden, grad_units, part = refs[11:14]
    rows_s, rows_g = refs[14:]
    i = pl.program_id(0)
    pick(i, second, rows_s)
    pick(i, grads, rows_g)
    s = rows_s[...]
    gate = matmul(s, wg[...])
    up = matmul(s, wu[...])
    sig = 1.0 / (1.0 + jnp.exp(-gate))
    swish = gate * sig
    hidden[...] = (swish * up).astype(bf16)
    gh = matmul(rows_g[...], wd[...])
    gg = (gh * up * sig * (1.0 + gate * (1.0 - sig))).astype(bf16)
    gu = (gh * swish).astype(bf16)
    units = wg.shape[1]
    grad_units[:, :units] = gg
    grad_units[:, units:] = gu
    part[0] = (matmul_t(gg, wg[...]) + matmul_t(gu, wu[...])).astype(bf16)


def feed_step(second, grads, weights, units):
    width = second[0].shape[1]
    length = 4 * ROWS
    row = lambda cols: pl.BlockSpec((ROWS, cols), lambda i: (i, 0))
    return pl.pallas_call(
        feed_kernel,
        grid=(4,),
        in_specs=[
            *[whole((ROWS, width))] * 8,
            whole((width, units)),
            whole((width, units), (0, 1)),
            whole((width, units), (0, 2)),
        ],
        out_specs=[row(units), row(2 * units), pl.BlockSpec((1, ROWS, width), lambda i: (i, 0, 0))],
        out_shape=[
            jax.ShapeDtypeStruct((length, units), bf16),
            jax.ShapeDtypeStruct((length, 2 * units), bf16),
            jax.ShapeDtypeStruct((4, ROWS, width), bf16),
        ],
        scratch_shapes=[pltpu.VMEM((ROWS, width), bf16)] * 2,
        compiler_params=params(),
        cost_estimate=cost(8e9, 16e6, 1e6),
        name="feed_step",
    )(*second, *grads, weights, weights, weights)


def feed_out_kernel(hidden, wd, part):
    part[0] = matmul_t(hidden[...], wd[...]).astype(bf16)


def feed_out(hidden, weights):
    length, units = hidden.shape
    width = weights.shape[0]
    return pl.pallas_call(
        feed_out_kernel,
        grid=(4,),
        in_specs=[pl.BlockSpec((ROWS, units), lambda i: (i, 0)), whole((width, units), (0, 2))],
        out_specs=pl.BlockSpec((1, ROWS, width), lambda i: (i, 0, 0)),
        out_shape=jax.ShapeDtypeStruct((4, ROWS, width), bf16),
        compiler_params=params(),
        cost_estimate=cost(1.6e9, 5e6),
        name="feed_out",
    )(hidden, weights)


def feed_weights_kernel(*refs):
    second, grads = refs[:4], refs[4:8]
    grad_units, hidden, out = refs[8:]
    wide = grad_units.shape[1]

    def over(pieces, other):
        total = None
        for k, piece in enumerate(pieces):
            term = t_matmul(piece[...], other[k * ROWS : (k + 1) * ROWS, :])
            total = term if total is None else total + term
        return total.astype(bf16)

    out[:, :wide] = over(second, grad_units)
    out[:, wide:] = over(grads, hidden)


def feed_weights(second, grads, grad_units, hidden):
    width = second[0].shape[1]
    length, wide = grad_units.shape
    units = hidden.shape[1]
    return pl.pallas_call(
        feed_weights_kernel,
        grid=(width // 256,),
        in_specs=[
            *[pl.BlockSpec((ROWS, 256), lambda i: (0, i))] * 8,
            whole((length, wide)),
            whole((length, units)),
        ],
        out_specs=pl.BlockSpec((256, wide + units), lambda i: (i, 0)),
        out_shape=jax.ShapeDtypeStruct((width, wide + units), bf16),
        compiler_params=params(),
        cost_estimate=cost(4.8e9, 14e6),
        name="feed_weights",
    )(*second, *grads, grad_units, hidden)


def middle_back_kernel(middle, mine, from_core, from_z, cotangent, gain, grad_middle, branch, gain_part):
    u = mine[...].astype(f32) + from_core[...].astype(f32) + from_z[...].astype(f32)
    grad, part = norm_back(middle[...], gain[...], u)
    grad = cotangent[...].astype(f32) + grad
    grad_middle[...] = grad
    branch[...] = grad.astype(bf16)

    @pl.when(pl.program_id(0) == 0)
    def _():
        gain_part[...] = jnp.zeros_like(gain_part)

    gain_part[:1, :] += part


def middle_back(middle, part, from_core, from_z, cotangent, gain):
    width = middle.shape[1]
    half = ROWS // 2
    row = pl.BlockSpec((half, width), lambda i: (i, 0))
    first = pl.BlockSpec((None, None, half, width), lambda i: (0, 0, i, 0))
    return pl.pallas_call(
        middle_back_kernel,
        grid=(2,),
        in_specs=[row, first, pl.BlockSpec((None, half, width), lambda i: (0, i, 0)), row, row, whole((1, width))],
        out_specs=[row, row, whole((8, width))],
        out_shape=[
            jax.ShapeDtypeStruct((ROWS, width), f32),
            jax.ShapeDtypeStruct((ROWS, width), bf16),
            jax.ShapeDtypeStruct((8, width), f32),
        ],
        compiler_params=params(),
        cost_estimate=cost(4e6, 5e6),
        name="middle_back",
    )(middle, part, from_core, from_z, cotangent, gain)


def backward_attention_kernel(place, *refs):
    branch = refs[:4]
    wqkv, wo, low, att, totals, qraw, kraw, cos, sin, qgain, kgain = refs[4:15]
    grads, part, branch_out, qpart, kpart = refs[15:20]
    rows, dk, dv, dq = refs[20:]
    step_id = pl.program_id(0)
    i = pl.num_programs(0) - 1 - step_id
    nq, nk = qraw.shape[1], kraw.shape[1]

    @pl.when(step_id == 0)
    def _():
        dk[...] = jnp.zeros_like(dk)
        dv[...] = jnp.zeros_like(dv)
        qpart[...] = jnp.zeros_like(qpart)
        kpart[...] = jnp.zeros_like(kpart)

    pick(place[i], branch, rows)
    b = rows[...]
    branch_out[...] = b
    grad_att = matmul(b, wo[...]).astype(bf16)
    here = pl.ds(pl.multiple_of(i * ROWS, ROWS), ROWS)
    c, s = cos[...], sin[...]
    mask_k = lax.broadcasted_iota(jnp.int32, (ROWS, GROUP * ROWS), 0)
    mask_q = lax.broadcasted_iota(jnp.int32, (ROWS, GROUP * ROWS), 1) % ROWS

    def unturned(w):
        return w * c - pltpu.roll(w, HD // 2, 1) * s

    for h in range(nk // HD):
        cols = [(h * GROUP + a) * HD for a in range(GROUP)]
        q2 = jnp.concatenate([low[here, col : col + HD] for col in cols], axis=0)
        g2 = jnp.concatenate([grad_att[:, col : col + HD] for col in cols], axis=0)
        o2 = jnp.concatenate([att[:, col : col + HD] for col in cols], axis=0)
        total = totals[0, h : h + 1, :]
        dot = jnp.sum((g2.astype(f32) * o2.astype(f32)).T, axis=0, keepdims=True)
        kcol = slice(nq + h * HD, nq + (h + 1) * HD)
        vcol = slice(nq + nk + h * HD, nq + nk + (h + 1) * HD)

        def block(there, masked, h=h, q2=q2, g2=g2, total=total, dot=dot, kcol=kcol, vcol=vcol):
            k = low[there, kcol]
            v = low[there, vcol]
            probs = jnp.exp2(matmul_t(k, q2) * log2_scale - total)
            if masked:
                probs = jnp.where(mask_k <= mask_q, probs, 0.0)
            grad_scores = (probs * (matmul_t(v, g2) - dot)).astype(bf16)
            dv[h, there, :] += matmul(probs.astype(bf16), g2)
            dk[h, there, :] += matmul(grad_scores, q2)
            return t_matmul(grad_scores, k)

        dq[...] = block(here, True)

        def step(j, _, block=block):
            dq[...] += block(pl.ds(pl.multiple_of(j * ROWS, ROWS), ROWS), False)
            return 0

        lax.fori_loop(0, i, step, 0)
        for a, col in enumerate(cols):
            w = unturned(dq[a * ROWS : (a + 1) * ROWS, :] * score_scale)
            grad, gp = norm_back(qraw[:, col : col + HD], qgain[...], w)
            grads[:, col : col + HD] = grad.astype(bf16)
            qpart[:1, :] += gp
        w = unturned(dk[h, here, :] * score_scale)
        grad, gp = norm_back(kraw[:, h * HD : (h + 1) * HD], kgain[...], w)
        grads[:, kcol] = grad.astype(bf16)
        kpart[:1, :] += gp
        grads[:, vcol] = dv[h, here, :].astype(bf16)
    part[0] = matmul_t(grads[...], wqkv[...]).astype(bf16)


def backward_attention(place, branch, weights, low, att, totals, qraw, kraw, cos, sin, qgain, kgain):
    n, width = 4, branch[0].shape[1]
    length, nqkv = low.shape
    nq, nk = qraw.shape[1], kraw.shape[1]
    row = lambda cols: pl.BlockSpec((ROWS, cols), lambda i, p: (n - 1 - i, 0))
    out = [
        ((length, nqkv), bf16, row(nqkv)),
        ((n, ROWS, width), bf16, pl.BlockSpec((1, ROWS, width), lambda i, p: (p[n - 1 - i], 0, 0))),
        ((length, width), bf16, row(width)),
        ((8, HD), f32, whole((8, HD))),
        ((8, HD), f32, whole((8, HD))),
    ]
    return pl.pallas_call(
        backward_attention_kernel,
        grid_spec=pltpu.PrefetchScalarGridSpec(
            num_scalar_prefetch=1,
            grid=(n,),
            in_specs=[
                *[whole((ROWS, width))] * 4,
                whole((width, nqkv)),
                whole((width, nq), (0, nqkv // nq)),
                whole((length, nqkv)),
                row(nq),
                pl.BlockSpec((1, 8, GROUP * ROWS), lambda i, p: (n - 1 - i, 0, 0)),
                row(nq),
                row(nk),
                row(HD),
                row(HD),
                whole((1, HD)),
                whole((1, HD)),
            ],
            out_specs=[o[2] for o in out],
            scratch_shapes=[
                pltpu.VMEM((ROWS, width), bf16),
                pltpu.VMEM((nk // HD, length, HD), f32),
                pltpu.VMEM((nk // HD, length, HD), f32),
                pltpu.VMEM((GROUP * ROWS, HD), f32),
            ],
        ),
        out_shape=[jax.ShapeDtypeStruct(o[0], o[1]) for o in out],
        compiler_params=params(),
        cost_estimate=cost(9e9, 18e6, 3e6),
        name="backward_attention",
    )(place, *branch, weights, weights, low, att, totals, qraw, kraw, cos, sin, qgain, kgain)


def projection_weights_kernel(first, branch, grads, att, out):
    wide = grads.shape[1]
    out[:, :wide] = t_matmul(first[...], grads[...]).astype(bf16)
    out[:, wide:] = t_matmul(branch[...], att[...]).astype(bf16)


def projection_weights(first, branch, grads, att):
    length, width = first.shape
    wide, nq = grads.shape[1], att.shape[1]
    return pl.pallas_call(
        projection_weights_kernel,
        grid=(width // 256,),
        in_specs=[
            pl.BlockSpec((length, 256), lambda i: (0, i)),
            pl.BlockSpec((length, 256), lambda i: (0, i)),
            whole((length, wide)),
            whole((length, nq)),
        ],
        out_specs=pl.BlockSpec((256, wide + nq), lambda i: (i, 0)),
        out_shape=jax.ShapeDtypeStruct((width, wide + nq), bf16),
        compiler_params=params(),
        cost_estimate=cost(3.2e9, 10e6),
        name="projection_weights",
    )(first, branch, grads, att)


def tokens_back_kernel(tokens, mine, from_core, from_z, grad_middle, gain, grad_tokens, gain_part):
    u = mine[...].astype(f32) + from_core[...].astype(f32) + from_z[...].astype(f32)
    grad, part = norm_back(tokens[...].astype(f32), gain[...], u)
    grad_tokens[...] = grad_middle[...] + grad

    @pl.when(pl.program_id(0) == 0)
    def _():
        gain_part[...] = jnp.zeros_like(gain_part)

    gain_part[:1, :] += part


def tokens_back(tokens, part, from_core, from_z, grad_middle, gain):
    width = tokens.shape[1]
    half = ROWS // 2
    row = pl.BlockSpec((half, width), lambda i: (i, 0))
    first = pl.BlockSpec((None, None, half, width), lambda i: (0, 0, i, 0))
    return pl.pallas_call(
        tokens_back_kernel,
        grid=(2,),
        in_specs=[row, first, pl.BlockSpec((None, half, width), lambda i: (0, i, 0)), row, row, whole((1, width))],
        out_specs=[row, whole((8, width))],
        out_shape=[
            jax.ShapeDtypeStruct((ROWS, width), f32),
            jax.ShapeDtypeStruct((8, width), f32),
        ],
        compiler_params=params(),
        cost_estimate=cost(4e6, 4e6),
        name="tokens_back",
    )(tokens, part, from_core, from_z, grad_middle, gain)


def swapped(value, axis):
    return lax.ppermute(value, axis, [(0, 1), (1, 0)])


def tp_gather(own):
    over_z = swapped(own, "zl")
    return [own, over_z, swapped(own, "core"), swapped(over_z, "core")]


def tp_scatter(part):
    part = part.reshape(2, 2, *part.shape[1:])
    from_core = swapped(part[1], "core")
    passed = (part[0, 1].astype(f32) + from_core[1].astype(f32)).astype(bf16)
    return part, from_core, swapped(passed, "zl")


def from_everyone(shard, axes):
    copies = jnp.broadcast_to(shard, (lax.axis_size(axes), *shard.shape))
    return lax.all_to_all(copies, axes, split_axis=0, concat_axis=0, tiled=True)


def summed_rows(part):
    count = lax.axis_size(FSDP)
    blocks = part.reshape(count, part.shape[0] // count, part.shape[1])
    parts = lax.all_to_all(blocks, FSDP, 0, 0, tiled=True)
    return jnp.sum(parts.astype(f32), axis=0)


def rotary_tables(length):
    midway = HD // 2
    frequency = 1.0 / rope_base ** (jnp.arange(midway, dtype=f32) * 2.0 / HD)
    angles = jnp.arange(length, dtype=f32)[:, None] * frequency[None, :]
    cos, sin = jnp.cos(angles), jnp.sin(angles)
    return jnp.concatenate([cos, cos], axis=1), jnp.concatenate([-sin, sin], axis=1)


def local(
    tokens,
    attention_gain,
    query_weight,
    key_weight,
    value_weight,
    query_gain,
    key_gain,
    output_weight,
    feed_gain,
    gate_weight,
    up_weight,
    down_weight,
    cotangent,
):
    count = lax.axis_size(FSDP)
    width = tokens.shape[2]
    nq, nk = query_weight.shape[1], key_weight.shape[1]
    units = gate_weight.shape[1]
    rows = query_weight.shape[0]
    x = tokens[0]
    dy = cotangent[0]
    zl, core = lax.axis_index("zl"), lax.axis_index("core")
    block = jnp.arange(4, dtype=jnp.int32)
    place = ((block % 2) ^ core) * 2 + ((block // 2) ^ zl)
    place = place.astype(jnp.int32)
    cos, sin = rotary_tables(4 * ROWS)

    gains = jnp.concatenate([attention_gain, feed_gain, query_gain, key_gain])
    gains = jnp.pad(gains, (0, -gains.shape[0] % 128))[None]
    gains = from_everyone(gains, FSDP)[:, 0].astype(f32)
    heads = query_gain.shape[0]
    first_gain = gains[:, :rows].reshape(1, width)
    second_gain = gains[:, rows : 2 * rows].reshape(1, width)
    qgain = gains[:, 2 * rows : 2 * rows + heads].reshape(1, HD)
    kgain = gains[:, 2 * rows + heads : 2 * rows + 2 * heads].reshape(1, HD)

    weights = jnp.concatenate([query_weight, key_weight, value_weight, output_weight], axis=1)
    weights = from_everyone(weights, FSDP).reshape(width, -1)
    feed = jnp.concatenate([gate_weight, up_weight, down_weight], axis=1)
    feed = lax.all_gather(feed, FSDP, axis=0, tiled=True)

    token_blocks = tp_gather(x)
    grad_blocks = tp_gather(dy)

    first, qraw, kraw, low, att, totals, part = forward_attention(
        place, token_blocks, first_gain, qgain, kgain, weights, nq, nk, cos, sin
    )
    middle, second = middle_step(x, *tp_scatter(part), second_gain)
    second_blocks = tp_gather(second)
    hidden, grad_units, part = feed_step(second_blocks, grad_blocks, feed, units)
    grad_middle, branch, feed_gain_part = middle_back(middle, *tp_scatter(part), dy, second_gain)
    feed_sums = summed_rows(feed_weights(second_blocks, grad_blocks, grad_units, hidden))

    mine, from_core, from_z = tp_scatter(feed_out(hidden, feed))
    output = middle + mine[0, 0].astype(f32) + from_core[0].astype(f32) + from_z.astype(f32)
    output = output.astype(bf16)

    branch_blocks = tp_gather(branch)
    grads, part, branch_rows, qpart, kpart = backward_attention(
        place, branch_blocks, weights, low, att, totals, qraw, kraw, cos, sin, qgain, kgain
    )
    sums = summed_rows(projection_weights(first, branch_rows, grads, att))
    tokens_grad, first_gain_part = tokens_back(x, *tp_scatter(part), grad_middle, first_gain)

    gain_parts = jnp.concatenate(
        [
            first_gain_part[0].reshape(count, rows),
            feed_gain_part[0].reshape(count, rows),
            qpart[0].reshape(count, heads),
            kpart[0].reshape(count, heads),
        ],
        axis=1,
    )
    gain_parts = jnp.pad(gain_parts, ((0, 0), (0, -gain_parts.shape[1] % 128)))
    gain_parts = jnp.repeat(gain_parts, 4, axis=0)[:, None, :]
    gain_sums = jnp.sum(lax.all_to_all(gain_parts, EVERY, 0, 0, tiled=True), axis=(0, 1))

    return (
        output[None],
        tokens_grad[None],
        gain_sums[:rows],
        sums[:, :nq],
        sums[:, nq : nq + nk],
        sums[:, nq + nk : nq + 2 * nk],
        gain_sums[2 * rows : 2 * rows + heads],
        gain_sums[2 * rows + heads : 2 * rows + 2 * heads],
        sums[:, nq + 2 * nk :],
        gain_sums[rows : 2 * rows],
        feed_sums[:, :units],
        feed_sums[:, units : 2 * units],
        feed_sums[:, 2 * units :],
    )


def solution(mesh):
    fsdp, tp = mesh.devices.shape
    cut = {32: (4, 4, 2), 2: (1, 1, 2), 1: (1, 1, 1)}[fsdp]
    fine = Mesh(mesh.devices.reshape(*cut, 2, tp // 2), EVERY)
    split = ("zl", "core")
    data = P(FSDP, split, None)
    matrix = P(FSDP, split)
    vector = P(FSDP)
    return jax.shard_map(
        local,
        mesh=fine,
        in_specs=(
            data, vector, matrix, matrix, matrix, vector, vector,
            matrix, vector, matrix, matrix, matrix, data,
        ),
        out_specs=(
            data, data, vector, matrix, matrix, matrix, vector, vector,
            matrix, vector, matrix, matrix, matrix,
        ),
        check_vma=False,
    )
```

```python
import functools
import math

import jax
import jax.numpy as jnp
from jax import lax
from jax.experimental import pallas as pl
from jax.experimental.pallas import tpu as pltpu
from jax.sharding import Mesh, PartitionSpec as P

HD = 128
ROWS = 256
WIDTH = 1024
GROUP = 2
epsilon = 1e-06
rope_base = 1000000.0
score_scale = 1.0 / math.sqrt(HD)
log2_scale = score_scale / math.log(2.0)
FSDP = ("x", "y", "zh")
EVERY = ("x", "y", "zh", "zl", "core")
f32 = jnp.float32
bf16 = jnp.bfloat16


def matmul(a, b):
    return lax.dot_general(a, b, (((1,), (0,)), ((), ())), preferred_element_type=f32)


def matmul_t(a, b):
    return lax.dot_general(a, b, (((1,), (1,)), ((), ())), preferred_element_type=f32)


def t_matmul(a, b):
    return lax.dot_general(a, b, (((0,), (0,)), ((), ())), preferred_element_type=f32)


def inverse_rms(values):
    return lax.rsqrt(jnp.mean(values * values, axis=-1, keepdims=True) + epsilon)


def norm_back(values, gain, upstream):
    inverse = inverse_rms(values)
    scaled = gain * upstream
    moment = jnp.mean(scaled * values, axis=-1, keepdims=True)
    grad = inverse * scaled - values * (inverse * inverse * inverse) * moment
    return grad, jnp.sum(upstream * values * inverse, axis=0, keepdims=True)


def params(**kw):
    return pltpu.CompilerParams(vmem_limit_bytes=56 * 1024 * 1024, **kw)


def cost(flops, nbytes, trans=0):
    return pl.CostEstimate(flops=int(flops / 8), bytes_accessed=int(nbytes / 8), transcendentals=int(trans / 8))


def whole(shape, index=None):
    index = index or (0,) * len(shape)
    return pl.BlockSpec(shape, lambda i, *_: index)


def halves(width):
    return [
        pl.BlockSpec((1, ROWS, width), lambda i: (jnp.minimum(i, 1), 0, 0)),
        pl.BlockSpec((1, ROWS, width), lambda i: (jnp.maximum(i - 2, 0), 0, 0)),
    ]


def pick(which, pieces, target):
    for k, piece in enumerate(pieces):

        @pl.when(which == k)
        def _(piece=piece):
            target[...] = piece[...]


def equal_iota(rows, cols, make):
    r = lax.broadcasted_iota(jnp.int32, (rows, cols), 0)
    c = lax.broadcasted_iota(jnp.int32, (rows, cols), 1)
    return make(r, c)


def row_of(columns, k):
    same = equal_iota(128, 128, lambda r, c: r == c)
    parts = []
    for m in range(columns.shape[0] // 128):
        col = columns[m * 128 : (m + 1) * 128, k : k + 1].astype(f32)
        parts.append(jnp.sum(jnp.where(same, col, 0.0), axis=0, keepdims=True))
    return jnp.concatenate(parts, axis=1)


def of_head(rows, per_device, first_row=0):
    held = HD * per_device // WIDTH
    return equal_iota(
        rows, HD, lambda r, c: ((r + first_row) // per_device * held + (r + first_row) % per_device == c)
        & ((r + first_row) % per_device < held)
    )


def heads_of(columns, k, per_device):
    col = columns[:, k : k + 1].astype(f32)
    return jnp.sum(jnp.where(of_head(columns.shape[0], per_device), col, 0.0), axis=0, keepdims=True)


def put(which, value, mine, other):
    @pl.when(which < 2)
    def _():
        mine[0] = value

    @pl.when(which >= 2)
    def _():
        other[0] = value


def forward_attention_kernel(per_device, place, *refs):
    tokens = refs[:4]
    columns, wqkv, wo, cos, sin = refs[4:9]
    first, qraw, kraw, low, att, totals, mine, other, gains, head_gains = refs[9:19]
    rows, keys, values, acc = refs[19:]
    i = pl.program_id(0)

    @pl.when(i == 0)
    def _():
        gains[:2, :] = jnp.concatenate([row_of(columns, 0), row_of(columns, 1)], axis=0)
        gains[2:, :] = jnp.zeros_like(gains[2:, :])
        head_gains[:2, :] = jnp.concatenate([heads_of(columns, k, per_device) for k in (2, 3)], axis=0)
        head_gains[2:, :] = jnp.zeros_like(head_gains[2:, :])

    gain, qgain, kgain = gains[:1, :], head_gains[:1, :], head_gains[1:2, :]
    pick(place[i], tokens, rows)
    x = rows[...].astype(f32)
    normed = (x * inverse_rms(x) * gain).astype(bf16)
    first[...] = normed
    qkv = matmul(normed, wqkv[...])
    nq = qraw.shape[1]
    nk = kraw.shape[1]
    qraw[...] = qkv[:, :nq]
    kraw[...] = qkv[:, nq : nq + nk]
    here = pl.ds(i * ROWS, ROWS)
    c, s = cos[...], sin[...]

    def turned(v, g):
        n = v * inverse_rms(v) * g
        return (n * c + pltpu.roll(n, HD // 2, 1) * s).astype(bf16)

    for h in range(nk // HD):
        k_low = turned(qkv[:, nq + h * HD : nq + (h + 1) * HD], kgain)
        v_low = qkv[:, nq + nk + h * HD : nq + nk + (h + 1) * HD].astype(bf16)
        low[:, nq + h * HD : nq + (h + 1) * HD] = k_low
        low[:, nq + nk + h * HD : nq + nk + (h + 1) * HD] = v_low
        keys[h, here, :] = k_low
        values[h, here, :HD] = v_low
        values[h, here, HD:] = jnp.ones((ROWS, HD), bf16)
    mask_q = lax.broadcasted_iota(jnp.int32, (GROUP * ROWS, ROWS), 0) % ROWS
    mask_k = lax.broadcasted_iota(jnp.int32, (GROUP * ROWS, ROWS), 1)
    outs = []
    sums = []
    for h in range(nk // HD):
        qs = []
        for a in range(GROUP):
            col = (h * GROUP + a) * HD
            q_low = turned(qkv[:, col : col + HD], qgain)
            low[:, col : col + HD] = q_low
            qs.append(q_low)
        q2 = jnp.concatenate(qs, axis=0)
        scores = matmul_t(q2, keys[h, here, :])
        weights = jnp.where(mask_k <= mask_q, jnp.exp2(scores * log2_scale), 0.0)
        acc[...] = matmul(weights.astype(bf16), values[h, here, :])

        def step(j, _, h=h, q2=q2):
            there = pl.ds(pl.multiple_of(j * ROWS, ROWS), ROWS)
            scores = matmul_t(q2, keys[h, there, :])
            weights = jnp.exp2(scores * log2_scale).astype(bf16)
            acc[...] += matmul(weights, values[h, there, :])
            return 0

        lax.fori_loop(0, i, step, 0)
        total = acc[:, HD:]
        o = (acc[:, :HD] / total).astype(bf16)
        outs += [o[a * ROWS : (a + 1) * ROWS] for a in range(GROUP)]
        sums.append(jnp.log2(total).T[:1, :])
    totals[0] = jnp.concatenate(sums + [jnp.zeros((8 - len(sums), GROUP * ROWS), f32)], axis=0)
    together = jnp.concatenate(outs, axis=1)
    att[...] = together
    put(place[i], matmul_t(together, wo[...]).astype(bf16), mine, other)


def forward_attention(place, tokens, weights, nq, nk, cos, sin):
    n, width = 4, tokens[0].shape[1]
    length = n * ROWS
    nqkv = nq + 2 * nk
    row = lambda cols: pl.BlockSpec((ROWS, cols), lambda i, p: (i, 0))
    out = [
        ((length, width), bf16, row(width)),
        ((length, nq), f32, row(nq)),
        ((length, nk), f32, row(nk)),
        ((length, nqkv), bf16, row(nqkv)),
        ((length, nq), bf16, row(nq)),
        ((n, 8, GROUP * ROWS), f32, pl.BlockSpec((1, 8, GROUP * ROWS), lambda i, p: (i, 0, 0))),
        *[((2, ROWS, width), bf16, pl.BlockSpec((1, ROWS, width), lambda i, p: (p[i] % 2, 0, 0)))] * 2,
        ((8, width), f32, whole((8, width))),
        ((8, HD), f32, whole((8, HD))),
    ]
    return pl.pallas_call(
        functools.partial(forward_attention_kernel, width // lax.axis_size(FSDP)),
        grid_spec=pltpu.PrefetchScalarGridSpec(
            num_scalar_prefetch=1,
            grid=(n,),
            in_specs=[
                *[whole((ROWS, width))] * 4,
                whole((width, HD), (0, (nqkv + nq) // HD)),
                whole((width, nqkv)),
                whole((width, nq), (0, nqkv // nq)),
                row(HD),
                row(HD),
            ],
            out_specs=[o[2] for o in out],
            scratch_shapes=[
                pltpu.VMEM((ROWS, width), bf16),
                pltpu.VMEM((nk // HD, length, HD), bf16),
                pltpu.VMEM((nk // HD, length, 2 * HD), bf16),
                pltpu.VMEM((GROUP * ROWS, 2 * HD), f32),
            ],
        ),
        out_shape=[jax.ShapeDtypeStruct(o[0], o[1]) for o in out],
        compiler_params=params(),
        cost_estimate=cost(7e9, 16e6, 3e6),
        name="forward_attention",
    )(place, *tokens, weights, weights, weights, cos, sin)


def middle_kernel(tokens, mine, from_core, from_z, gain, middle, second):
    total = mine[...].astype(f32) + from_core[...].astype(f32) + from_z[...].astype(f32)
    v = tokens[...].astype(f32) + total
    middle[...] = v
    second[...] = (v * inverse_rms(v) * gain[1:2, :]).astype(bf16)


def middle_step(tokens, part, from_core, from_z, gain):
    width = tokens.shape[1]
    half = ROWS // 2
    row = pl.BlockSpec((half, width), lambda i: (i, 0))
    first = pl.BlockSpec((None, half, width), lambda i: (0, i, 0))
    return pl.pallas_call(
        middle_kernel,
        grid=(2,),
        in_specs=[row, first, first, row, whole((8, width))],
        out_specs=[row, row],
        out_shape=[jax.ShapeDtypeStruct((ROWS, width), f32), jax.ShapeDtypeStruct((ROWS, width), bf16)],
        compiler_params=params(),
        cost_estimate=cost(2e6, 4e6),
        name="middle_step",
    )(tokens, part, from_core, from_z, gain)


def feed_kernel(*refs):
    second, grads = refs[:4], refs[4:8]
    wg, wu, wd = refs[8:11]
    hidden, grad_units, mine, other = refs[11:15]
    rows_s, rows_g = refs[15:]
    i = pl.program_id(0)
    pick(i, second, rows_s)
    pick(i, grads, rows_g)
    s = rows_s[...]
    gate = matmul(s, wg[...])
    up = matmul(s, wu[...])
    sig = 1.0 / (1.0 + jnp.exp(-gate))
    swish = gate * sig
    hidden[...] = (swish * up).astype(bf16)
    gh = matmul(rows_g[...], wd[...])
    gg = (gh * up * sig * (1.0 + gate * (1.0 - sig))).astype(bf16)
    gu = (gh * swish).astype(bf16)
    units = wg.shape[1]
    grad_units[:, :units] = gg
    grad_units[:, units:] = gu
    put(i, (matmul_t(gg, wg[...]) + matmul_t(gu, wu[...])).astype(bf16), mine, other)


def feed_step(second, grads, weights, units):
    width = second[0].shape[1]
    length = 4 * ROWS
    row = lambda cols: pl.BlockSpec((ROWS, cols), lambda i: (i, 0))
    return pl.pallas_call(
        feed_kernel,
        grid=(4,),
        in_specs=[
            *[whole((ROWS, width))] * 8,
            whole((width, units)),
            whole((width, units), (0, 1)),
            whole((width, units), (0, 2)),
        ],
        out_specs=[row(units), row(2 * units), *halves(width)],
        out_shape=[
            jax.ShapeDtypeStruct((length, units), bf16),
            jax.ShapeDtypeStruct((length, 2 * units), bf16),
            *[jax.ShapeDtypeStruct((2, ROWS, width), bf16)] * 2,
        ],
        scratch_shapes=[pltpu.VMEM((ROWS, width), bf16)] * 2,
        compiler_params=params(),
        cost_estimate=cost(8e9, 16e6, 1e6),
        name="feed_step",
    )(*second, *grads, weights, weights, weights)


def feed_out_kernel(hidden, wd, mine, other):
    put(pl.program_id(0), matmul_t(hidden[...], wd[...]).astype(bf16), mine, other)


def feed_out(hidden, weights):
    length, units = hidden.shape
    width = weights.shape[0]
    return pl.pallas_call(
        feed_out_kernel,
        grid=(4,),
        in_specs=[pl.BlockSpec((ROWS, units), lambda i: (i, 0)), whole((width, units), (0, 2))],
        out_specs=halves(width),
        out_shape=[jax.ShapeDtypeStruct((2, ROWS, width), bf16)] * 2,
        compiler_params=params(),
        cost_estimate=cost(1.6e9, 5e6),
        name="feed_out",
    )(hidden, weights)


def feed_weights_kernel(*refs):
    second, grads = refs[:4], refs[4:8]
    grad_units, hidden, out = refs[8:]
    wide = grad_units.shape[1]

    def over(pieces, other):
        total = None
        for k, piece in enumerate(pieces):
            term = t_matmul(piece[...], other[k * ROWS : (k + 1) * ROWS, :])
            total = term if total is None else total + term
        return total.astype(bf16)

    out[:, :wide] = over(second, grad_units)
    out[:, wide:] = over(grads, hidden)


def feed_weights(second, grads, grad_units, hidden):
    width = second[0].shape[1]
    length, wide = grad_units.shape
    units = hidden.shape[1]
    return pl.pallas_call(
        feed_weights_kernel,
        grid=(width // 256,),
        in_specs=[
            *[pl.BlockSpec((ROWS, 256), lambda i: (0, i))] * 8,
            whole((length, wide)),
            whole((length, units)),
        ],
        out_specs=pl.BlockSpec((256, wide + units), lambda i: (i, 0)),
        out_shape=jax.ShapeDtypeStruct((width, wide + units), bf16),
        compiler_params=params(),
        cost_estimate=cost(4.8e9, 14e6),
        name="feed_weights",
    )(*second, *grads, grad_units, hidden)


def middle_back_kernel(middle, mine, from_core, from_z, cotangent, gain, grad_middle, branch, gain_part):
    u = mine[...].astype(f32) + from_core[...].astype(f32) + from_z[...].astype(f32)
    grad, part = norm_back(middle[...], gain[1:2, :], u)
    grad = cotangent[...].astype(f32) + grad
    grad_middle[...] = grad
    branch[...] = grad.astype(bf16)

    @pl.when(pl.program_id(0) == 0)
    def _():
        gain_part[...] = jnp.zeros_like(gain_part)

    gain_part[:1, :] += part


def middle_back(middle, part, from_core, from_z, cotangent, gain):
    width = middle.shape[1]
    half = ROWS // 2
    row = pl.BlockSpec((half, width), lambda i: (i, 0))
    first = pl.BlockSpec((None, half, width), lambda i: (0, i, 0))
    return pl.pallas_call(
        middle_back_kernel,
        grid=(2,),
        in_specs=[row, first, first, row, row, whole((8, width))],
        out_specs=[row, row, whole((8, width))],
        out_shape=[
            jax.ShapeDtypeStruct((ROWS, width), f32),
            jax.ShapeDtypeStruct((ROWS, width), bf16),
            jax.ShapeDtypeStruct((8, width), f32),
        ],
        compiler_params=params(),
        cost_estimate=cost(4e6, 5e6),
        name="middle_back",
    )(middle, part, from_core, from_z, cotangent, gain)


def backward_attention_kernel(place, *refs):
    branch = refs[:4]
    tokens = refs[4:8]
    wqkv, wo, low, att, totals, qraw, kraw, cos, sin, head_gains = refs[8:18]
    grads, mine, other, branch_out, gain_part, head_part = refs[18:24]
    rows, xs, dk, dv, dq = refs[24:]
    qgain, kgain = head_gains[:1, :], head_gains[1:2, :]
    step_id = pl.program_id(0)
    i = pl.num_programs(0) - 1 - step_id
    nq, nk = qraw.shape[1], kraw.shape[1]

    @pl.when(step_id == 0)
    def _():
        dk[...] = jnp.zeros_like(dk)
        dv[...] = jnp.zeros_like(dv)
        gain_part[...] = jnp.zeros_like(gain_part)
        head_part[...] = jnp.zeros_like(head_part)

    pick(place[i], branch, rows)
    pick(place[i], tokens, xs)
    b = rows[...]
    branch_out[...] = b
    grad_att = matmul(b, wo[...]).astype(bf16)
    here = pl.ds(pl.multiple_of(i * ROWS, ROWS), ROWS)
    c, s = cos[...], sin[...]
    mask_k = lax.broadcasted_iota(jnp.int32, (ROWS, GROUP * ROWS), 0)
    mask_q = lax.broadcasted_iota(jnp.int32, (ROWS, GROUP * ROWS), 1) % ROWS

    def unturned(w):
        return w * c - pltpu.roll(w, HD // 2, 1) * s

    for h in range(nk // HD):
        cols = [(h * GROUP + a) * HD for a in range(GROUP)]
        q2 = jnp.concatenate([low[here, col : col + HD] for col in cols], axis=0)
        g2 = jnp.concatenate([grad_att[:, col : col + HD] for col in cols], axis=0)
        o2 = jnp.concatenate([att[:, col : col + HD] for col in cols], axis=0)
        total = totals[0, h : h + 1, :]
        dot = jnp.sum((g2.astype(f32) * o2.astype(f32)).T, axis=0, keepdims=True)
        kcol = slice(nq + h * HD, nq + (h + 1) * HD)
        vcol = slice(nq + nk + h * HD, nq + nk + (h + 1) * HD)

        def block(there, masked, h=h, q2=q2, g2=g2, total=total, dot=dot, kcol=kcol, vcol=vcol):
            k = low[there, kcol]
            v = low[there, vcol]
            probs = jnp.exp2(matmul_t(k, q2) * log2_scale - total)
            if masked:
                probs = jnp.where(mask_k <= mask_q, probs, 0.0)
            grad_scores = (probs * (matmul_t(v, g2) - dot)).astype(bf16)
            dv[h, there, :] += matmul(probs.astype(bf16), g2)
            dk[h, there, :] += matmul(grad_scores, q2)
            return t_matmul(grad_scores, k)

        dq[...] = block(here, True)

        def step(j, _, block=block):
            dq[...] += block(pl.ds(pl.multiple_of(j * ROWS, ROWS), ROWS), False)
            return 0

        lax.fori_loop(0, i, step, 0)
        for a, col in enumerate(cols):
            w = unturned(dq[a * ROWS : (a + 1) * ROWS, :] * score_scale)
            grad, gp = norm_back(qraw[:, col : col + HD], qgain, w)
            grads[:, col : col + HD] = grad.astype(bf16)
            head_part[:1, :] += gp
        w = unturned(dk[h, here, :] * score_scale)
        grad, gp = norm_back(kraw[:, h * HD : (h + 1) * HD], kgain, w)
        grads[:, kcol] = grad.astype(bf16)
        head_part[1:2, :] += gp
        grads[:, vcol] = dv[h, here, :].astype(bf16)
    upstream = matmul_t(grads[...], wqkv[...])
    put(place[i], upstream.astype(bf16), mine, other)
    x = xs[...].astype(f32)
    gain_part[:1, :] += jnp.sum(upstream * x * inverse_rms(x), axis=0, keepdims=True)


def backward_attention(place, branch, tokens, weights, low, att, totals, qraw, kraw, cos, sin, head_gains):
    n, width = 4, branch[0].shape[1]
    length, nqkv = low.shape
    nq, nk = qraw.shape[1], kraw.shape[1]
    row = lambda cols: pl.BlockSpec((ROWS, cols), lambda i, p: (n - 1 - i, 0))
    out = [
        ((length, nqkv), bf16, row(nqkv)),
        *[((2, ROWS, width), bf16, pl.BlockSpec((1, ROWS, width), lambda i, p: (p[n - 1 - i] % 2, 0, 0)))] * 2,
        ((length, width), bf16, row(width)),
        ((8, width), f32, whole((8, width))),
        ((8, HD), f32, whole((8, HD))),
    ]
    return pl.pallas_call(
        backward_attention_kernel,
        grid_spec=pltpu.PrefetchScalarGridSpec(
            num_scalar_prefetch=1,
            grid=(n,),
            in_specs=[
                *[whole((ROWS, width))] * 8,
                whole((width, nqkv)),
                whole((width, nq), (0, nqkv // nq)),
                whole((length, nqkv)),
                row(nq),
                pl.BlockSpec((1, 8, GROUP * ROWS), lambda i, p: (n - 1 - i, 0, 0)),
                row(nq),
                row(nk),
                row(HD),
                row(HD),
                whole((8, HD)),
            ],
            out_specs=[o[2] for o in out],
            scratch_shapes=[
                pltpu.VMEM((ROWS, width), bf16),
                pltpu.VMEM((ROWS, width), bf16),
                pltpu.VMEM((nk // HD, length, HD), f32),
                pltpu.VMEM((nk // HD, length, HD), f32),
                pltpu.VMEM((GROUP * ROWS, HD), f32),
            ],
        ),
        out_shape=[jax.ShapeDtypeStruct(o[0], o[1]) for o in out],
        compiler_params=params(),
        cost_estimate=cost(9e9, 18e6, 3e6),
        name="backward_attention",
    )(place, *branch, *tokens, weights, weights, low, att, totals, qraw, kraw, cos, sin, head_gains)


def projection_weights_kernel(per_device, first, branch, grads, att, gain, second_gain, heads, out):
    wide = grads.shape[1]
    more = wide + att.shape[1]
    out[:, :wide] = t_matmul(first[...], grads[...]).astype(bf16)
    out[:, wide:more] = t_matmul(branch[...], att[...]).astype(bf16)
    rows = out.shape[0]
    same = equal_iota(rows, rows, lambda r, c: r == c)
    stands = of_head(rows, per_device, pl.program_id(0) * rows)
    lane = lax.broadcasted_iota(jnp.int32, (rows, HD), 1)
    columns = jnp.zeros((rows, HD), f32)
    for k, (mask, values) in enumerate(
        [(same, gain[:1, :]), (same, second_gain[:1, :]), (stands, heads[:1, :]), (stands, heads[1:2, :])]
    ):
        column = jnp.sum(jnp.where(mask, values, 0.0), axis=1, keepdims=True)
        columns = jnp.where(lane == k, column, columns)
    out[:, more:] = columns.astype(bf16)


def projection_weights(first, branch, grads, att, gain, second_gain, heads):
    length, width = first.shape
    wide, nq = grads.shape[1], att.shape[1]
    return pl.pallas_call(
        functools.partial(projection_weights_kernel, width // lax.axis_size(FSDP)),
        grid=(width // 256,),
        in_specs=[
            pl.BlockSpec((length, 256), lambda i: (0, i)),
            pl.BlockSpec((length, 256), lambda i: (0, i)),
            whole((length, wide)),
            whole((length, nq)),
            pl.BlockSpec((8, 256), lambda i: (0, i)),
            pl.BlockSpec((8, 256), lambda i: (0, i)),
            whole((8, HD)),
        ],
        out_specs=pl.BlockSpec((256, wide + nq + HD), lambda i: (i, 0)),
        out_shape=jax.ShapeDtypeStruct((width, wide + nq + HD), bf16),
        compiler_params=params(),
        cost_estimate=cost(3.2e9, 10e6),
        name="projection_weights",
    )(first, branch, grads, att, gain, second_gain, heads)


def tokens_back_kernel(tokens, mine, from_core, from_z, grad_middle, gain, grad_tokens):
    u = mine[...].astype(f32) + from_core[...].astype(f32) + from_z[...].astype(f32)
    grad, _ = norm_back(tokens[...].astype(f32), gain[:1, :], u)
    grad_tokens[...] = grad_middle[...] + grad


def tokens_back(tokens, mine, from_core, from_z, grad_middle, gain):
    width = tokens.shape[1]
    half = ROWS // 2
    row = pl.BlockSpec((half, width), lambda i: (i, 0))
    first = pl.BlockSpec((None, half, width), lambda i: (0, i, 0))
    return pl.pallas_call(
        tokens_back_kernel,
        grid=(2,),
        in_specs=[row, first, first, row, row, whole((8, width))],
        out_specs=row,
        out_shape=jax.ShapeDtypeStruct((ROWS, width), f32),
        compiler_params=params(),
        cost_estimate=cost(4e6, 4e6),
        name="tokens_back",
    )(tokens, mine, from_core, from_z, grad_middle, gain)


def swapped(value, axis):
    return lax.ppermute(value, axis, [(0, 1), (1, 0)])


def tp_gather(own):
    over_z = swapped(own, "zl")
    return [own, over_z, swapped(own, "core"), swapped(over_z, "core")]


def tp_scatter(mine, other):
    from_core = swapped(other, "core")
    passed = (mine[1].astype(f32) + from_core[1].astype(f32)).astype(bf16)
    return mine, from_core, swapped(passed, "zl")


def after(value, *others):
    return lax.optimization_barrier((value, *others))[0]


def from_everyone(shard, axes):
    copies = jnp.broadcast_to(shard, (lax.axis_size(axes), *shard.shape))
    return lax.all_to_all(copies, axes, split_axis=0, concat_axis=0, tiled=True)


def summed_rows(part):
    count = lax.axis_size(FSDP)
    blocks = part.reshape(count, part.shape[0] // count, part.shape[1])
    parts = lax.all_to_all(blocks, FSDP, 0, 0, tiled=True)
    return jnp.sum(parts.astype(f32), axis=0)


def rotary_tables(length):
    midway = HD // 2
    frequency = 1.0 / rope_base ** (jnp.arange(midway, dtype=f32) * 2.0 / HD)
    angles = jnp.arange(length, dtype=f32)[:, None] * frequency[None, :]
    cos, sin = jnp.cos(angles), jnp.sin(angles)
    return jnp.concatenate([cos, cos], axis=1), jnp.concatenate([-sin, sin], axis=1)


def local(
    tokens,
    attention_gain,
    query_weight,
    key_weight,
    value_weight,
    query_gain,
    key_gain,
    output_weight,
    feed_gain,
    gate_weight,
    up_weight,
    down_weight,
    cotangent,
):
    width = tokens.shape[2]
    nq, nk = query_weight.shape[1], key_weight.shape[1]
    units = gate_weight.shape[1]
    rows = query_weight.shape[0]
    x = tokens[0]
    dy = cotangent[0]
    zl, core = lax.axis_index("zl"), lax.axis_index("core")
    block = jnp.arange(4, dtype=jnp.int32)
    place = ((block % 2) ^ core) * 2 + ((block // 2) ^ zl)
    place = place.astype(jnp.int32)
    cos, sin = rotary_tables(4 * ROWS)

    heads = query_gain.shape[0]
    tall = lambda v: jnp.pad(v, (0, rows - v.shape[0]))[:, None]
    columns = [tall(v) for v in (attention_gain, feed_gain, query_gain, key_gain)]
    weights = jnp.concatenate(
        [query_weight, key_weight, value_weight, output_weight, *columns, jnp.zeros((rows, HD - 4), bf16)], axis=1
    )
    weights = from_everyone(weights, FSDP).reshape(width, -1)
    feed = jnp.concatenate([gate_weight, up_weight, down_weight], axis=1)
    feed = lax.all_gather(feed, FSDP, axis=0, tiled=True)
    token_blocks = tp_gather(x)
    grad_blocks = tp_gather(after(dy, token_blocks[1]))

    first, qraw, kraw, low, att, totals, mine, other, gains, head_gains = forward_attention(
        place, token_blocks, weights, nq, nk, cos, sin
    )
    middle, second = middle_step(x, *tp_scatter(mine, other), gains)
    second_blocks = tp_gather(second)
    hidden, grad_units, mine, other = feed_step(second_blocks, grad_blocks, feed, units)
    feed_grads = feed_weights(second_blocks, grad_blocks, grad_units, hidden)
    mine, from_core, from_z = tp_scatter(mine, other)
    grad_middle, branch, feed_gain_part = middle_back(
        middle, mine, from_core, after(from_z, feed_grads), dy, gains
    )
    feed_sums = summed_rows(feed_grads)

    branch_blocks = tp_gather(branch)
    mine, from_core, from_z = tp_scatter(*feed_out(hidden, feed))
    output = middle + mine[0].astype(f32) + from_core[0].astype(f32) + from_z.astype(f32)
    output = output.astype(bf16)

    branch_blocks[3] = after(branch_blocks[3], from_core)
    grads, mine, other, branch_rows, gain_part, head_part = backward_attention(
        place, branch_blocks, token_blocks, weights, low, att, totals, qraw, kraw, cos, sin, head_gains
    )
    projection_grads = projection_weights(
        first, branch_rows, grads, att, gain_part, feed_gain_part, head_part
    )
    mine, from_core, from_z = tp_scatter(mine, other)
    tokens_grad = tokens_back(
        x, mine, from_core, after(from_z, projection_grads, feed_sums, output), grad_middle, gains
    )
    sums = summed_rows(projection_grads)

    gain_sums = sums[:, nq + 2 * nk + nq :]
    over_z = swapped(gain_sums, "zl")
    gain_sums = gain_sums + over_z + (swapped(gain_sums, "core") + swapped(over_z, "core"))

    return (
        output[None],
        tokens_grad[None],
        gain_sums[:, 0],
        sums[:, :nq],
        sums[:, nq : nq + nk],
        sums[:, nq + nk : nq + 2 * nk],
        gain_sums[:heads, 2],
        gain_sums[:heads, 3],
        sums[:, nq + 2 * nk : nq + 2 * nk + nq],
        gain_sums[:, 1],
        feed_sums[:, :units],
        feed_sums[:, units : 2 * units],
        feed_sums[:, 2 * units :],
    )


def solution(mesh):
    fsdp, tp = mesh.devices.shape
    cut = {32: (4, 4, 2), 2: (1, 1, 2), 1: (1, 1, 1)}[fsdp]
    fine = Mesh(mesh.devices.reshape(*cut, 2, tp // 2), EVERY)
    split = ("zl", "core")
    data = P(FSDP, split, None)
    matrix = P(FSDP, split)
    vector = P(FSDP)
    return jax.shard_map(
        local,
        mesh=fine,
        in_specs=(
            data, vector, matrix, matrix, matrix, vector, vector,
            matrix, vector, matrix, matrix, matrix, data,
        ),
        out_specs=(
            data, data, vector, matrix, matrix, matrix, vector, vector,
            matrix, vector, matrix, matrix, matrix,
        ),
        check_vma=False,
    )
```

```python
import functools
import math

import jax
import jax.numpy as jnp
import numpy as np
from jax import lax
from jax.experimental import pallas as pl
from jax.experimental.pallas import tpu as pltpu
from jax.sharding import Mesh, PartitionSpec as P

HD = 128
ROWS = 256
WIDTH = 1024
GROUP = 2
epsilon = 1e-06
rope_base = 1000000.0
score_scale = 1.0 / math.sqrt(HD)
log2_scale = score_scale / math.log(2.0)
FSDP = ("x", "y", "zh")
PLANE = ("x", "y")
EVERY = ("x", "y", "zh", "zl", "core")
f32 = jnp.float32
bf16 = jnp.bfloat16


def matmul(a, b):
    return lax.dot_general(a, b, (((1,), (0,)), ((), ())), preferred_element_type=f32)


def matmul_t(a, b):
    return lax.dot_general(a, b, (((1,), (1,)), ((), ())), preferred_element_type=f32)


def t_matmul(a, b):
    return lax.dot_general(a, b, (((0,), (0,)), ((), ())), preferred_element_type=f32)


def inverse_rms(values):
    return lax.rsqrt(jnp.mean(values * values, axis=-1, keepdims=True) + epsilon)


def norm_back(values, gain, upstream):
    inverse = inverse_rms(values)
    scaled = gain * upstream
    moment = jnp.mean(scaled * values, axis=-1, keepdims=True)
    grad = inverse * scaled - values * (inverse * inverse * inverse) * moment
    return grad, jnp.sum(upstream * values * inverse, axis=0, keepdims=True)


def params(**kw):
    return pltpu.CompilerParams(vmem_limit_bytes=56 * 1024 * 1024, **kw)


def cost(flops, nbytes, trans=0):
    return pl.CostEstimate(flops=int(flops / 8), bytes_accessed=int(nbytes / 8), transcendentals=int(trans / 8))


def whole(shape, index=None):
    index = index or (0,) * len(shape)
    return pl.BlockSpec(shape, lambda i, *_: index)


def halves(width):
    return [
        pl.BlockSpec((1, ROWS, width), lambda i: (jnp.minimum(i, 1), 0, 0)),
        pl.BlockSpec((1, ROWS, width), lambda i: (jnp.maximum(i - 2, 0), 0, 0)),
    ]


def pick(which, pieces, target):
    for k, piece in enumerate(pieces):

        @pl.when(which == k)
        def _(piece=piece):
            target[...] = piece[...]


def equal_iota(rows, cols, make):
    r = lax.broadcasted_iota(jnp.int32, (rows, cols), 0)
    c = lax.broadcasted_iota(jnp.int32, (rows, cols), 1)
    return make(r, c)


def row_of(columns, k):
    same = equal_iota(128, 128, lambda r, c: r == c)
    parts = []
    for m in range(columns.shape[0] // 128):
        col = columns[m * 128 : (m + 1) * 128, k : k + 1].astype(f32)
        parts.append(jnp.sum(jnp.where(same, col, 0.0), axis=0, keepdims=True))
    return jnp.concatenate(parts, axis=1)


def of_head(rows, per_device, first_row=0):
    held = HD * per_device // WIDTH
    return equal_iota(
        rows, HD, lambda r, c: ((r + first_row) // per_device * held + (r + first_row) % per_device == c)
        & ((r + first_row) % per_device < held)
    )


def heads_of(columns, k, per_device):
    col = columns[:, k : k + 1].astype(f32)
    return jnp.sum(jnp.where(of_head(columns.shape[0], per_device), col, 0.0), axis=0, keepdims=True)


def put(which, value, mine, other):
    @pl.when(which < 2)
    def _():
        mine[0] = value

    @pl.when(which >= 2)
    def _():
        other[0] = value


def forward_attention_kernel(per_device, place, *refs):
    tokens = refs[:4]
    columns, wqkv, wo, cos, sin = refs[4:9]
    first, qraw, kraw, low, att, totals, mine, other, gains, head_gains = refs[9:19]
    rows, keys, values, acc = refs[19:]
    i = pl.program_id(0)

    @pl.when(i == 0)
    def _():
        gains[:2, :] = jnp.concatenate([row_of(columns, 0), row_of(columns, 1)], axis=0)
        gains[2:, :] = jnp.zeros_like(gains[2:, :])
        head_gains[:2, :] = jnp.concatenate([heads_of(columns, k, per_device) for k in (2, 3)], axis=0)
        head_gains[2:, :] = jnp.zeros_like(head_gains[2:, :])

    gain, qgain, kgain = gains[:1, :], head_gains[:1, :], head_gains[1:2, :]
    pick(place[i], tokens, rows)
    x = rows[...].astype(f32)
    normed = (x * inverse_rms(x) * gain).astype(bf16)
    first[...] = normed
    qkv = matmul(normed, wqkv[...])
    nq = qraw.shape[1]
    nk = kraw.shape[1]
    qraw[...] = qkv[:, :nq]
    kraw[...] = qkv[:, nq : nq + nk]
    here = pl.ds(i * ROWS, ROWS)
    c, s = cos[...], sin[...]

    def turned(v, g):
        n = v * inverse_rms(v) * g
        return (n * c + pltpu.roll(n, HD // 2, 1) * s).astype(bf16)

    for h in range(nk // HD):
        k_low = turned(qkv[:, nq + h * HD : nq + (h + 1) * HD], kgain)
        v_low = qkv[:, nq + nk + h * HD : nq + nk + (h + 1) * HD].astype(bf16)
        low[:, nq + h * HD : nq + (h + 1) * HD] = k_low
        low[:, nq + nk + h * HD : nq + nk + (h + 1) * HD] = v_low
        keys[h, here, :] = k_low
        values[h, here, :HD] = v_low
        values[h, here, HD:] = jnp.ones((ROWS, HD), bf16)
    mask_q = lax.broadcasted_iota(jnp.int32, (GROUP * ROWS, ROWS), 0) % ROWS
    mask_k = lax.broadcasted_iota(jnp.int32, (GROUP * ROWS, ROWS), 1)
    outs = []
    sums = []
    for h in range(nk // HD):
        qs = []
        for a in range(GROUP):
            col = (h * GROUP + a) * HD
            q_low = turned(qkv[:, col : col + HD], qgain)
            low[:, col : col + HD] = q_low
            qs.append(q_low)
        q2 = jnp.concatenate(qs, axis=0)
        scores = matmul_t(q2, keys[h, here, :])
        weights = jnp.where(mask_k <= mask_q, jnp.exp2(scores * log2_scale), 0.0)
        acc[...] = matmul(weights.astype(bf16), values[h, here, :])

        def step(j, _, h=h, q2=q2):
            there = pl.ds(pl.multiple_of(j * ROWS, ROWS), ROWS)
            scores = matmul_t(q2, keys[h, there, :])
            weights = jnp.exp2(scores * log2_scale).astype(bf16)
            acc[...] += matmul(weights, values[h, there, :])
            return 0

        lax.fori_loop(0, i, step, 0)
        total = acc[:, HD:]
        o = (acc[:, :HD] / total).astype(bf16)
        outs += [o[a * ROWS : (a + 1) * ROWS] for a in range(GROUP)]
        sums.append(jnp.log2(total).T[:1, :])
    totals[0] = jnp.concatenate(sums + [jnp.zeros((8 - len(sums), GROUP * ROWS), f32)], axis=0)
    together = jnp.concatenate(outs, axis=1)
    att[...] = together
    put(place[i], matmul_t(together, wo[...]).astype(bf16), mine, other)


def forward_attention(place, tokens, weights, nq, nk, cos, sin):
    n, width = 4, tokens[0].shape[1]
    length = n * ROWS
    nqkv = nq + 2 * nk
    row = lambda cols: pl.BlockSpec((ROWS, cols), lambda i, p: (i, 0))
    out = [
        ((length, width), bf16, row(width)),
        ((length, nq), f32, row(nq)),
        ((length, nk), f32, row(nk)),
        ((length, nqkv), bf16, row(nqkv)),
        ((length, nq), bf16, row(nq)),
        ((n, 8, GROUP * ROWS), f32, pl.BlockSpec((1, 8, GROUP * ROWS), lambda i, p: (i, 0, 0))),
        *[((2, ROWS, width), bf16, pl.BlockSpec((1, ROWS, width), lambda i, p: (p[i] % 2, 0, 0)))] * 2,
        ((8, width), f32, whole((8, width))),
        ((8, HD), f32, whole((8, HD))),
    ]
    return pl.pallas_call(
        functools.partial(forward_attention_kernel, width // lax.axis_size(FSDP)),
        grid_spec=pltpu.PrefetchScalarGridSpec(
            num_scalar_prefetch=1,
            grid=(n,),
            in_specs=[
                *[whole((ROWS, width))] * 4,
                whole((width, HD), (0, (nqkv + nq) // HD)),
                whole((width, nqkv)),
                whole((width, nq), (0, nqkv // nq)),
                row(HD),
                row(HD),
            ],
            out_specs=[o[2] for o in out],
            scratch_shapes=[
                pltpu.VMEM((ROWS, width), bf16),
                pltpu.VMEM((nk // HD, length, HD), bf16),
                pltpu.VMEM((nk // HD, length, 2 * HD), bf16),
                pltpu.VMEM((GROUP * ROWS, 2 * HD), f32),
            ],
        ),
        out_shape=[jax.ShapeDtypeStruct(o[0], o[1]) for o in out],
        compiler_params=params(),
        cost_estimate=cost(7e9, 16e6, 3e6),
        name="forward_attention",
    )(place, *tokens, weights, weights, weights, cos, sin)


def middle_kernel(tokens, mine, from_core, from_z, gain, middle, second):
    total = mine[...].astype(f32) + from_core[...].astype(f32) + from_z[...].astype(f32)
    v = tokens[...].astype(f32) + total
    middle[...] = v
    second[...] = (v * inverse_rms(v) * gain[1:2, :]).astype(bf16)


def middle_step(tokens, part, from_core, from_z, gain):
    width = tokens.shape[1]
    half = ROWS // 2
    row = pl.BlockSpec((half, width), lambda i: (i, 0))
    first = pl.BlockSpec((None, half, width), lambda i: (0, i, 0))
    return pl.pallas_call(
        middle_kernel,
        grid=(2,),
        in_specs=[row, first, first, row, whole((8, width))],
        out_specs=[row, row],
        out_shape=[jax.ShapeDtypeStruct((ROWS, width), f32), jax.ShapeDtypeStruct((ROWS, width), bf16)],
        compiler_params=params(),
        cost_estimate=cost(2e6, 4e6),
        name="middle_step",
    )(tokens, part, from_core, from_z, gain)


def feed_kernel(*refs):
    second, grads = refs[:4], refs[4:8]
    wg, wu, wd = refs[8:11]
    hidden, grad_units, mine, other = refs[11:15]
    rows_s, rows_g = refs[15:]
    i = pl.program_id(0)
    pick(i, second, rows_s)
    pick(i, grads, rows_g)
    s = rows_s[...]
    gate = matmul(s, wg[...])
    up = matmul(s, wu[...])
    sig = 1.0 / (1.0 + jnp.exp(-gate))
    swish = gate * sig
    hidden[...] = (swish * up).astype(bf16)
    gh = matmul(rows_g[...], wd[...])
    gg = (gh * up * sig * (1.0 + gate * (1.0 - sig))).astype(bf16)
    gu = (gh * swish).astype(bf16)
    units = wg.shape[1]
    grad_units[:, :units] = gg
    grad_units[:, units:] = gu
    put(i, (matmul_t(gg, wg[...]) + matmul_t(gu, wu[...])).astype(bf16), mine, other)


def feed_step(second, grads, weights, units):
    width = second[0].shape[1]
    length = 4 * ROWS
    row = lambda cols: pl.BlockSpec((ROWS, cols), lambda i: (i, 0))
    return pl.pallas_call(
        feed_kernel,
        grid=(4,),
        in_specs=[
            *[whole((ROWS, width))] * 8,
            whole((width, units)),
            whole((width, units), (0, 1)),
            whole((width, units), (0, 2)),
        ],
        out_specs=[row(units), row(2 * units), *halves(width)],
        out_shape=[
            jax.ShapeDtypeStruct((length, units), bf16),
            jax.ShapeDtypeStruct((length, 2 * units), bf16),
            *[jax.ShapeDtypeStruct((2, ROWS, width), bf16)] * 2,
        ],
        scratch_shapes=[pltpu.VMEM((ROWS, width), bf16)] * 2,
        compiler_params=params(),
        cost_estimate=cost(8e9, 16e6, 1e6),
        name="feed_step",
    )(*second, *grads, weights, weights, weights)


def feed_out_kernel(hidden, wd, mine, other):
    put(pl.program_id(0), matmul_t(hidden[...], wd[...]).astype(bf16), mine, other)


def feed_out(hidden, weights):
    length, units = hidden.shape
    width = weights.shape[0]
    return pl.pallas_call(
        feed_out_kernel,
        grid=(4,),
        in_specs=[pl.BlockSpec((ROWS, units), lambda i: (i, 0)), whole((width, units), (0, 2))],
        out_specs=halves(width),
        out_shape=[jax.ShapeDtypeStruct((2, ROWS, width), bf16)] * 2,
        compiler_params=params(),
        cost_estimate=cost(1.6e9, 5e6),
        name="feed_out",
    )(hidden, weights)


def feed_weights_kernel(*refs):
    second, grads = refs[:4], refs[4:8]
    grad_units, hidden, out = refs[8:]
    wide = grad_units.shape[1]

    def over(pieces, other):
        total = None
        for k, piece in enumerate(pieces):
            term = t_matmul(piece[...], other[k * ROWS : (k + 1) * ROWS, :])
            total = term if total is None else total + term
        return total.astype(bf16)

    out[:, :wide] = over(second, grad_units)
    out[:, wide:] = over(grads, hidden)


def feed_weights(second, grads, grad_units, hidden):
    width = second[0].shape[1]
    length, wide = grad_units.shape
    units = hidden.shape[1]
    return pl.pallas_call(
        feed_weights_kernel,
        grid=(width // 256,),
        in_specs=[
            *[pl.BlockSpec((ROWS, 256), lambda i: (0, i))] * 8,
            whole((length, wide)),
            whole((length, units)),
        ],
        out_specs=pl.BlockSpec((256, wide + units), lambda i: (i, 0)),
        out_shape=jax.ShapeDtypeStruct((width, wide + units), bf16),
        compiler_params=params(),
        cost_estimate=cost(4.8e9, 14e6),
        name="feed_weights",
    )(*second, *grads, grad_units, hidden)


def middle_back_kernel(middle, mine, from_core, from_z, cotangent, gain, grad_middle, branch, gain_part):
    u = mine[...].astype(f32) + from_core[...].astype(f32) + from_z[...].astype(f32)
    grad, part = norm_back(middle[...], gain[1:2, :], u)
    grad = cotangent[...].astype(f32) + grad
    grad_middle[...] = grad
    branch[...] = grad.astype(bf16)

    @pl.when(pl.program_id(0) == 0)
    def _():
        gain_part[...] = jnp.zeros_like(gain_part)

    gain_part[:1, :] += part


def middle_back(middle, part, from_core, from_z, cotangent, gain):
    width = middle.shape[1]
    half = ROWS // 2
    row = pl.BlockSpec((half, width), lambda i: (i, 0))
    first = pl.BlockSpec((None, half, width), lambda i: (0, i, 0))
    return pl.pallas_call(
        middle_back_kernel,
        grid=(2,),
        in_specs=[row, first, first, row, row, whole((8, width))],
        out_specs=[row, row, whole((8, width))],
        out_shape=[
            jax.ShapeDtypeStruct((ROWS, width), f32),
            jax.ShapeDtypeStruct((ROWS, width), bf16),
            jax.ShapeDtypeStruct((8, width), f32),
        ],
        compiler_params=params(),
        cost_estimate=cost(4e6, 5e6),
        name="middle_back",
    )(middle, part, from_core, from_z, cotangent, gain)


def backward_attention_kernel(place, *refs):
    branch = refs[:4]
    tokens = refs[4:8]
    wqkv, wo, low, att, totals, qraw, kraw, cos, sin, head_gains = refs[8:18]
    grads, mine, other, branch_out, gain_part, head_part = refs[18:24]
    rows, xs, dk, dv, dq = refs[24:]
    qgain, kgain = head_gains[:1, :], head_gains[1:2, :]
    step_id = pl.program_id(0)
    i = pl.num_programs(0) - 1 - step_id
    nq, nk = qraw.shape[1], kraw.shape[1]

    @pl.when(step_id == 0)
    def _():
        dk[...] = jnp.zeros_like(dk)
        dv[...] = jnp.zeros_like(dv)
        gain_part[...] = jnp.zeros_like(gain_part)
        head_part[...] = jnp.zeros_like(head_part)

    pick(place[i], branch, rows)
    pick(place[i], tokens, xs)
    b = rows[...]
    branch_out[...] = b
    grad_att = matmul(b, wo[...]).astype(bf16)
    here = pl.ds(pl.multiple_of(i * ROWS, ROWS), ROWS)
    c, s = cos[...], sin[...]
    mask_k = lax.broadcasted_iota(jnp.int32, (ROWS, GROUP * ROWS), 0)
    mask_q = lax.broadcasted_iota(jnp.int32, (ROWS, GROUP * ROWS), 1) % ROWS

    def unturned(w):
        return w * c - pltpu.roll(w, HD // 2, 1) * s

    for h in range(nk // HD):
        cols = [(h * GROUP + a) * HD for a in range(GROUP)]
        q2 = jnp.concatenate([low[here, col : col + HD] for col in cols], axis=0)
        g2 = jnp.concatenate([grad_att[:, col : col + HD] for col in cols], axis=0)
        o2 = jnp.concatenate([att[:, col : col + HD] for col in cols], axis=0)
        total = totals[0, h : h + 1, :]
        dot = jnp.sum((g2.astype(f32) * o2.astype(f32)).T, axis=0, keepdims=True)
        kcol = slice(nq + h * HD, nq + (h + 1) * HD)
        vcol = slice(nq + nk + h * HD, nq + nk + (h + 1) * HD)

        def block(there, masked, h=h, q2=q2, g2=g2, total=total, dot=dot, kcol=kcol, vcol=vcol):
            k = low[there, kcol]
            v = low[there, vcol]
            probs = jnp.exp2(matmul_t(k, q2) * log2_scale - total)
            if masked:
                probs = jnp.where(mask_k <= mask_q, probs, 0.0)
            grad_scores = (probs * (matmul_t(v, g2) - dot)).astype(bf16)
            dv[h, there, :] += matmul(probs.astype(bf16), g2)
            dk[h, there, :] += matmul(grad_scores, q2)
            return t_matmul(grad_scores, k)

        dq[...] = block(here, True)

        def step(j, _, block=block):
            dq[...] += block(pl.ds(pl.multiple_of(j * ROWS, ROWS), ROWS), False)
            return 0

        lax.fori_loop(0, i, step, 0)
        for a, col in enumerate(cols):
            w = unturned(dq[a * ROWS : (a + 1) * ROWS, :] * score_scale)
            grad, gp = norm_back(qraw[:, col : col + HD], qgain, w)
            grads[:, col : col + HD] = grad.astype(bf16)
            head_part[:1, :] += gp
        w = unturned(dk[h, here, :] * score_scale)
        grad, gp = norm_back(kraw[:, h * HD : (h + 1) * HD], kgain, w)
        grads[:, kcol] = grad.astype(bf16)
        head_part[1:2, :] += gp
        grads[:, vcol] = dv[h, here, :].astype(bf16)
    upstream = matmul_t(grads[...], wqkv[...])
    put(place[i], upstream.astype(bf16), mine, other)
    x = xs[...].astype(f32)
    gain_part[:1, :] += jnp.sum(upstream * x * inverse_rms(x), axis=0, keepdims=True)


def backward_attention(place, branch, tokens, weights, low, att, totals, qraw, kraw, cos, sin, head_gains):
    n, width = 4, branch[0].shape[1]
    length, nqkv = low.shape
    nq, nk = qraw.shape[1], kraw.shape[1]
    row = lambda cols: pl.BlockSpec((ROWS, cols), lambda i, p: (n - 1 - i, 0))
    out = [
        ((length, nqkv), bf16, row(nqkv)),
        *[((2, ROWS, width), bf16, pl.BlockSpec((1, ROWS, width), lambda i, p: (p[n - 1 - i] % 2, 0, 0)))] * 2,
        ((length, width), bf16, row(width)),
        ((8, width), f32, whole((8, width))),
        ((8, HD), f32, whole((8, HD))),
    ]
    return pl.pallas_call(
        backward_attention_kernel,
        grid_spec=pltpu.PrefetchScalarGridSpec(
            num_scalar_prefetch=1,
            grid=(n,),
            in_specs=[
                *[whole((ROWS, width))] * 8,
                whole((width, nqkv)),
                whole((width, nq), (0, nqkv // nq)),
                whole((length, nqkv)),
                row(nq),
                pl.BlockSpec((1, 8, GROUP * ROWS), lambda i, p: (n - 1 - i, 0, 0)),
                row(nq),
                row(nk),
                row(HD),
                row(HD),
                whole((8, HD)),
            ],
            out_specs=[o[2] for o in out],
            scratch_shapes=[
                pltpu.VMEM((ROWS, width), bf16),
                pltpu.VMEM((ROWS, width), bf16),
                pltpu.VMEM((nk // HD, length, HD), f32),
                pltpu.VMEM((nk // HD, length, HD), f32),
                pltpu.VMEM((GROUP * ROWS, HD), f32),
            ],
        ),
        out_shape=[jax.ShapeDtypeStruct(o[0], o[1]) for o in out],
        compiler_params=params(),
        cost_estimate=cost(9e9, 18e6, 3e6),
        name="backward_attention",
    )(place, *branch, *tokens, weights, weights, low, att, totals, qraw, kraw, cos, sin, head_gains)


def projection_weights_kernel(per_device, first, branch, grads, att, gain, second_gain, heads, out):
    wide = grads.shape[1]
    more = wide + att.shape[1]
    out[:, :wide] = t_matmul(first[...], grads[...]).astype(bf16)
    out[:, wide:more] = t_matmul(branch[...], att[...]).astype(bf16)
    rows = out.shape[0]
    same = equal_iota(rows, rows, lambda r, c: r == c)
    stands = of_head(rows, per_device, pl.program_id(0) * rows)
    lane = lax.broadcasted_iota(jnp.int32, (rows, HD), 1)
    columns = jnp.zeros((rows, HD), f32)
    for k, (mask, values) in enumerate(
        [(same, gain[:1, :]), (same, second_gain[:1, :]), (stands, heads[:1, :]), (stands, heads[1:2, :])]
    ):
        column = jnp.sum(jnp.where(mask, values, 0.0), axis=1, keepdims=True)
        columns = jnp.where(lane == k, column, columns)
    out[:, more:] = columns.astype(bf16)


def projection_weights(first, branch, grads, att, gain, second_gain, heads):
    length, width = first.shape
    wide, nq = grads.shape[1], att.shape[1]
    return pl.pallas_call(
        functools.partial(projection_weights_kernel, width // lax.axis_size(FSDP)),
        grid=(width // 256,),
        in_specs=[
            pl.BlockSpec((length, 256), lambda i: (0, i)),
            pl.BlockSpec((length, 256), lambda i: (0, i)),
            whole((length, wide)),
            whole((length, nq)),
            pl.BlockSpec((8, 256), lambda i: (0, i)),
            pl.BlockSpec((8, 256), lambda i: (0, i)),
            whole((8, HD)),
        ],
        out_specs=pl.BlockSpec((256, wide + nq + HD), lambda i: (i, 0)),
        out_shape=jax.ShapeDtypeStruct((width, wide + nq + HD), bf16),
        compiler_params=params(),
        cost_estimate=cost(3.2e9, 10e6),
        name="projection_weights",
    )(first, branch, grads, att, gain, second_gain, heads)


def tokens_back_kernel(tokens, mine, from_core, from_z, grad_middle, gain, grad_tokens):
    u = mine[...].astype(f32) + from_core[...].astype(f32) + from_z[...].astype(f32)
    grad, _ = norm_back(tokens[...].astype(f32), gain[:1, :], u)
    grad_tokens[...] = grad_middle[...] + grad


def tokens_back(tokens, mine, from_core, from_z, grad_middle, gain):
    width = tokens.shape[1]
    half = ROWS // 2
    row = pl.BlockSpec((half, width), lambda i: (i, 0))
    first = pl.BlockSpec((None, half, width), lambda i: (0, i, 0))
    return pl.pallas_call(
        tokens_back_kernel,
        grid=(2,),
        in_specs=[row, first, first, row, row, whole((8, width))],
        out_specs=row,
        out_shape=jax.ShapeDtypeStruct((ROWS, width), f32),
        compiler_params=params(),
        cost_estimate=cost(4e6, 4e6),
        name="tokens_back",
    )(tokens, mine, from_core, from_z, grad_middle, gain)


def pack(first, second, gains, rows, heads):
    widths = [a.shape[1] for a in first], [a.shape[1] for a in second]
    split = sum(widths[0])

    def kernel(gains, *refs):
        out = refs[-1]
        at = 0
        for k, ref in enumerate(refs[:-1]):
            at += HD * (k == len(first))
            out[:, at : at + ref.shape[1]] = ref[...]
            at += ref.shape[1]
        g = gains[...].astype(f32)
        lane = lax.broadcasted_iota(jnp.int32, (rows, HD), 1)
        line = lax.broadcasted_iota(jnp.int32, (rows, HD), 0)
        columns = jnp.zeros((rows, HD), f32)
        places = [(0, rows), (rows, rows), (2 * rows, heads), (2 * rows + heads, heads)]
        for k, (start, count) in enumerate(places):
            mask = (lane == line + start) & (line < count)
            column = jnp.sum(jnp.where(mask, g, 0.0), axis=1, keepdims=True)
            columns = jnp.where(lane == k, column, columns)
        out[:, split : split + HD] = columns.astype(bf16)

    return pl.pallas_call(
        kernel,
        out_shape=jax.ShapeDtypeStruct((rows, split + HD + sum(widths[1])), bf16),
        compiler_params=params(),
        cost_estimate=cost(1e3, 5e5),
        name="pack",
    )(gains, *first, *second)


def spread(zh, shard, other, split, planes):
    rows, wide = shard.shape

    def kernel(zh, shard, other, copies, rest, block, semaphores):
        places = [pl.ds(pl.multiple_of((zh[0] ^ k) * rows, rows), rows) for k in range(2)]
        for at, ref in zip(places, (shard, other)):
            block[at, :] = ref[:, :split]
        sent = [pltpu.make_async_copy(block, copies.at[k], semaphores.at[k]) for k in range(planes)]
        for copy in sent:
            copy.start()
        for at, ref in zip(places, (shard, other)):
            rest[at, :] = ref[:, split:]
        for copy in sent:
            copy.wait()

    return pl.pallas_call(
        kernel,
        grid_spec=pltpu.PrefetchScalarGridSpec(
            num_scalar_prefetch=1,
            grid=(1,),
            in_specs=[whole((rows, wide))] * 2,
            out_specs=[pl.BlockSpec(memory_space=pl.ANY), whole((2 * rows, wide - split))],
            scratch_shapes=[pltpu.VMEM((2 * rows, split), bf16), pltpu.SemaphoreType.DMA((planes,))],
        ),
        out_shape=[
            jax.ShapeDtypeStruct((planes, 2 * rows, split), bf16),
            jax.ShapeDtypeStruct((2 * rows, wide - split), bf16),
        ],
        compiler_params=params(),
        cost_estimate=cost(1e3, 5e6),
        name="spread",
    )(zh, shard, other)


def swapped(value, axis):
    return lax.ppermute(value, axis, [(0, 1), (1, 0)])


def tp_gather(own, over_z=None):
    over_z = swapped(own, "zl") if over_z is None else over_z
    return [own, over_z, swapped(own, "core"), swapped(over_z, "core")]


def tp_scatter(mine, other):
    from_core = swapped(other, "core")
    passed = (mine[1].astype(f32) + from_core[1].astype(f32)).astype(bf16)
    return mine, from_core, swapped(passed, "zl"), passed


def after(value, *others):
    return lax.optimization_barrier((value, *others))[0]


def sent_rows(part):
    planes = lax.axis_size(PLANE)
    rows, wide = part.shape[0] // (2 * planes), part.shape[1]
    blocks = part.reshape(planes, 2 * rows, wide)
    return lax.all_to_all(blocks, PLANE, 0, 0, tiled=True).reshape(planes, 2, rows, wide)


def summed_rows(parts):
    zh = lax.axis_index("zh")
    half = lambda which: jnp.sum(
        lax.dynamic_index_in_dim(parts, which, 1, keepdims=False).astype(f32), axis=0
    )
    return half(zh) + swapped(half(1 - zh).astype(bf16), "zh").astype(f32)


def rotary_tables(length):
    midway = HD // 2
    frequency = 1.0 / rope_base ** (np.arange(midway) * 2.0 / HD)
    angles = np.arange(length)[:, None] * frequency[None, :]
    cos, sin = np.cos(angles), np.sin(angles)
    tables = np.concatenate([cos, cos], axis=1), np.concatenate([-sin, sin], axis=1)
    return [jnp.asarray(t.astype(np.float32)) for t in tables]


def local(
    tokens,
    attention_gain,
    query_weight,
    key_weight,
    value_weight,
    query_gain,
    key_gain,
    output_weight,
    feed_gain,
    gate_weight,
    up_weight,
    down_weight,
    cotangent,
):
    width = tokens.shape[2]
    nq, nk = query_weight.shape[1], key_weight.shape[1]
    units = gate_weight.shape[1]
    rows = query_weight.shape[0]
    x = tokens[0]
    dy = cotangent[0]
    zl, core = lax.axis_index("zl"), lax.axis_index("core")
    block = jnp.arange(4, dtype=jnp.int32)
    place = ((block % 2) ^ core) * 2 + ((block // 2) ^ zl)
    place = place.astype(jnp.int32)
    cos, sin = rotary_tables(4 * ROWS)

    heads = query_gain.shape[0]
    gains = jnp.concatenate([attention_gain, feed_gain, query_gain, key_gain])
    gains = jnp.pad(gains, (0, HD - gains.shape[0]))[None]
    shard = pack(
        [query_weight, key_weight, value_weight, output_weight],
        [gate_weight, up_weight, down_weight],
        gains,
        rows,
        heads,
    )
    over_zh = swapped(shard, "zh")
    split = nq + 2 * nk + nq + HD
    copies, feed = spread(lax.axis_index("zh").reshape(1), shard, over_zh, split, lax.axis_size(PLANE))
    weights = lax.all_to_all(copies, PLANE, 0, 0, tiled=True).reshape(width, -1)
    feed = lax.all_gather(feed, PLANE, axis=0, tiled=True)
    token_blocks = tp_gather(x)
    grad_blocks = tp_gather(after(dy, over_zh))
    token_blocks[3] = after(token_blocks[3], *grad_blocks)

    first, qraw, kraw, low, att, totals, mine, other, gains, head_gains = forward_attention(
        place, token_blocks, weights, nq, nk, cos, sin
    )
    mine, from_core, from_z, _ = tp_scatter(mine, other)
    middle, second = middle_step(x, mine, from_core, from_z, gains)
    second_blocks = tp_gather(second)
    hidden, grad_units, mine, other = feed_step(second_blocks, grad_blocks, feed, units)
    mine, from_core, from_z, passed = tp_scatter(mine, other)
    feed_grads = feed_weights(second_blocks, grad_blocks, after(grad_units, passed), hidden)
    from_z, feed_grads = lax.optimization_barrier((from_z, feed_grads))
    grad_middle, branch, feed_gain_part = middle_back(middle, mine, from_core, from_z, dy, gains)
    feed_sums = lax.psum_scatter(feed_grads, PLANE, scatter_dimension=0, tiled=True)
    feed_sums = feed_sums.reshape(2, rows, -1)
    take = lambda which: lax.dynamic_index_in_dim(feed_sums, which, 0, keepdims=False)
    zh = lax.axis_index("zh")
    feed_sums = take(zh).astype(f32) + swapped(take(1 - zh), "zh").astype(f32)

    over_z = swapped(branch, "zl")
    mine, other = feed_out(after(hidden, branch), feed)
    branch_blocks = tp_gather(branch, after(over_z, other))
    mine, from_core, from_z, _ = tp_scatter(mine, other)
    output = middle + mine[0].astype(f32) + from_core[0].astype(f32) + from_z.astype(f32)
    output = output.astype(bf16)

    grads, mine, other, branch_rows, gain_part, head_part = backward_attention(
        place, branch_blocks, token_blocks, weights, low, att, totals, qraw, kraw, cos, sin, head_gains
    )
    projection_grads = projection_weights(
        first, branch_rows, grads, att, gain_part, feed_gain_part, head_part
    )
    mine, from_core, from_z, _ = tp_scatter(mine, other)
    tokens_grad = tokens_back(
        x, mine, from_core, after(from_z, projection_grads), grad_middle, gains
    )
    sums = summed_rows(after(sent_rows(projection_grads), tokens_grad, output))

    gain_sums = sums[:, nq + 2 * nk + nq :]
    over_z = swapped(gain_sums, "zl")
    gain_sums = gain_sums + over_z + (swapped(gain_sums, "core") + swapped(over_z, "core"))

    return (
        output[None],
        tokens_grad[None],
        gain_sums[:, 0],
        sums[:, :nq],
        sums[:, nq : nq + nk],
        sums[:, nq + nk : nq + 2 * nk],
        gain_sums[:heads, 2],
        gain_sums[:heads, 3],
        sums[:, nq + 2 * nk : nq + 2 * nk + nq],
        gain_sums[:, 1],
        feed_sums[:, :units],
        feed_sums[:, units : 2 * units],
        feed_sums[:, 2 * units :],
    )


def solution(mesh):
    fsdp, tp = mesh.devices.shape
    cut = {32: (4, 4, 2), 2: (1, 1, 2), 1: (1, 1, 1)}[fsdp]
    fine = Mesh(mesh.devices.reshape(*cut, 2, tp // 2), EVERY)
    split = ("zl", "core")
    data = P(FSDP, split, None)
    matrix = P(FSDP, split)
    vector = P(FSDP)
    return jax.shard_map(
        local,
        mesh=fine,
        in_specs=(
            data, vector, matrix, matrix, matrix, vector, vector,
            matrix, vector, matrix, matrix, matrix, data,
        ),
        out_specs=(
            data, data, vector, matrix, matrix, matrix, vector, vector,
            matrix, vector, matrix, matrix, matrix,
        ),
        check_vma=False,
    )
```

```python
import functools
import math

import jax
import jax.numpy as jnp
import numpy as np
from jax import lax
from jax.experimental import pallas as pl
from jax.experimental.pallas import tpu as pltpu
from jax.sharding import Mesh, PartitionSpec as P

HD = 128
ROWS = 256
WIDTH = 1024
GROUP = 2
CHUNK = 256
epsilon = 1e-06
rope_base = 1000000.0
score_scale = 1.0 / math.sqrt(HD)
log2_scale = score_scale / math.log(2.0)
FSDP = ("x", "y", "zh")
PLANE = ("x", "y")
EVERY = ("x", "y", "zh", "zl", "core")
f32 = jnp.float32
bf16 = jnp.bfloat16


def matmul(a, b):
    return lax.dot_general(a, b, (((1,), (0,)), ((), ())), preferred_element_type=f32)


def matmul_t(a, b):
    return lax.dot_general(a, b, (((1,), (1,)), ((), ())), preferred_element_type=f32)


def t_matmul(a, b):
    return lax.dot_general(a, b, (((0,), (0,)), ((), ())), preferred_element_type=f32)


def inverse_rms(values):
    return lax.rsqrt(jnp.mean(values * values, axis=-1, keepdims=True) + epsilon)


def norm_back(values, gain, upstream):
    inverse = inverse_rms(values)
    scaled = gain * upstream
    moment = jnp.mean(scaled * values, axis=-1, keepdims=True)
    grad = inverse * scaled - values * (inverse * inverse * inverse) * moment
    return grad, jnp.sum(upstream * values * inverse, axis=0, keepdims=True)


def far(value):
    return pltpu.with_memory_space_constraint(value, pltpu.HBM)


def params(mib):
    return pltpu.CompilerParams(vmem_limit_bytes=mib * 1024 * 1024)


def cost(flops, nbytes, trans=0):
    return pl.CostEstimate(flops=int(flops / 8), bytes_accessed=int(nbytes / 8), transcendentals=int(trans / 8))


def whole(shape, index=None):
    index = index or (0,) * len(shape)
    return pl.BlockSpec(shape, lambda i, *_: index, pipeline_mode=pl.Buffered(1))


def halves(width):
    return [
        pl.BlockSpec((1, ROWS, width), lambda i: (jnp.minimum(i, 1), 0, 0)),
        pl.BlockSpec((1, ROWS, width), lambda i: (jnp.maximum(i - 2, 0), 0, 0)),
    ]


def whole_out(shape):
    return pl.BlockSpec(shape, lambda i, *_: (0,) * len(shape))


def pick(which, pieces, target):
    for k, piece in enumerate(pieces):

        @pl.when(which == k)
        def _(piece=piece):
            target[...] = piece[...]


def equal_iota(rows, cols, make):
    r = lax.broadcasted_iota(jnp.int32, (rows, cols), 0)
    c = lax.broadcasted_iota(jnp.int32, (rows, cols), 1)
    return make(r, c)


def row_of(columns, k):
    same = equal_iota(128, 128, lambda r, c: r == c)
    parts = []
    for m in range(columns.shape[0] // 128):
        col = columns[m * 128 : (m + 1) * 128, k : k + 1].astype(f32)
        parts.append(jnp.sum(jnp.where(same, col, 0.0), axis=0, keepdims=True))
    return jnp.concatenate(parts, axis=1)


def of_head(rows, per_device, first_row=0):
    held = HD * per_device // WIDTH
    return equal_iota(
        rows, HD, lambda r, c: ((r + first_row) // per_device * held + (r + first_row) % per_device == c)
        & ((r + first_row) % per_device < held)
    )


def heads_of(columns, k, per_device):
    col = columns[:, k : k + 1].astype(f32)
    return jnp.sum(jnp.where(of_head(columns.shape[0], per_device), col, 0.0), axis=0, keepdims=True)


def put_pair(which, value, mine, other):
    top, bottom = value[:ROWS], value[ROWS:]

    @pl.when(which < 2)
    def _():
        mine[0] = top
        other[0] = bottom

    @pl.when(which >= 2)
    def _():
        mine[0] = bottom
        other[0] = top


def put(which, value, mine, other):
    @pl.when(which < 2)
    def _():
        mine[0] = value

    @pl.when(which >= 2)
    def _():
        other[0] = value


def forward_attention_kernel(per_device, place, *refs):
    tokens = refs[:4]
    columns, wqkv, wo, cos, sin = refs[4:9]
    first, qraw, kraw, low, att, totals, mine, other, gains, head_gains = refs[9:19]
    rows, keys, values = refs[19:]
    i = pl.program_id(0)

    @pl.when(i == 0)
    def _():
        gains[:2, :] = jnp.concatenate([row_of(columns, 0), row_of(columns, 1)], axis=0)
        gains[2:, :] = jnp.zeros_like(gains[2:, :])
        head_gains[:2, :] = jnp.concatenate([heads_of(columns, k, per_device) for k in (2, 3)], axis=0)
        head_gains[2:, :] = jnp.zeros_like(head_gains[2:, :])

    gain, qgain, kgain = gains[:1, :], head_gains[:1, :], head_gains[1:2, :]
    for a in range(2):
        pick(place[2 * i + a], tokens, rows.at[a * ROWS : (a + 1) * ROWS, :])
    x = rows[...].astype(f32)
    normed = (x * inverse_rms(x) * gain).astype(bf16)
    first[...] = normed
    qkv = matmul(normed, wqkv[...])
    nq, nk = qraw.shape[1], kraw.shape[1]
    qraw[...] = qkv[:, :nq]
    kraw[...] = qkv[:, nq : nq + nk]
    here = pl.ds(pl.multiple_of(i * 2 * ROWS, 2 * ROWS), 2 * ROWS)
    c, s = cos[...], sin[...]

    def turned(v, g):
        n = v * inverse_rms(v) * g
        return (n * c + pltpu.roll(n, HD // 2, 1) * s).astype(bf16)

    for h in range(nk // HD):
        k_low = turned(qkv[:, nq + h * HD : nq + (h + 1) * HD], kgain)
        v_low = qkv[:, nq + nk + h * HD : nq + nk + (h + 1) * HD].astype(bf16)
        low[:, nq + h * HD : nq + (h + 1) * HD] = k_low
        low[:, nq + nk + h * HD : nq + nk + (h + 1) * HD] = v_low
        keys[h, here, :] = k_low
        values[h, here, :HD] = v_low
        values[h, here, HD:] = jnp.ones((2 * ROWS, HD), bf16)
    for h in range(nq // HD):
        low[:, h * HD : (h + 1) * HD] = turned(qkv[:, h * HD : (h + 1) * HD], qgain)
    mask_q = lax.broadcasted_iota(jnp.int32, (GROUP * ROWS, ROWS), 0) % ROWS
    mask_k = lax.broadcasted_iota(jnp.int32, (GROUP * ROWS, ROWS), 1)

    def attend(block):
        half = block % 2 * ROWS
        n = block * ROWS
        sums = []
        for h in range(nk // HD):
            cols = [(h * GROUP + a) * HD for a in range(GROUP)]
            q2 = jnp.concatenate([low[half : half + ROWS, col : col + HD] for col in cols], axis=0)
            scores = matmul_t(q2, keys[h, : n + ROWS, :]) * log2_scale
            weights = jnp.exp2(scores[:, n:])
            weights = jnp.where(mask_k <= mask_q, weights, 0.0).astype(bf16)
            if n:
                weights = jnp.concatenate([jnp.exp2(scores[:, :n]).astype(bf16), weights], axis=1)
            acc = matmul(weights, values[h, : n + ROWS, :])
            total = acc[:, HD:]
            o = (acc[:, :HD] / total).astype(bf16)
            for a, col in enumerate(cols):
                att[half : half + ROWS, col : col + HD] = o[a * ROWS : (a + 1) * ROWS]
            sums.append(jnp.log2(total).T[:1, :])
        sums = jnp.concatenate(sums + [jnp.zeros((8 - len(sums), GROUP * ROWS), f32)], axis=0)
        totals[block % 2] = sums

    for k in range(2):

        @pl.when(i == k)
        def _(k=k):
            attend(2 * k)
            attend(2 * k + 1)

    put_pair(place[2 * i], matmul_t(att[...], wo[...]).astype(bf16), mine, other)


def forward_attention(place, tokens, weights, nq, nk, cos, sin):
    n, width = 4, tokens[0].shape[1]
    length = n * ROWS
    nqkv = nq + 2 * nk
    row = lambda cols: pl.BlockSpec((2 * ROWS, cols), lambda i, p: (i, 0))
    out = [
        ((length, width), bf16, row(width)),
        ((length, nq), f32, row(nq)),
        ((length, nk), f32, row(nk)),
        ((length, nqkv), bf16, row(nqkv)),
        ((length, nq), bf16, row(nq)),
        ((n, 8, GROUP * ROWS), f32, pl.BlockSpec((2, 8, GROUP * ROWS), lambda i, p: (i, 0, 0))),
        *[((2, ROWS, width), bf16, pl.BlockSpec((1, ROWS, width), lambda i, p: (p[2 * i] % 2, 0, 0)))] * 2,
        ((8, width), f32, whole_out((8, width))),
        ((8, HD), f32, whole_out((8, HD))),
    ]
    return pl.pallas_call(
        functools.partial(forward_attention_kernel, width // lax.axis_size(FSDP)),
        grid_spec=pltpu.PrefetchScalarGridSpec(
            num_scalar_prefetch=1,
            grid=(n // 2,),
            in_specs=[
                *[whole((ROWS, width))] * 4,
                whole((width, HD), (0, (nqkv + nq) // HD)),
                whole((width, nqkv)),
                whole((width, nq), (0, nqkv // nq)),
                row(HD),
                row(HD),
            ],
            out_specs=[o[2] for o in out],
            scratch_shapes=[
                pltpu.VMEM((2 * ROWS, width), bf16),
                pltpu.VMEM((nk // HD, length, HD), bf16),
                pltpu.VMEM((nk // HD, length, 2 * HD), bf16),
            ],
        ),
        out_shape=[(pltpu.HBM if k < 6 else jax.ShapeDtypeStruct)(o[0], o[1]) for k, o in enumerate(out)],
        compiler_params=params(40),
        cost_estimate=cost(7e9, 16e6, 3e6),
        name="forward_attention",
    )(place, far(tokens[0]), *tokens[1:], weights, weights, weights, far(cos), far(sin))


def middle_kernel(tokens, mine, from_core, from_z, gain, middle, second):
    total = mine[...].astype(f32) + from_core[...].astype(f32) + from_z[...].astype(f32)
    v = tokens[...].astype(f32) + total
    middle[...] = v
    second[...] = (v * inverse_rms(v) * gain[1:2, :]).astype(bf16)


def middle_step(tokens, part, from_core, from_z, gain):
    width = tokens.shape[1]
    half = ROWS // 2
    row = pl.BlockSpec((half, width), lambda i: (i, 0))
    first = pl.BlockSpec((None, half, width), lambda i: (0, i, 0))
    return pl.pallas_call(
        middle_kernel,
        grid=(2,),
        in_specs=[row, first, first, row, whole((8, width))],
        out_specs=[row, row],
        out_shape=[pltpu.HBM((ROWS, width), f32), jax.ShapeDtypeStruct((ROWS, width), bf16)],
        compiler_params=params(12),
        cost_estimate=cost(2e6, 4e6),
        name="middle_step",
    )(far(tokens), part, from_core, from_z, gain)


def feed_kernel(*refs):
    second, grads, weights = refs[:4], refs[4:8], refs[8]
    hidden, grad_units, mine, other = refs[9:13]
    rows_s, rows_g, matrices, row_sems, matrix_sem = refs[13:]
    i = pl.program_id(0)
    units = hidden.shape[1]
    loads = []
    for k in range(4):
        at = slice(k * ROWS, (k + 1) * ROWS)
        loads.append(pltpu.make_async_copy(second[k], rows_s.at[at, :], row_sems.at[0, k]))
        loads.append(pltpu.make_async_copy(grads[k], rows_g.at[at, :], row_sems.at[1, k]))
    load_weights = pltpu.make_async_copy(weights, matrices, matrix_sem)

    @pl.when(i == 0)
    def _():
        for copy in [*loads[:4], load_weights, *loads[4:]]:
            copy.start()
        for copy in [*loads[:4], load_weights]:
            copy.wait()

    @pl.when(i == 1)
    def _():
        for copy in loads[4:]:
            copy.wait()

    here = pl.ds(pl.multiple_of(i * 2 * ROWS, 2 * ROWS), 2 * ROWS)
    s, g = rows_s[here, :], rows_g[here, :]
    for at in range(0, units, CHUNK):
        wg = matrices[:, at : at + CHUNK]
        wu = matrices[:, units + at : units + at + CHUNK]
        gate = matmul(s, wg)
        up = matmul(s, wu)
        gh = matmul(g, matrices[:, 2 * units + at : 2 * units + at + CHUNK])
        sig = 0.5 * jnp.tanh(0.5 * gate) + 0.5
        swish = gate * sig
        hidden[:, at : at + CHUNK] = (swish * up).astype(bf16)
        gg = (gh * up * (sig + swish * (1.0 - sig))).astype(bf16)
        gu = (gh * swish).astype(bf16)
        grad_units[:, at : at + CHUNK] = gg
        grad_units[:, units + at : units + at + CHUNK] = gu
    part = matmul_t(grad_units[...], matrices[:, : 2 * units]).astype(bf16)
    for k, ref in enumerate((mine, other)):

        @pl.when(i == k)
        def _(ref=ref):
            ref[0] = part[:ROWS]
            ref[1] = part[ROWS:]


def feed_step(second, grads, weights, units):
    width = second[0].shape[1]
    length = 4 * ROWS
    row = lambda cols: pl.BlockSpec((2 * ROWS, cols), lambda i: (i, 0))
    return pl.pallas_call(
        feed_kernel,
        grid=(2,),
        in_specs=[pl.BlockSpec(memory_space=pl.ANY)] * 9,
        out_specs=[row(units), row(2 * units), *[whole_out((2, ROWS, width))] * 2],
        out_shape=[
            pltpu.HBM((length, units), bf16),
            pltpu.HBM((length, 2 * units), bf16),
            *[jax.ShapeDtypeStruct((2, ROWS, width), bf16)] * 2,
        ],
        scratch_shapes=[
            *[pltpu.VMEM((length, width), bf16)] * 2,
            pltpu.VMEM((width, 3 * units), bf16),
            pltpu.SemaphoreType.DMA((2, 4)),
            pltpu.SemaphoreType.DMA,
        ],
        compiler_params=params(40),
        cost_estimate=cost(8e9, 16e6, 1e6),
        name="feed_step",
    )(*second, *map(far, grads), far(weights))


def feed_out_kernel(hidden, wd, mine, other):
    put(pl.program_id(0), matmul_t(hidden[...], wd[...]).astype(bf16), mine, other)


def feed_out(hidden, weights):
    length, units = hidden.shape
    width = weights.shape[0]
    return pl.pallas_call(
        feed_out_kernel,
        grid=(4,),
        in_specs=[pl.BlockSpec((ROWS, units), lambda i: (i, 0)), whole((width, units), (0, 2))],
        out_specs=halves(width),
        out_shape=[jax.ShapeDtypeStruct((2, ROWS, width), bf16)] * 2,
        compiler_params=params(20),
        cost_estimate=cost(1.6e9, 5e6),
        name="feed_out",
    )(far(hidden), far(weights))


def feed_weights_kernel(*refs):
    second, grads = refs[:4], refs[4:8]
    grad_units, hidden, out = refs[8:]
    wide = grad_units.shape[1]

    def over(pieces, other):
        total = None
        for k, piece in enumerate(pieces):
            term = t_matmul(piece[...], other[k * ROWS : (k + 1) * ROWS, :])
            total = term if total is None else total + term
        return total.astype(bf16)

    out[:, :wide] = over(second, grad_units)
    out[:, wide:] = over(grads, hidden)


def feed_weights(second, grads, grad_units, hidden):
    width = second[0].shape[1]
    length, wide = grad_units.shape
    units = hidden.shape[1]
    return pl.pallas_call(
        feed_weights_kernel,
        grid=(width // 256,),
        in_specs=[
            *[pl.BlockSpec((ROWS, 256), lambda i: (0, i))] * 8,
            whole((length, wide)),
            whole((length, units)),
        ],
        out_specs=pl.BlockSpec((256, wide + units), lambda i: (i, 0)),
        out_shape=pltpu.HBM((width, wide + units), bf16),
        compiler_params=params(36),
        cost_estimate=cost(4.8e9, 14e6),
        name="feed_weights",
    )(*map(far, second), *map(far, grads), far(grad_units), far(hidden))


def middle_back_kernel(middle, mine, from_core, from_z, cotangent, gain, grad_middle, branch, gain_part):
    u = mine[...].astype(f32) + from_core[...].astype(f32) + from_z[...].astype(f32)
    grad, part = norm_back(middle[...], gain[1:2, :], u)
    grad = cotangent[...].astype(f32) + grad
    grad_middle[...] = grad
    branch[...] = grad.astype(bf16)

    @pl.when(pl.program_id(0) == 0)
    def _():
        gain_part[...] = jnp.zeros_like(gain_part)

    gain_part[:1, :] += part


def middle_back(middle, part, from_core, from_z, cotangent, gain):
    width = middle.shape[1]
    half = ROWS // 2
    row = pl.BlockSpec((half, width), lambda i: (i, 0))
    first = pl.BlockSpec((None, half, width), lambda i: (0, i, 0))
    return pl.pallas_call(
        middle_back_kernel,
        grid=(2,),
        in_specs=[row, first, first, row, row, whole((8, width))],
        out_specs=[row, row, whole_out((8, width))],
        out_shape=[
            pltpu.HBM((ROWS, width), f32),
            jax.ShapeDtypeStruct((ROWS, width), bf16),
            pltpu.HBM((8, width), f32),
        ],
        compiler_params=params(14),
        cost_estimate=cost(4e6, 5e6),
        name="middle_back",
    )(far(middle), part, from_core, from_z, far(cotangent), gain)


def backward_attention_kernel(place, *refs):
    branch = refs[:4]
    tokens = refs[4:8]
    weights, low, att, totals, qraw, kraw, cos, sin, head_gains = refs[8:17]
    grads, mine, other, branch_out, gain_part, head_part = refs[17:23]
    matrices, rows_all, xs_all, grad_att, dk, dv, dq, row_sems, matrix_sems = refs[23:]
    qgain, kgain = head_gains[:1, :], head_gains[1:2, :]
    step_id = pl.program_id(0)
    i = pl.num_programs(0) - 1 - step_id
    nq, nk = qraw.shape[1], kraw.shape[1]

    @pl.when(step_id == 0)
    def _():
        gain_part[...] = jnp.zeros_like(gain_part)
        head_part[...] = jnp.zeros_like(head_part)

    nqkv = nq + 2 * nk
    wqkv = matrices.at[:, :nqkv]
    wo = matrices.at[:, nqkv:]
    load_o = pltpu.make_async_copy(weights.at[:, nqkv : nqkv + nq], wo, matrix_sems.at[0])
    load_qkv = pltpu.make_async_copy(weights.at[:, :nqkv], wqkv, matrix_sems.at[1])
    loads = []
    for pieces, target, sem in ((branch, rows_all, row_sems.at[0]), (tokens, xs_all, row_sems.at[1])):
        for k, piece in enumerate(pieces):
            at = pl.ds(pl.multiple_of(place[4 + k] * ROWS, ROWS), ROWS)
            loads.append(pltpu.make_async_copy(piece, target.at[at, :], sem.at[k]))

    @pl.when(step_id == 0)
    def _():
        for copy in [load_o, *loads[:4], load_qkv, *loads[4:]]:
            copy.start()
        for copy in [load_o, *loads[:4]]:
            copy.wait()

    here = pl.ds(pl.multiple_of(i * 2 * ROWS, 2 * ROWS), 2 * ROWS)
    branch_out[...] = rows_all[here, :]
    grad_att[...] = matmul(rows_all[here, :], wo[...]).astype(bf16)
    mask_k = lax.broadcasted_iota(jnp.int32, (ROWS, GROUP * ROWS), 0)
    mask_q = lax.broadcasted_iota(jnp.int32, (ROWS, GROUP * ROWS), 1) % ROWS

    def attend_back(block):
        half = block % 2 * ROWS
        n = block * ROWS
        end = n + ROWS
        for h in range(nk // HD):
            cols = [(h * GROUP + a) * HD for a in range(GROUP)]
            q2 = jnp.concatenate([low[n:end, col : col + HD] for col in cols], axis=0)
            g2 = jnp.concatenate([grad_att[half : half + ROWS, col : col + HD] for col in cols], axis=0)
            o2 = jnp.concatenate([att[half : half + ROWS, col : col + HD] for col in cols], axis=0)
            total = totals[block % 2, h : h + 1, :]
            dot = jnp.sum((g2.astype(f32) * o2.astype(f32)).T, axis=0, keepdims=True)
            k = low[:end, nq + h * HD : nq + (h + 1) * HD]
            v = low[:end, nq + nk + h * HD : nq + nk + (h + 1) * HD]
            probs = jnp.exp2(matmul_t(k, q2) * log2_scale - total)
            last = jnp.where(mask_k <= mask_q, probs[n:], 0.0)
            probs = jnp.concatenate([probs[:n], last], axis=0) if n else last
            grad_scores = (probs * (matmul_t(v, g2) - dot)).astype(bf16)
            dv_part = matmul(probs.astype(bf16), g2)
            dk_part = matmul(grad_scores, q2)
            if end == keys:
                dv[h] = dv_part
                dk[h] = dk_part
            else:
                dv[h, :end, :] += dv_part
                dk[h, :end, :] += dk_part
            d = t_matmul(grad_scores, k) * score_scale
            for a, col in enumerate(cols):
                dq[half : half + ROWS, col : col + HD] = d[a * ROWS : (a + 1) * ROWS]

    keys = low.shape[0]
    for k in range(keys // (2 * ROWS)):

        @pl.when(i == k)
        def _(k=k):
            attend_back(2 * k + 1)
            attend_back(2 * k)

    c, s = cos[...], sin[...]

    def unturned(w):
        return w * c - pltpu.roll(w, HD // 2, 1) * s

    for h in range(nq // HD):
        col = slice(h * HD, (h + 1) * HD)
        grad, gp = norm_back(qraw[:, col], qgain, unturned(dq[:, col]))
        grads[:, col] = grad.astype(bf16)
        head_part[:1, :] += gp
    for h in range(nk // HD):
        col = slice(h * HD, (h + 1) * HD)
        grad, gp = norm_back(kraw[:, col], kgain, unturned(dk[h, here, :] * score_scale))
        grads[:, nq + h * HD : nq + (h + 1) * HD] = grad.astype(bf16)
        head_part[1:2, :] += gp
        grads[:, nq + nk + h * HD : nq + nk + (h + 1) * HD] = dv[h, here, :].astype(bf16)
    @pl.when(step_id == 0)
    def _():
        for copy in [load_qkv, *loads[4:]]:
            copy.wait()

    upstream = matmul_t(grads[...], wqkv[...])
    put_pair(place[2 * i], upstream.astype(bf16), mine, other)
    x = xs_all[here, :].astype(f32)
    gain_part[:1, :] += jnp.sum(upstream * x * inverse_rms(x), axis=0, keepdims=True)


def backward_attention(place, branch, tokens, weights, low, att, totals, qraw, kraw, cos, sin, head_gains):
    n, width = 4, branch[0].shape[1]
    length, nqkv = low.shape
    nq, nk = qraw.shape[1], kraw.shape[1]
    row = lambda cols: pl.BlockSpec((2 * ROWS, cols), lambda i, p: (n // 2 - 1 - i, 0))
    out = [
        ((length, nqkv), bf16, row(nqkv)),
        *[((2, ROWS, width), bf16, pl.BlockSpec((1, ROWS, width), lambda i, p: (p[n - 2 - 2 * i] % 2, 0, 0)))] * 2,
        ((length, width), bf16, row(width)),
        ((8, width), f32, whole_out((8, width))),
        ((8, HD), f32, whole_out((8, HD))),
    ]
    return pl.pallas_call(
        backward_attention_kernel,
        grid_spec=pltpu.PrefetchScalarGridSpec(
            num_scalar_prefetch=1,
            grid=(n // 2,),
            in_specs=[
                *[pl.BlockSpec(memory_space=pl.ANY)] * 9,
                whole((length, nqkv)),
                row(nq),
                pl.BlockSpec((2, 8, GROUP * ROWS), lambda i, p: (n // 2 - 1 - i, 0, 0)),
                row(nq),
                row(nk),
                row(HD),
                row(HD),
                whole((8, HD)),
            ],
            out_specs=[o[2] for o in out],
            scratch_shapes=[
                pltpu.VMEM((width, nqkv + nq), bf16),
                pltpu.VMEM((length, width), bf16),
                pltpu.VMEM((length, width), bf16),
                pltpu.VMEM((2 * ROWS, nq), bf16),
                pltpu.VMEM((nk // HD, length, HD), f32),
                pltpu.VMEM((nk // HD, length, HD), f32),
                pltpu.VMEM((2 * ROWS, nq), f32),
                pltpu.SemaphoreType.DMA((2, 4)),
                pltpu.SemaphoreType.DMA((2,)),
            ],
        ),
        out_shape=[(pltpu.HBM if k in (0, 1, 3) else jax.ShapeDtypeStruct)(o[0], o[1]) for k, o in enumerate(out)],
        compiler_params=params(48),
        cost_estimate=cost(9e9, 18e6, 3e6),
        name="backward_attention",
    )(
        place, *branch, *map(far, tokens), far(weights), far(low), far(att), far(totals),
        far(qraw), far(kraw), far(cos), far(sin), far(head_gains),
    )


def projection_weights_kernel(per_device, first, branch, grads, att, gain, second_gain, heads, out):
    wide = grads.shape[1]
    more = wide + att.shape[1]
    out[:, :wide] = t_matmul(first[...], grads[...]).astype(bf16)
    out[:, wide:more] = t_matmul(branch[...], att[...]).astype(bf16)
    rows = out.shape[0]
    same = equal_iota(rows, rows, lambda r, c: r == c)
    stands = of_head(rows, per_device, pl.program_id(0) * rows)
    lane = lax.broadcasted_iota(jnp.int32, (rows, HD), 1)
    columns = jnp.zeros((rows, HD), f32)
    for k, (mask, values) in enumerate(
        [(same, gain[:1, :]), (same, second_gain[:1, :]), (stands, heads[:1, :]), (stands, heads[1:2, :])]
    ):
        column = jnp.sum(jnp.where(mask, values, 0.0), axis=1, keepdims=True)
        columns = jnp.where(lane == k, column, columns)
    out[:, more:] = columns.astype(bf16)


def projection_weights(first, branch, grads, att, gain, second_gain, heads):
    length, width = first.shape
    wide, nq = grads.shape[1], att.shape[1]
    return pl.pallas_call(
        functools.partial(projection_weights_kernel, width // lax.axis_size(FSDP)),
        grid=(width // 512,),
        in_specs=[
            pl.BlockSpec((length, 512), lambda i: (0, i)),
            pl.BlockSpec((length, 512), lambda i: (0, i)),
            whole((length, wide)),
            whole((length, nq)),
            pl.BlockSpec((8, 512), lambda i: (0, i)),
            pl.BlockSpec((8, 512), lambda i: (0, i)),
            whole((8, HD)),
        ],
        out_specs=pl.BlockSpec((512, wide + nq + HD), lambda i: (i, 0)),
        out_shape=pltpu.HBM((width, wide + nq + HD), bf16),
        compiler_params=params(30),
        cost_estimate=cost(3.2e9, 10e6),
        name="projection_weights",
    )(far(first), far(branch), far(grads), far(att), gain, far(second_gain), heads)


def tokens_back_kernel(tokens, mine, from_core, from_z, grad_middle, gain, grad_tokens):
    u = mine[...].astype(f32) + from_core[...].astype(f32) + from_z[...].astype(f32)
    grad, _ = norm_back(tokens[...].astype(f32), gain[:1, :], u)
    grad_tokens[...] = grad_middle[...] + grad


def tokens_back(tokens, mine, from_core, from_z, grad_middle, gain):
    width = tokens.shape[1]
    half = ROWS // 2
    row = pl.BlockSpec((half, width), lambda i: (i, 0))
    first = pl.BlockSpec((None, half, width), lambda i: (0, i, 0))
    return pl.pallas_call(
        tokens_back_kernel,
        grid=(2,),
        in_specs=[row, first, first, row, row, whole((8, width))],
        out_specs=row,
        out_shape=pltpu.HBM((ROWS, width), f32),
        compiler_params=params(14),
        cost_estimate=cost(4e6, 4e6),
        name="tokens_back",
    )(far(tokens), mine, from_core, from_z, far(grad_middle), far(gain))


def pack(first, second, gains, rows, heads):
    widths = [a.shape[1] for a in first], [a.shape[1] for a in second]
    split = sum(widths[0])

    def kernel(gains, *refs):
        out = refs[-1]
        at = 0
        for k, ref in enumerate(refs[:-1]):
            at += HD * (k == len(first))
            out[:, at : at + ref.shape[1]] = ref[...]
            at += ref.shape[1]
        g = gains[...].astype(f32)
        lane = lax.broadcasted_iota(jnp.int32, (rows, HD), 1)
        line = lax.broadcasted_iota(jnp.int32, (rows, HD), 0)
        columns = jnp.zeros((rows, HD), f32)
        places = [(0, rows), (rows, rows), (2 * rows, heads), (2 * rows + heads, heads)]
        for k, (start, count) in enumerate(places):
            mask = (lane == line + start) & (line < count)
            column = jnp.sum(jnp.where(mask, g, 0.0), axis=1, keepdims=True)
            columns = jnp.where(lane == k, column, columns)
        out[:, split : split + HD] = columns.astype(bf16)

    return pl.pallas_call(
        kernel,
        out_shape=jax.ShapeDtypeStruct((rows, split + HD + sum(widths[1])), bf16),
        compiler_params=params(8),
        cost_estimate=cost(1e3, 5e5),
        name="pack",
    )(gains, *map(far, first), *map(far, second))


def spread(zh, shard, other, split, planes):
    rows, wide = shard.shape

    def kernel(zh, shard, other, copies, rest, block, semaphores):
        places = [pl.ds(pl.multiple_of((zh[0] ^ k) * rows, rows), rows) for k in range(2)]
        for at, ref in zip(places, (shard, other)):
            block[at, :] = ref[:, :split]
        sent = [pltpu.make_async_copy(block, copies.at[k], semaphores.at[k]) for k in range(planes)]
        for copy in sent:
            copy.start()
        for at, ref in zip(places, (shard, other)):
            rest[at, :] = ref[:, split:]
        for copy in sent:
            copy.wait()

    return pl.pallas_call(
        kernel,
        grid_spec=pltpu.PrefetchScalarGridSpec(
            num_scalar_prefetch=1,
            grid=(1,),
            in_specs=[whole((rows, wide))] * 2,
            out_specs=[pl.BlockSpec(memory_space=pltpu.HBM), whole_out((2 * rows, wide - split))],
            scratch_shapes=[pltpu.VMEM((2 * rows, split), bf16), pltpu.SemaphoreType.DMA((planes,))],
        ),
        out_shape=[
            pltpu.HBM((planes, 2 * rows, split), bf16),
            pltpu.HBM((2 * rows, wide - split), bf16),
        ],
        compiler_params=params(8),
        cost_estimate=cost(1e3, 5e6),
        name="spread",
    )(zh, shard, other)


def swapped(value, axis):
    return lax.ppermute(value, axis, [(0, 1), (1, 0)])


def tp_gather(own, over_z=None):
    over_z = swapped(own, "zl") if over_z is None else over_z
    return [own, over_z, swapped(own, "core"), swapped(over_z, "core")]


def tp_scatter(mine, other):
    from_core = swapped(other, "core")
    passed = (mine[1].astype(f32) + from_core[1].astype(f32)).astype(bf16)
    return mine, from_core, swapped(passed, "zl"), passed


def after(value, *others):
    return lax.optimization_barrier((value, *others))[0]


def sent_rows(part):
    planes = lax.axis_size(PLANE)
    rows, wide = part.shape[0] // (2 * planes), part.shape[1]
    blocks = part.reshape(planes, 2 * rows, wide)
    return lax.all_to_all(blocks, PLANE, 0, 0, tiled=True).reshape(planes, 2, rows, wide)


def summed_rows(parts):
    zh = lax.axis_index("zh")
    half = lambda which: jnp.sum(
        lax.dynamic_index_in_dim(parts, which, 1, keepdims=False).astype(f32), axis=0
    )
    return half(zh) + swapped(half(1 - zh).astype(bf16), "zh").astype(f32)


def rotary_tables(length):
    midway = HD // 2
    frequency = 1.0 / rope_base ** (np.arange(midway) * 2.0 / HD)
    angles = np.arange(length)[:, None] * frequency[None, :]
    cos, sin = np.cos(angles), np.sin(angles)
    tables = np.concatenate([cos, cos], axis=1), np.concatenate([-sin, sin], axis=1)
    return [jnp.asarray(t.astype(np.float32)) for t in tables]


def local(
    tokens,
    attention_gain,
    query_weight,
    key_weight,
    value_weight,
    query_gain,
    key_gain,
    output_weight,
    feed_gain,
    gate_weight,
    up_weight,
    down_weight,
    cotangent,
):
    width = tokens.shape[2]
    nq, nk = query_weight.shape[1], key_weight.shape[1]
    units = gate_weight.shape[1]
    rows = query_weight.shape[0]
    x = tokens[0]
    dy = cotangent[0]
    zl, core = lax.axis_index("zl"), lax.axis_index("core")
    block = jnp.arange(4, dtype=jnp.int32)
    place = ((block % 2) ^ core) * 2 + ((block // 2) ^ zl)
    block_of = ((block // 2) ^ core) + ((block % 2) ^ zl) * 2
    place = jnp.concatenate([place, block_of]).astype(jnp.int32)
    cos, sin = rotary_tables(4 * ROWS)

    heads = query_gain.shape[0]
    gains = jnp.concatenate([attention_gain, feed_gain, query_gain, key_gain])
    gains = jnp.pad(gains, (0, HD - gains.shape[0]))[None]
    shard = pack(
        [query_weight, key_weight, value_weight, output_weight],
        [gate_weight, up_weight, down_weight],
        gains,
        rows,
        heads,
    )
    over_zh = swapped(shard, "zh")
    split = nq + 2 * nk + nq + HD
    copies, feed = spread(lax.axis_index("zh").reshape(1), shard, over_zh, split, lax.axis_size(PLANE))
    weights = lax.all_to_all(copies, PLANE, 0, 0, tiled=True).reshape(width, -1)
    feed = lax.all_gather(feed, PLANE, axis=0, tiled=True)
    token_blocks = tp_gather(x)
    grad_blocks = tp_gather(after(dy, over_zh))
    token_blocks[3] = after(token_blocks[3], *grad_blocks)

    first, qraw, kraw, low, att, totals, mine, other, gains, head_gains = forward_attention(
        place, token_blocks, weights, nq, nk, cos, sin
    )
    mine, from_core, from_z, _ = tp_scatter(mine, other)
    middle, second = middle_step(x, mine, from_core, from_z, gains)
    second_blocks = tp_gather(second)
    hidden, grad_units, mine, other = feed_step(second_blocks, grad_blocks, feed, units)
    mine, from_core, from_z, passed = tp_scatter(mine, other)
    feed_grads = feed_weights(second_blocks, grad_blocks, after(grad_units, passed), hidden)
    from_z, feed_grads = lax.optimization_barrier((from_z, feed_grads))
    grad_middle, branch, feed_gain_part = middle_back(middle, mine, from_core, from_z, dy, gains)
    feed_sums = lax.psum_scatter(feed_grads, PLANE, scatter_dimension=0, tiled=True)
    feed_sums = feed_sums.reshape(2, rows, -1)
    take = lambda which: lax.dynamic_index_in_dim(feed_sums, which, 0, keepdims=False)
    zh = lax.axis_index("zh")
    feed_sums = take(zh).astype(f32) + swapped(take(1 - zh), "zh").astype(f32)

    over_z = swapped(branch, "zl")
    mine, other = feed_out(after(hidden, branch), feed)
    branch_blocks = tp_gather(branch, after(over_z, other))
    mine, from_core, from_z, _ = tp_scatter(mine, other)
    output = middle + mine[0].astype(f32) + from_core[0].astype(f32) + from_z.astype(f32)
    output = output.astype(bf16)

    grads, mine, other, branch_rows, gain_part, head_part = backward_attention(
        place, branch_blocks, token_blocks, weights, low, att, totals, qraw, kraw, cos, sin, head_gains
    )
    projection_grads = projection_weights(
        first, branch_rows, grads, att, gain_part, feed_gain_part, head_part
    )
    mine, from_core, from_z, _ = tp_scatter(mine, other)
    tokens_grad = tokens_back(
        x, mine, from_core, after(from_z, projection_grads), grad_middle, gains
    )
    sums = summed_rows(after(sent_rows(projection_grads), tokens_grad, output, feed_sums))

    gain_sums = sums[:, nq + 2 * nk + nq :]
    over_z = swapped(gain_sums, "zl")
    gain_sums = gain_sums + over_z + (swapped(gain_sums, "core") + swapped(over_z, "core"))

    return (
        output[None],
        tokens_grad[None],
        gain_sums[:, 0],
        sums[:, :nq],
        sums[:, nq : nq + nk],
        sums[:, nq + nk : nq + 2 * nk],
        gain_sums[:heads, 2],
        gain_sums[:heads, 3],
        sums[:, nq + 2 * nk : nq + 2 * nk + nq],
        gain_sums[:, 1],
        feed_sums[:, :units],
        feed_sums[:, units : 2 * units],
        feed_sums[:, 2 * units :],
    )


def solution(mesh):
    fsdp, tp = mesh.devices.shape
    cut = {32: (4, 4, 2), 2: (1, 1, 2), 1: (1, 1, 1)}[fsdp]
    fine = Mesh(mesh.devices.reshape(*cut, 2, tp // 2), EVERY)
    split = ("zl", "core")
    data = P(FSDP, split, None)
    matrix = P(FSDP, split)
    vector = P(FSDP)
    return jax.shard_map(
        local,
        mesh=fine,
        in_specs=(
            data, vector, matrix, matrix, matrix, vector, vector,
            matrix, vector, matrix, matrix, matrix, data,
        ),
        out_specs=(
            data, data, vector, matrix, matrix, matrix, vector, vector,
            matrix, vector, matrix, matrix, matrix,
        ),
        check_vma=False,
    )
```

```python
import functools
import math

import jax
import jax.numpy as jnp
import numpy as np
from jax import lax
from jax.experimental import pallas as pl
from jax.experimental.pallas import tpu as pltpu
from jax.sharding import Mesh, PartitionSpec as P

HD = 128
ROWS = 256
WIDTH = 1024
GROUP = 2
CHUNK = 256
BLOCK_ORDER = (0, 2, 1, 3)
epsilon = 1e-06
rope_base = 1000000.0
score_scale = 1.0 / math.sqrt(HD)
log2_scale = score_scale / math.log(2.0)
FSDP = ("x", "y", "zh")
PLANE = ("x", "y")
EVERY = ("x", "y", "zh", "zl", "core")
f32 = jnp.float32
bf16 = jnp.bfloat16


def matmul(a, b):
    return lax.dot_general(a, b, (((1,), (0,)), ((), ())), preferred_element_type=f32)


def matmul_t(a, b):
    return lax.dot_general(a, b, (((1,), (1,)), ((), ())), preferred_element_type=f32)


def t_matmul(a, b):
    return lax.dot_general(a, b, (((0,), (0,)), ((), ())), preferred_element_type=f32)


def inverse_rms(values):
    return lax.rsqrt(jnp.mean(values * values, axis=-1, keepdims=True) + epsilon)


def norm_back(values, gain, upstream):
    inverse = inverse_rms(values)
    scaled = gain * upstream
    moment = jnp.mean(scaled * values, axis=-1, keepdims=True)
    grad = inverse * scaled - values * (inverse * inverse * inverse) * moment
    return grad, jnp.sum(upstream * values * inverse, axis=0, keepdims=True)


def far(value):
    return pltpu.with_memory_space_constraint(value, pltpu.HBM)


def params(mib):
    return pltpu.CompilerParams(vmem_limit_bytes=mib * 1024 * 1024)


def cost(flops, nbytes, trans=0):
    return pl.CostEstimate(flops=int(flops / 8), bytes_accessed=int(nbytes / 8), transcendentals=int(trans / 8))


def whole(shape, index=None):
    index = index or (0,) * len(shape)
    return pl.BlockSpec(shape, lambda i, *_: index, pipeline_mode=pl.Buffered(1))


def halves(width):
    return [
        pl.BlockSpec((1, ROWS, width), lambda i: (jnp.minimum(i, 1), 0, 0)),
        pl.BlockSpec((1, ROWS, width), lambda i: (jnp.maximum(i - 2, 0), 0, 0)),
    ]


def whole_out(shape):
    return pl.BlockSpec(shape, lambda i, *_: (0,) * len(shape))


def pick(which, pieces, target):
    for k, piece in enumerate(pieces):

        @pl.when(which == k)
        def _(piece=piece):
            target[...] = piece[...]


def equal_iota(rows, cols, make):
    r = lax.broadcasted_iota(jnp.int32, (rows, cols), 0)
    c = lax.broadcasted_iota(jnp.int32, (rows, cols), 1)
    return make(r, c)


def row_of(columns, k):
    same = equal_iota(128, 128, lambda r, c: r == c)
    parts = []
    for m in range(columns.shape[0] // 128):
        col = columns[m * 128 : (m + 1) * 128, k : k + 1].astype(f32)
        parts.append(jnp.sum(jnp.where(same, col, 0.0), axis=0, keepdims=True))
    return jnp.concatenate(parts, axis=1)


def of_head(rows, per_device, first_row=0):
    held = HD * per_device // WIDTH
    return equal_iota(
        rows, HD, lambda r, c: ((r + first_row) // per_device * held + (r + first_row) % per_device == c)
        & ((r + first_row) % per_device < held)
    )


def heads_of(columns, k, per_device):
    col = columns[:, k : k + 1].astype(f32)
    return jnp.sum(jnp.where(of_head(columns.shape[0], per_device), col, 0.0), axis=0, keepdims=True)


def put_pair(which, value, mine, other):
    top, bottom = value[:ROWS], value[ROWS:]

    @pl.when(which < 2)
    def _():
        mine[0] = top
        other[0] = bottom

    @pl.when(which >= 2)
    def _():
        mine[0] = bottom
        other[0] = top


def put(which, value, mine, other):
    @pl.when(which < 2)
    def _():
        mine[0] = value

    @pl.when(which >= 2)
    def _():
        other[0] = value


def forward_attention_kernel(per_device, n_pieces, place, order, *refs):
    tokens = refs[:4]
    pieces, refs = refs[4 : 4 + n_pieces], refs[4 + n_pieces :]
    cos, sin = refs[:2]
    first, qraw, kraw, low, att, totals, mine, other, gains, head_gains, ordered = refs[2:13]
    rows, keys, values, weights, piece_sems, ordered_sem = refs[13:]
    i = pl.program_id(0)
    nq, nqkv = qraw.shape[1], low.shape[1]
    wqkv = weights.at[:, :nqkv]
    wo = weights.at[:, nqkv : nqkv + nq]
    columns = weights.at[:, nqkv + nq :]
    keep = pltpu.make_async_copy(weights, ordered, ordered_sem)

    @pl.when(i == 0)
    def _():
        for copy in load_pieces(order, pieces, weights, piece_sems):
            copy.wait()
        keep.start()
        gains[:2, :] = jnp.concatenate([row_of(columns, 0), row_of(columns, 1)], axis=0)
        gains[2:, :] = jnp.zeros_like(gains[2:, :])
        head_gains[:2, :] = jnp.concatenate([heads_of(columns, k, per_device) for k in (2, 3)], axis=0)
        head_gains[2:, :] = jnp.zeros_like(head_gains[2:, :])

    gain, qgain, kgain = gains[:1, :], head_gains[:1, :], head_gains[1:2, :]
    for a in range(2):
        pick(place[2 * i + a], tokens, rows.at[a * ROWS : (a + 1) * ROWS, :])
    x = rows[...].astype(f32)
    normed = (x * inverse_rms(x) * gain).astype(bf16)
    first[...] = normed
    qkv = matmul(normed, wqkv[...])
    nq, nk = qraw.shape[1], kraw.shape[1]
    qraw[...] = qkv[:, :nq]
    kraw[...] = qkv[:, nq : nq + nk]
    here = pl.ds(pl.multiple_of(i * 2 * ROWS, 2 * ROWS), 2 * ROWS)
    c, s = cos[...], sin[...]

    def turned(v, g):
        n = v * inverse_rms(v) * g
        return (n * c + pltpu.roll(n, HD // 2, 1) * s).astype(bf16)

    for h in range(nk // HD):
        k_low = turned(qkv[:, nq + h * HD : nq + (h + 1) * HD], kgain)
        v_low = qkv[:, nq + nk + h * HD : nq + nk + (h + 1) * HD].astype(bf16)
        low[:, nq + h * HD : nq + (h + 1) * HD] = k_low
        low[:, nq + nk + h * HD : nq + nk + (h + 1) * HD] = v_low
        keys[h, here, :] = k_low
        values[h, here, :HD] = v_low
        values[h, here, HD:] = jnp.ones((2 * ROWS, HD), bf16)
    for h in range(nq // HD):
        low[:, h * HD : (h + 1) * HD] = turned(qkv[:, h * HD : (h + 1) * HD], qgain)
    mask_q = lax.broadcasted_iota(jnp.int32, (GROUP * ROWS, ROWS), 0) % ROWS
    mask_k = lax.broadcasted_iota(jnp.int32, (GROUP * ROWS, ROWS), 1)

    def attend(block):
        half = block % 2 * ROWS
        n = block * ROWS
        sums = []
        for h in range(nk // HD):
            cols = [(h * GROUP + a) * HD for a in range(GROUP)]
            q2 = jnp.concatenate([low[half : half + ROWS, col : col + HD] for col in cols], axis=0)
            scores = matmul_t(q2, keys[h, : n + ROWS, :]) * log2_scale
            weights = jnp.exp2(scores[:, n:])
            weights = jnp.where(mask_k <= mask_q, weights, 0.0).astype(bf16)
            if n:
                weights = jnp.concatenate([jnp.exp2(scores[:, :n]).astype(bf16), weights], axis=1)
            acc = matmul(weights, values[h, : n + ROWS, :])
            total = acc[:, HD:]
            o = (acc[:, :HD] / total).astype(bf16)
            for a, col in enumerate(cols):
                att[half : half + ROWS, col : col + HD] = o[a * ROWS : (a + 1) * ROWS]
            sums.append(jnp.log2(total).T[:1, :])
        sums = jnp.concatenate(sums + [jnp.zeros((8 - len(sums), GROUP * ROWS), f32)], axis=0)
        totals[block % 2] = sums

    for k in range(2):

        @pl.when(i == k)
        def _(k=k):
            attend(2 * k)
            attend(2 * k + 1)

    put_pair(place[2 * i], matmul_t(att[...], wo[...]).astype(bf16), mine, other)

    @pl.when(i == pl.num_programs(0) - 1)
    def _():
        keep.wait()


def forward_attention(place, order, tokens, pieces, nq, nk, cos, sin):
    n, width = 4, tokens[0].shape[1]
    length = n * ROWS
    nqkv = nq + 2 * nk
    row = lambda cols: pl.BlockSpec((2 * ROWS, cols), lambda i, p, o: (i, 0))
    out = [
        ((length, width), bf16, row(width)),
        ((length, nq), f32, row(nq)),
        ((length, nk), f32, row(nk)),
        ((length, nqkv), bf16, row(nqkv)),
        ((length, nq), bf16, row(nq)),
        ((n, 8, GROUP * ROWS), f32, pl.BlockSpec((2, 8, GROUP * ROWS), lambda i, p, o: (i, 0, 0))),
        *[((2, ROWS, width), bf16, pl.BlockSpec((1, ROWS, width), lambda i, p, o: (p[2 * i] % 2, 0, 0)))] * 2,
        ((8, width), f32, whole_out((8, width))),
        ((8, HD), f32, whole_out((8, HD))),
        ((width, nqkv + nq + HD), bf16, pl.BlockSpec(memory_space=pltpu.HBM)),
    ]
    return pl.pallas_call(
        functools.partial(forward_attention_kernel, width // lax.axis_size(FSDP), len(pieces)),
        grid_spec=pltpu.PrefetchScalarGridSpec(
            num_scalar_prefetch=2,
            grid=(n // 2,),
            in_specs=[
                *[whole((ROWS, width))] * 4,
                *[pl.BlockSpec(memory_space=pl.ANY)] * len(pieces),
                row(HD),
                row(HD),
            ],
            out_specs=[o[2] for o in out],
            scratch_shapes=[
                pltpu.VMEM((2 * ROWS, width), bf16),
                pltpu.VMEM((nk // HD, length, HD), bf16),
                pltpu.VMEM((nk // HD, length, 2 * HD), bf16),
                pltpu.VMEM((width, nqkv + nq + HD), bf16),
                pltpu.SemaphoreType.DMA(order.shape),
                pltpu.SemaphoreType.DMA,
            ],
        ),
        out_shape=[(pltpu.HBM if k < 6 or k == 10 else jax.ShapeDtypeStruct)(o[0], o[1]) for k, o in enumerate(out)],
        compiler_params=params(40),
        cost_estimate=cost(7e9, 16e6, 3e6),
        name="forward_attention",
    )(place, order, far(tokens[0]), *tokens[1:], *pieces, far(cos), far(sin))


def middle_kernel(tokens, mine, from_core, from_z, gain, middle, second):
    total = mine[...].astype(f32) + from_core[...].astype(f32) + from_z[...].astype(f32)
    v = tokens[...].astype(f32) + total
    middle[...] = v
    second[...] = (v * inverse_rms(v) * gain[1:2, :]).astype(bf16)


def middle_step(tokens, part, from_core, from_z, gain):
    width = tokens.shape[1]
    half = ROWS // 2
    row = pl.BlockSpec((half, width), lambda i: (i, 0))
    first = pl.BlockSpec((None, half, width), lambda i: (0, i, 0))
    return pl.pallas_call(
        middle_kernel,
        grid=(2,),
        in_specs=[row, first, first, row, whole((8, width))],
        out_specs=[row, row],
        out_shape=[pltpu.HBM((ROWS, width), f32), jax.ShapeDtypeStruct((ROWS, width), bf16)],
        compiler_params=params(12),
        cost_estimate=cost(2e6, 4e6),
        name="middle_step",
    )(far(tokens), part, from_core, from_z, gain)


def feed_kernel(*refs):
    second, grads, weights = refs[:2], refs[2:4], refs[4]
    hidden, grad_units, mine, other = refs[5:9]
    rows_s, rows_g, matrices, row_sems, matrix_sems = refs[9:]
    units = hidden.shape[1]
    loads = []
    for k in range(2):
        at = slice(k * ROWS, (k + 1) * ROWS)
        loads.append(pltpu.make_async_copy(second[k], rows_s.at[at, :], row_sems.at[0, k]))
        loads.append(pltpu.make_async_copy(grads[k], rows_g.at[at, :], row_sems.at[1, k]))
    chunks = []
    for c in range(units // CHUNK):
        for m in range(3):
            some = slice(m * units + c * CHUNK, m * units + (c + 1) * CHUNK)
            chunks.append(
                pltpu.make_async_copy(weights.at[:, some], matrices.at[:, some], matrix_sems.at[m, c])
            )
    for copy in loads + chunks:
        copy.start()
    for copy in loads:
        copy.wait()
    s, g = rows_s[...], rows_g[...]
    for c, at in enumerate(range(0, units, CHUNK)):
        for copy in chunks[3 * c : 3 * c + 3]:
            copy.wait()
        gate = matmul(s, matrices[:, at : at + CHUNK])
        up = matmul(s, matrices[:, units + at : units + at + CHUNK])
        gh = matmul(g, matrices[:, 2 * units + at : 2 * units + at + CHUNK])
        sig = 0.5 * jnp.tanh(0.5 * gate) + 0.5
        swish = gate * sig
        hidden[:, at : at + CHUNK] = (swish * up).astype(bf16)
        grad_units[:, at : at + CHUNK] = (gh * up * (sig + swish * (1.0 - sig))).astype(bf16)
        grad_units[:, units + at : units + at + CHUNK] = (gh * swish).astype(bf16)
    part = matmul_t(grad_units[...], matrices[:, : 2 * units]).astype(bf16)
    mine[...] = part[:ROWS]
    other[...] = part[ROWS:]


def feed_step(second, grads, weights, units):
    width = second[0].shape[1]
    return pl.pallas_call(
        feed_kernel,
        in_specs=[pl.BlockSpec(memory_space=pl.ANY)] * 5,
        out_shape=[
            pltpu.HBM((2 * ROWS, units), bf16),
            pltpu.HBM((2 * ROWS, 2 * units), bf16),
            *[jax.ShapeDtypeStruct((ROWS, width), bf16)] * 2,
        ],
        scratch_shapes=[
            *[pltpu.VMEM((2 * ROWS, width), bf16)] * 2,
            pltpu.VMEM((width, 3 * units), bf16),
            pltpu.SemaphoreType.DMA((2, 2)),
            pltpu.SemaphoreType.DMA((3, units // CHUNK)),
        ],
        compiler_params=params(32),
        cost_estimate=cost(4e9, 8e6, 1e6),
        name="feed_step",
    )(*second, *map(far, grads), far(weights))


def feed_out_kernel(first, then, wd, mine, other):
    for k, hidden in enumerate((first, then)):

        @pl.when(pl.program_id(0) == k)
        def _(hidden=hidden):
            part = matmul_t(hidden[...], wd[...]).astype(bf16)
            mine[0] = part[:ROWS]
            other[0] = part[ROWS:]


def feed_out(hidden, weights):
    pair, units = hidden[0].shape
    width = weights.shape[0]
    block = pl.BlockSpec((1, ROWS, width), lambda i: (i, 0, 0))
    return pl.pallas_call(
        feed_out_kernel,
        grid=(2,),
        in_specs=[whole((pair, units)), whole((pair, units)), whole((width, units), (0, 2))],
        out_specs=[block, block],
        out_shape=[jax.ShapeDtypeStruct((2, ROWS, width), bf16)] * 2,
        compiler_params=params(20),
        cost_estimate=cost(1.6e9, 5e6),
        name="feed_out",
    )(*map(far, hidden), far(weights))


def feed_weights_kernel(*refs):
    second, grads, grad_units, hidden = refs[:4], refs[4:8], refs[8:10], refs[10:12]
    out, rows_s, rows_g = refs[12:]
    wide = grad_units[0].shape[1]
    pair = 2 * ROWS
    for k, block in enumerate(BLOCK_ORDER):
        rows_s[k * ROWS : (k + 1) * ROWS, :] = second[block][...]
        rows_g[k * ROWS : (k + 1) * ROWS, :] = grads[block][...]
    both = lambda rows, others: sum(
        t_matmul(rows[k * pair : (k + 1) * pair, :], other[...]) for k, other in enumerate(others)
    )
    out[:, :wide] = both(rows_s, grad_units).astype(bf16)
    out[:, wide:] = both(rows_g, hidden).astype(bf16)


def feed_weights(second, grads, grad_units, hidden):
    width = second[0].shape[1]
    pair, wide = grad_units[0].shape
    units = hidden[0].shape[1]
    return pl.pallas_call(
        feed_weights_kernel,
        grid=(width // 512,),
        in_specs=[
            *[pl.BlockSpec((ROWS, 512), lambda i: (0, i))] * 8,
            *[whole((pair, wide))] * 2,
            *[whole((pair, units))] * 2,
        ],
        out_specs=pl.BlockSpec((512, wide + units), lambda i: (i, 0)),
        out_shape=pltpu.HBM((width, wide + units), bf16),
        scratch_shapes=[pltpu.VMEM((2 * pair, 512), bf16)] * 2,
        compiler_params=params(36),
        cost_estimate=cost(4.8e9, 14e6),
        name="feed_weights",
    )(*map(far, second), *map(far, grads), *map(far, grad_units), *map(far, hidden))


def middle_back_kernel(middle, mine, from_core, from_z, cotangent, gain, grad_middle, branch, gain_part):
    u = mine[...].astype(f32) + from_core[...].astype(f32) + from_z[...].astype(f32)
    grad, part = norm_back(middle[...], gain[1:2, :], u)
    grad = cotangent[...].astype(f32) + grad
    grad_middle[...] = grad
    branch[...] = grad.astype(bf16)

    @pl.when(pl.program_id(0) == 0)
    def _():
        gain_part[...] = jnp.zeros_like(gain_part)

    gain_part[:1, :] += part


def middle_back(middle, part, from_core, from_z, cotangent, gain):
    width = middle.shape[1]
    half = ROWS // 2
    row = pl.BlockSpec((half, width), lambda i: (i, 0))
    return pl.pallas_call(
        middle_back_kernel,
        grid=(2,),
        in_specs=[row, row, row, row, row, whole((8, width))],
        out_specs=[row, row, whole_out((8, width))],
        out_shape=[
            pltpu.HBM((ROWS, width), f32),
            jax.ShapeDtypeStruct((ROWS, width), bf16),
            pltpu.HBM((8, width), f32),
        ],
        compiler_params=params(14),
        cost_estimate=cost(4e6, 5e6),
        name="middle_back",
    )(far(middle), part, from_core, from_z, far(cotangent), gain)


def backward_attention_kernel(place, *refs):
    branch = refs[:4]
    tokens = refs[4:8]
    weights, low, att, totals, qraw, kraw, cos, sin, head_gains = refs[8:17]
    grads, mine, other, branch_out, gain_part, head_part = refs[17:23]
    matrices, rows_all, xs_all, grad_att, dk, dv, dq, row_sems, matrix_sems = refs[23:]
    qgain, kgain = head_gains[:1, :], head_gains[1:2, :]
    step_id = pl.program_id(0)
    i = pl.num_programs(0) - 1 - step_id
    nq, nk = qraw.shape[1], kraw.shape[1]

    @pl.when(step_id == 0)
    def _():
        gain_part[...] = jnp.zeros_like(gain_part)
        head_part[...] = jnp.zeros_like(head_part)

    nqkv = nq + 2 * nk
    wqkv = matrices.at[:, :nqkv]
    wo = matrices.at[:, nqkv:]
    load_o = pltpu.make_async_copy(weights.at[:, nqkv : nqkv + nq], wo, matrix_sems.at[0])
    load_qkv = pltpu.make_async_copy(weights.at[:, :nqkv], wqkv, matrix_sems.at[1])
    loads = []
    for pieces, target, sem in ((branch, rows_all, row_sems.at[0]), (tokens, xs_all, row_sems.at[1])):
        for k, piece in enumerate(pieces):
            at = pl.ds(pl.multiple_of(place[4 + k] * ROWS, ROWS), ROWS)
            loads.append(pltpu.make_async_copy(piece, target.at[at, :], sem.at[k]))

    @pl.when(step_id == 0)
    def _():
        for copy in [load_o, *loads[:4], load_qkv, *loads[4:]]:
            copy.start()
        for copy in [load_o, *loads[:4]]:
            copy.wait()

    here = pl.ds(pl.multiple_of(i * 2 * ROWS, 2 * ROWS), 2 * ROWS)
    branch_out[...] = rows_all[here, :]
    grad_att[...] = matmul(rows_all[here, :], wo[...]).astype(bf16)
    mask_k = lax.broadcasted_iota(jnp.int32, (ROWS, GROUP * ROWS), 0)
    mask_q = lax.broadcasted_iota(jnp.int32, (ROWS, GROUP * ROWS), 1) % ROWS

    def attend_back(block):
        half = block % 2 * ROWS
        n = block * ROWS
        end = n + ROWS
        for h in range(nk // HD):
            cols = [(h * GROUP + a) * HD for a in range(GROUP)]
            q2 = jnp.concatenate([low[n:end, col : col + HD] for col in cols], axis=0)
            g2 = jnp.concatenate([grad_att[half : half + ROWS, col : col + HD] for col in cols], axis=0)
            o2 = jnp.concatenate([att[half : half + ROWS, col : col + HD] for col in cols], axis=0)
            total = totals[block % 2, h : h + 1, :]
            dot = jnp.sum((g2.astype(f32) * o2.astype(f32)).T, axis=0, keepdims=True)
            k = low[:end, nq + h * HD : nq + (h + 1) * HD]
            v = low[:end, nq + nk + h * HD : nq + nk + (h + 1) * HD]
            probs = jnp.exp2(matmul_t(k, q2) * log2_scale - total)
            last = jnp.where(mask_k <= mask_q, probs[n:], 0.0)
            probs = jnp.concatenate([probs[:n], last], axis=0) if n else last
            grad_scores = (probs * (matmul_t(v, g2) - dot)).astype(bf16)
            dv_part = matmul(probs.astype(bf16), g2)
            dk_part = matmul(grad_scores, q2)
            if end == keys:
                dv[h] = dv_part
                dk[h] = dk_part
            else:
                dv[h, :end, :] += dv_part
                dk[h, :end, :] += dk_part
            d = t_matmul(grad_scores, k) * score_scale
            for a, col in enumerate(cols):
                dq[half : half + ROWS, col : col + HD] = d[a * ROWS : (a + 1) * ROWS]

    keys = low.shape[0]
    for k in range(keys // (2 * ROWS)):

        @pl.when(i == k)
        def _(k=k):
            attend_back(2 * k + 1)
            attend_back(2 * k)

    c, s = cos[...], sin[...]

    def unturned(w):
        return w * c - pltpu.roll(w, HD // 2, 1) * s

    for h in range(nq // HD):
        col = slice(h * HD, (h + 1) * HD)
        grad, gp = norm_back(qraw[:, col], qgain, unturned(dq[:, col]))
        grads[:, col] = grad.astype(bf16)
        head_part[:1, :] += gp
    for h in range(nk // HD):
        col = slice(h * HD, (h + 1) * HD)
        grad, gp = norm_back(kraw[:, col], kgain, unturned(dk[h, here, :] * score_scale))
        grads[:, nq + h * HD : nq + (h + 1) * HD] = grad.astype(bf16)
        head_part[1:2, :] += gp
        grads[:, nq + nk + h * HD : nq + nk + (h + 1) * HD] = dv[h, here, :].astype(bf16)
    @pl.when(step_id == 0)
    def _():
        for copy in [load_qkv, *loads[4:]]:
            copy.wait()

    upstream = matmul_t(grads[...], wqkv[...])
    put_pair(place[2 * i], upstream.astype(bf16), mine, other)
    x = xs_all[here, :].astype(f32)
    gain_part[:1, :] += jnp.sum(upstream * x * inverse_rms(x), axis=0, keepdims=True)


def backward_attention(place, branch, tokens, weights, low, att, totals, qraw, kraw, cos, sin, head_gains):
    n, width = 4, branch[0].shape[1]
    length, nqkv = low.shape
    nq, nk = qraw.shape[1], kraw.shape[1]
    row = lambda cols: pl.BlockSpec((2 * ROWS, cols), lambda i, p: (n // 2 - 1 - i, 0))
    out = [
        ((length, nqkv), bf16, row(nqkv)),
        *[((2, ROWS, width), bf16, pl.BlockSpec((1, ROWS, width), lambda i, p: (p[n - 2 - 2 * i] % 2, 0, 0)))] * 2,
        ((length, width), bf16, row(width)),
        ((8, width), f32, whole_out((8, width))),
        ((8, HD), f32, whole_out((8, HD))),
    ]
    return pl.pallas_call(
        backward_attention_kernel,
        grid_spec=pltpu.PrefetchScalarGridSpec(
            num_scalar_prefetch=1,
            grid=(n // 2,),
            in_specs=[
                *[pl.BlockSpec(memory_space=pl.ANY)] * 9,
                whole((length, nqkv)),
                row(nq),
                pl.BlockSpec((2, 8, GROUP * ROWS), lambda i, p: (n // 2 - 1 - i, 0, 0)),
                row(nq),
                row(nk),
                row(HD),
                row(HD),
                whole((8, HD)),
            ],
            out_specs=[o[2] for o in out],
            scratch_shapes=[
                pltpu.VMEM((width, nqkv + nq), bf16),
                pltpu.VMEM((length, width), bf16),
                pltpu.VMEM((length, width), bf16),
                pltpu.VMEM((2 * ROWS, nq), bf16),
                pltpu.VMEM((nk // HD, length, HD), f32),
                pltpu.VMEM((nk // HD, length, HD), f32),
                pltpu.VMEM((2 * ROWS, nq), f32),
                pltpu.SemaphoreType.DMA((2, 4)),
                pltpu.SemaphoreType.DMA((2,)),
            ],
        ),
        out_shape=[(pltpu.HBM if k in (0, 1, 3) else jax.ShapeDtypeStruct)(o[0], o[1]) for k, o in enumerate(out)],
        compiler_params=params(48),
        cost_estimate=cost(9e9, 18e6, 3e6),
        name="backward_attention",
    )(
        place, *branch, *map(far, tokens), far(weights), far(low), far(att), far(totals),
        far(qraw), far(kraw), far(cos), far(sin), far(head_gains),
    )


def projection_weights_kernel(per_device, first, branch, grads, att, gain, second_gain, heads, out):
    wide = grads.shape[1]
    more = wide + att.shape[1]
    out[:, :wide] = t_matmul(first[...], grads[...]).astype(bf16)
    out[:, wide:more] = t_matmul(branch[...], att[...]).astype(bf16)
    rows = out.shape[0]
    same = equal_iota(rows, rows, lambda r, c: r == c)
    stands = of_head(rows, per_device, pl.program_id(0) * rows)
    lane = lax.broadcasted_iota(jnp.int32, (rows, HD), 1)
    columns = jnp.zeros((rows, HD), f32)
    for k, (mask, values) in enumerate(
        [(same, gain[:1, :]), (same, second_gain[:1, :]), (stands, heads[:1, :]), (stands, heads[1:2, :])]
    ):
        column = jnp.sum(jnp.where(mask, values, 0.0), axis=1, keepdims=True)
        columns = jnp.where(lane == k, column, columns)
    out[:, more:] = columns.astype(bf16)


def projection_weights(first, branch, grads, att, gain, second_gain, heads):
    length, width = first.shape
    wide, nq = grads.shape[1], att.shape[1]
    return pl.pallas_call(
        functools.partial(projection_weights_kernel, width // lax.axis_size(FSDP)),
        grid=(width // 512,),
        in_specs=[
            pl.BlockSpec((length, 512), lambda i: (0, i)),
            pl.BlockSpec((length, 512), lambda i: (0, i)),
            whole((length, wide)),
            whole((length, nq)),
            pl.BlockSpec((8, 512), lambda i: (0, i)),
            pl.BlockSpec((8, 512), lambda i: (0, i)),
            whole((8, HD)),
        ],
        out_specs=pl.BlockSpec((512, wide + nq + HD), lambda i: (i, 0)),
        out_shape=pltpu.HBM((width, wide + nq + HD), bf16),
        compiler_params=params(30),
        cost_estimate=cost(3.2e9, 10e6),
        name="projection_weights",
    )(far(first), far(branch), far(grads), far(att), gain, far(second_gain), heads)


def tokens_back_kernel(tokens, mine, from_core, from_z, grad_middle, gain, grad_tokens):
    u = mine[...].astype(f32) + from_core[...].astype(f32) + from_z[...].astype(f32)
    grad, _ = norm_back(tokens[...].astype(f32), gain[:1, :], u)
    grad_tokens[...] = grad_middle[...] + grad


def tokens_back(tokens, mine, from_core, from_z, grad_middle, gain):
    width = tokens.shape[1]
    half = ROWS // 2
    row = pl.BlockSpec((half, width), lambda i: (i, 0))
    first = pl.BlockSpec((None, half, width), lambda i: (0, i, 0))
    return pl.pallas_call(
        tokens_back_kernel,
        grid=(2,),
        in_specs=[row, first, first, row, row, whole((8, width))],
        out_specs=row,
        out_shape=pltpu.HBM((ROWS, width), f32),
        compiler_params=params(14),
        cost_estimate=cost(4e6, 4e6),
        name="tokens_back",
    )(far(tokens), mine, from_core, from_z, far(grad_middle), far(gain))


def close(zh, parts, summed):
    planes, both, wide = parts.shape
    rows = both // 2
    total = wide + summed.shape[1]

    def kernel(zh, parts, summed, keep, give):
        for which, out in ((zh[0], keep), (1 - zh[0], give)):
            at = pl.ds(pl.multiple_of(which * rows, rows), rows)
            added = parts[0, at, :].astype(f32)
            for k in range(1, planes):
                added = added + parts[k, at, :].astype(f32)
            out[:, :wide] = added.astype(out.dtype)
            out[:, wide:] = summed[at, :].astype(out.dtype)

    return pl.pallas_call(
        kernel,
        grid_spec=pltpu.PrefetchScalarGridSpec(
            num_scalar_prefetch=1,
            grid=(1,),
            in_specs=[whole(parts.shape), whole(summed.shape)],
            out_specs=[whole_out((rows, total))] * 2,
        ),
        out_shape=[
            jax.ShapeDtypeStruct((rows, total), f32),
            jax.ShapeDtypeStruct((rows, total), bf16),
        ],
        compiler_params=params(14),
        cost_estimate=cost(2e6, 4e6),
        name="close",
    )(zh, parts, summed)


def finish(keep, arrived, widths):
    rows = keep.shape[0]

    def kernel(keep, arrived, *outs):
        at = 0
        for out in outs:
            some = slice(at, at + out.shape[1])
            out[...] = keep[:, some] + arrived[:, some].astype(f32)
            at += out.shape[1]

    return pl.pallas_call(
        kernel,
        out_shape=[jax.ShapeDtypeStruct((rows, w), f32) for w in widths],
        compiler_params=params(8),
        cost_estimate=cost(1e5, 1e6),
        name="finish",
    )(keep, arrived)


def finish_gains(parts, rows, heads):
    def kernel(*refs):
        total = refs[0][...] + refs[1][...] + refs[2][...] + refs[3][...]
        same = equal_iota(rows, rows, lambda r, c: r == c)
        for k, out in enumerate(refs[4:]):
            line = jnp.sum(jnp.where(same, total[:, k : k + 1], 0.0), axis=0, keepdims=True)
            out[...] = line[:, : out.shape[1]]

    widths = (rows, rows, heads, heads)
    outs = pl.pallas_call(
        kernel,
        out_shape=[jax.ShapeDtypeStruct((1, w), f32) for w in widths],
        compiler_params=params(4),
        cost_estimate=cost(1e4, 1e5),
        name="finish_gains",
    )(*parts)
    return [out.reshape(-1) for out in outs]


def pack(first, second, gains, rows, heads):
    widths = [a.shape[1] for a in first], [a.shape[1] for a in second]
    split = sum(widths[0])

    def kernel(gains, *refs):
        out = refs[-1]
        at = 0
        for k, ref in enumerate(refs[:-1]):
            at += HD * (k == len(first))
            out[:, at : at + ref.shape[1]] = ref[...]
            at += ref.shape[1]
        g = gains[...].astype(f32)
        lane = lax.broadcasted_iota(jnp.int32, (rows, HD), 1)
        line = lax.broadcasted_iota(jnp.int32, (rows, HD), 0)
        columns = jnp.zeros((rows, HD), f32)
        places = [(0, rows), (rows, rows), (2 * rows, heads), (2 * rows + heads, heads)]
        for k, (start, count) in enumerate(places):
            mask = (lane == line + start) & (line < count)
            column = jnp.sum(jnp.where(mask, g, 0.0), axis=1, keepdims=True)
            columns = jnp.where(lane == k, column, columns)
        out[:, split : split + HD] = columns.astype(bf16)

    return pl.pallas_call(
        kernel,
        out_shape=jax.ShapeDtypeStruct((rows, split + HD + sum(widths[1])), bf16),
        compiler_params=params(8),
        cost_estimate=cost(1e3, 5e5),
        name="pack",
    )(gains, *map(far, first), *map(far, second))


def pair(zh, shard, other, cut, split):
    rows, wide = shard.shape

    def kernel(zh, shard, other, left, right, rest):
        for k, ref in enumerate((shard, other)):
            left[k] = ref[:, :cut]
            right[k] = ref[:, cut:split]
            rest[pl.ds(pl.multiple_of((zh[0] ^ k) * rows, rows), rows), :] = ref[:, split:]

    shapes = [(2, rows, cut), (2, rows, split - cut), (2 * rows, wide - split)]
    return pl.pallas_call(
        kernel,
        grid_spec=pltpu.PrefetchScalarGridSpec(
            num_scalar_prefetch=1,
            grid=(1,),
            in_specs=[whole((rows, wide))] * 2,
            out_specs=[whole_out(s) for s in shapes],
        ),
        out_shape=[
            *[jax.ShapeDtypeStruct(s, bf16) for s in shapes[:2]],
            pltpu.HBM(shapes[2], bf16),
        ],
        compiler_params=params(8),
        cost_estimate=cost(1e3, 1e6),
        name="pair",
    )(zh, shard, other)


def load_pieces(order, pieces, target, semaphores):
    copies = []
    half = len(pieces) // 2
    cut = pieces[0].shape[3]
    for side in range(2):
        n = 0
        for piece in pieces[side * half : (side + 1) * half]:
            rows, wide = piece.shape[2:]
            for j in range(piece.shape[0]):
                for k in range(2):
                    place = pl.multiple_of(order[side, n] * rows, rows)
                    copy = pltpu.make_async_copy(
                        piece.at[j, k],
                        target.at[pl.ds(place, rows), side * cut : side * cut + wide],
                        semaphores.at[side, n],
                    )
                    copy.start()
                    copies.append(copy)
                    n += 1
    return copies


def swapped(value, axis):
    return lax.ppermute(value, axis, [(0, 1), (1, 0)])


def tp_gather(own, over_z=None):
    over_z = swapped(own, "zl") if over_z is None else over_z
    return [own, over_z, swapped(own, "core"), swapped(over_z, "core")]


def tp_scatter(mine, other):
    from_core = swapped(other, "core")
    passed = (mine[1].astype(f32) + from_core[1].astype(f32)).astype(bf16)
    return mine, from_core, swapped(passed, "zl"), passed


def after(value, *others):
    return lax.optimization_barrier((value, *others))[0]


def sent_rows(part):
    planes = lax.axis_size(PLANE)
    blocks = part.reshape(planes, part.shape[0] // planes, part.shape[1])
    return lax.all_to_all(blocks, PLANE, 0, 0, tiled=True)


def by_distance(sides):
    done = [{0: own} for own, _ in sides]
    before = []
    for near in (True, False):
        arrived = []
        for kept, (own, axis) in zip(done, sides):
            n = lax.axis_size(axis)
            for j in range(1, n):
                if (j in (1, n - 1)) == near:
                    perm = [(s, (s - j) % n) for s in range(n)]
                    kept[j] = lax.ppermute(after(own, *before) if before else own, axis, perm)
                    arrived.append(kept[j])
        before = arrived
    return [[kept[j] for j in sorted(kept)] for kept in done]


def gathered_order():
    nx, ny = lax.axis_size("x"), lax.axis_size("y")
    x, y = (lax.axis_index("x") + jnp.arange(nx)) % nx, (lax.axis_index("y") + jnp.arange(ny)) % ny
    z = lax.axis_index("zh") ^ jnp.arange(2)
    block = lambda x, y: ((x * ny + y) * 2 + z).reshape(-1)
    left = block(x[None, :, None], y[:, None, None])
    right = block(x[:, None, None], y[None, :, None])
    return jnp.stack([left, right]).astype(jnp.int32)


def rotary_tables(length):
    midway = HD // 2
    frequency = 1.0 / rope_base ** (np.arange(midway) * 2.0 / HD)
    angles = np.arange(length)[:, None] * frequency[None, :]
    cos, sin = np.cos(angles), np.sin(angles)
    tables = np.concatenate([cos, cos], axis=1), np.concatenate([-sin, sin], axis=1)
    return [jnp.asarray(t.astype(np.float32)) for t in tables]


def local(
    tokens,
    attention_gain,
    query_weight,
    key_weight,
    value_weight,
    query_gain,
    key_gain,
    output_weight,
    feed_gain,
    gate_weight,
    up_weight,
    down_weight,
    cotangent,
):
    width = tokens.shape[2]
    nq, nk = query_weight.shape[1], key_weight.shape[1]
    units = gate_weight.shape[1]
    rows = query_weight.shape[0]
    x = tokens[0]
    dy = cotangent[0]
    zl, core = lax.axis_index("zl"), lax.axis_index("core")
    block = jnp.arange(4, dtype=jnp.int32)
    place = ((block % 2) ^ core) * 2 + ((block // 2) ^ zl)
    block_of = ((block // 2) ^ core) + ((block % 2) ^ zl) * 2
    place = jnp.concatenate([place, block_of]).astype(jnp.int32)
    cos, sin = rotary_tables(4 * ROWS)

    heads = query_gain.shape[0]
    gains = jnp.concatenate([attention_gain, feed_gain, query_gain, key_gain])
    gains = jnp.pad(gains, (0, HD - gains.shape[0]))[None]
    shard = pack(
        [query_weight, key_weight, value_weight, output_weight],
        [gate_weight, up_weight, down_weight],
        gains,
        rows,
        heads,
    )
    over_zh = swapped(shard, "zh")
    split = nq + 2 * nk + nq + HD
    left, right, feed = pair(lax.axis_index("zh").reshape(1), shard, over_zh, nq + nk, split)
    order = gathered_order()
    left, right = by_distance([(left, "x"), (right, "y")])
    token_blocks = tp_gather(after(x, over_zh))
    left, right = by_distance([(jnp.stack(left), "y"), (jnp.stack(right), "x")])
    feed = lax.all_gather(after(feed, left[1], left[-1], right[1], right[-1]), PLANE, axis=0, tiled=True)
    grads_over_z = swapped(after(dy, *left, *right), "zl")

    first, qraw, kraw, low, att, totals, mine, other, gains, head_gains, weights = forward_attention(
        place, order, token_blocks, left + right, nq, nk, cos, sin
    )
    grad_blocks = tp_gather(dy, after(grads_over_z, other))
    other = after(other, grads_over_z)
    mine, from_core, from_z, _ = tp_scatter(mine, other)
    middle, second = middle_step(x, mine, from_core, from_z, gains)
    over_z = swapped(second, "zl")
    near = feed_step([second, swapped(second, "core")], grad_blocks[::2], feed, units)
    second_blocks = tp_gather(second, after(over_z, near[1]))
    far_ones = feed_step(second_blocks[1::2], grad_blocks[1::2], feed, units)
    hidden, grad_units = [near[0], far_ones[0]], [near[1], far_ones[1]]
    from_core = swapped(near[3], "core")
    passed = (after(far_ones[2], from_core).astype(f32) + swapped(far_ones[3], "core").astype(f32)).astype(bf16)
    from_z = swapped(passed, "zl")
    grad_units[0] = after(grad_units[0], passed)
    feed_grads = feed_weights(second_blocks, grad_blocks, grad_units, hidden)
    from_z, feed_grads = lax.optimization_barrier((from_z, feed_grads))
    grad_middle, branch, feed_gain_part = middle_back(middle, near[2], from_core, from_z, dy, gains)
    feed_sums = lax.psum_scatter(feed_grads, "x", scatter_dimension=0, tiled=True)
    feed_sums = lax.psum_scatter(feed_sums, "y", scatter_dimension=0, tiled=True)
    over_z = swapped(branch, "zl")
    mine, other = feed_out([after(hidden[0], branch), hidden[1]], feed)
    branch_blocks = tp_gather(branch, after(over_z, other))
    mine, from_core, from_z, _ = tp_scatter(mine, other)
    output = middle + mine[0].astype(f32) + from_core[0].astype(f32) + from_z.astype(f32)
    output = output.astype(bf16)

    grads, mine, other, branch_rows, gain_part, head_part = backward_attention(
        place, branch_blocks, token_blocks, weights, low, att, totals, qraw, kraw, cos, sin, head_gains
    )
    projection_grads = projection_weights(
        first, branch_rows, grads, att, gain_part, feed_gain_part, head_part
    )
    mine, from_core, from_z, _ = tp_scatter(mine, other)
    tokens_grad = tokens_back(
        x, mine, from_core, after(from_z, projection_grads), grad_middle, gains
    )
    parts = after(sent_rows(projection_grads), tokens_grad, output)
    keep, give = close(lax.axis_index("zh").reshape(1), parts, after(feed_sums, tokens_grad, output))
    widths = (nq, nk, nk, nq, HD, units, units, units)
    query, key, value, out, columns, gate, up, down = finish(keep, swapped(give, "zh"), widths)
    both = ("zl", "core")
    across = lax.ppermute(columns, both, [(s, 3 - s) for s in range(4)])
    parts = (columns, swapped(columns, "zl"), swapped(columns, "core"), across)
    first_sum, second_sum, query_sum, key_sum = finish_gains(parts, rows, heads)

    return (
        output[None],
        tokens_grad[None],
        first_sum,
        query,
        key,
        value,
        query_sum,
        key_sum,
        out,
        second_sum,
        gate,
        up,
        down,
    )


def solution(mesh):
    fsdp, tp = mesh.devices.shape
    cut = {32: (4, 4, 2), 2: (1, 1, 2), 1: (1, 1, 1)}[fsdp]
    fine = Mesh(mesh.devices.reshape(*cut, 2, tp // 2), EVERY)
    split = ("zl", "core")
    data = P(FSDP, split, None)
    matrix = P(FSDP, split)
    vector = P(FSDP)
    return jax.shard_map(
        local,
        mesh=fine,
        in_specs=(
            data, vector, matrix, matrix, matrix, vector, vector,
            matrix, vector, matrix, matrix, matrix, data,
        ),
        out_specs=(
            data, data, vector, matrix, matrix, matrix, vector, vector,
            matrix, vector, matrix, matrix, matrix,
        ),
        check_vma=False,
    )
```

```python
import functools
import math

import jax
import jax.numpy as jnp
import numpy as np
from jax import lax
from jax.experimental import pallas as pl
from jax.experimental.pallas import tpu as pltpu
from jax.sharding import Mesh, PartitionSpec as P

HD = 128
ROWS = 256
WIDTH = 1024
GROUP = 2
CHUNK = 256
BLOCK_ORDER = (0, 2, 1, 3)
epsilon = 1e-06
rope_base = 1000000.0
score_scale = 1.0 / math.sqrt(HD)
log2_scale = score_scale / math.log(2.0)
FSDP = ("x", "y", "zh")
PLANE = ("x", "y")
EVERY = ("x", "y", "zh", "zl", "core")
f32 = jnp.float32
bf16 = jnp.bfloat16


def matmul(a, b):
    return lax.dot_general(a, b, (((1,), (0,)), ((), ())), preferred_element_type=f32)


def matmul_t(a, b):
    return lax.dot_general(a, b, (((1,), (1,)), ((), ())), preferred_element_type=f32)


def t_matmul(a, b):
    return lax.dot_general(a, b, (((0,), (0,)), ((), ())), preferred_element_type=f32)


def inverse_rms(values):
    return lax.rsqrt(jnp.mean(values * values, axis=-1, keepdims=True) + epsilon)


def norm_back(values, gain, upstream):
    inverse = inverse_rms(values)
    scaled = gain * upstream
    moment = jnp.mean(scaled * values, axis=-1, keepdims=True)
    grad = inverse * scaled - values * (inverse * inverse * inverse) * moment
    return grad, jnp.sum(upstream * values * inverse, axis=0, keepdims=True)


def far(value):
    return pltpu.with_memory_space_constraint(value, pltpu.HBM)


def params(mib):
    return pltpu.CompilerParams(vmem_limit_bytes=mib * 1024 * 1024)


def cost(flops, nbytes, trans=0):
    return pl.CostEstimate(flops=int(flops / 8), bytes_accessed=int(nbytes / 8), transcendentals=int(trans / 8))


def whole(shape, index=None):
    index = index or (0,) * len(shape)
    return pl.BlockSpec(shape, lambda i, *_: index, pipeline_mode=pl.Buffered(1))


def halves(width):
    return [
        pl.BlockSpec((1, ROWS, width), lambda i: (jnp.minimum(i, 1), 0, 0)),
        pl.BlockSpec((1, ROWS, width), lambda i: (jnp.maximum(i - 2, 0), 0, 0)),
    ]


def whole_out(shape):
    return pl.BlockSpec(shape, lambda i, *_: (0,) * len(shape))


def pick(which, pieces, target):
    for k, piece in enumerate(pieces):

        @pl.when(which == k)
        def _(piece=piece):
            target[...] = piece[...]


def equal_iota(rows, cols, make):
    r = lax.broadcasted_iota(jnp.int32, (rows, cols), 0)
    c = lax.broadcasted_iota(jnp.int32, (rows, cols), 1)
    return make(r, c)


def row_of(columns, k):
    same = equal_iota(128, 128, lambda r, c: r == c)
    parts = []
    for m in range(columns.shape[0] // 128):
        col = columns[m * 128 : (m + 1) * 128, k : k + 1].astype(f32)
        parts.append(jnp.sum(jnp.where(same, col, 0.0), axis=0, keepdims=True))
    return jnp.concatenate(parts, axis=1)


def of_head(rows, per_device, first_row=0):
    held = HD * per_device // WIDTH
    return equal_iota(
        rows, HD, lambda r, c: ((r + first_row) // per_device * held + (r + first_row) % per_device == c)
        & ((r + first_row) % per_device < held)
    )


def heads_of(columns, k, per_device):
    col = columns[:, k : k + 1].astype(f32)
    return jnp.sum(jnp.where(of_head(columns.shape[0], per_device), col, 0.0), axis=0, keepdims=True)


def put_pair(which, value, mine, other):
    top, bottom = value[:ROWS], value[ROWS:]

    @pl.when(which < 2)
    def _():
        mine[0] = top
        other[0] = bottom

    @pl.when(which >= 2)
    def _():
        mine[0] = bottom
        other[0] = top


def put(which, value, mine, other):
    @pl.when(which < 2)
    def _():
        mine[0] = value

    @pl.when(which >= 2)
    def _():
        other[0] = value


def forward_attention_kernel(per_device, n_pieces, place, order, *refs):
    tokens = refs[:4]
    pieces, refs = refs[4 : 4 + n_pieces], refs[4 + n_pieces :]
    cos, sin = refs[:2]
    first, qraw, kraw, low, att, totals, mine, other, gains, head_gains, ordered = refs[2:13]
    rows, keys, values, weights, piece_sems, ordered_sem = refs[13:]
    i = pl.program_id(0)
    nq, nqkv = qraw.shape[1], low.shape[1]
    wqkv = weights.at[:, :nqkv]
    wo = weights.at[:, nqkv : nqkv + nq]
    columns = weights.at[:, nqkv + nq :]
    keep = pltpu.make_async_copy(weights, ordered, ordered_sem)

    @pl.when(i == 0)
    def _():
        for copy in load_pieces(order, pieces, weights, piece_sems):
            copy.wait()
        keep.start()
        gains[:2, :] = jnp.concatenate([row_of(columns, 0), row_of(columns, 1)], axis=0)
        gains[2:, :] = jnp.zeros_like(gains[2:, :])
        head_gains[:2, :] = jnp.concatenate([heads_of(columns, k, per_device) for k in (2, 3)], axis=0)
        head_gains[2:, :] = jnp.zeros_like(head_gains[2:, :])

    gain, qgain, kgain = gains[:1, :], head_gains[:1, :], head_gains[1:2, :]
    for a in range(2):
        pick(place[2 * i + a], tokens, rows.at[a * ROWS : (a + 1) * ROWS, :])
    x = rows[...].astype(f32)
    normed = (x * inverse_rms(x) * gain).astype(bf16)
    first[...] = normed
    qkv = matmul(normed, wqkv[...])
    nq, nk = qraw.shape[1], kraw.shape[1]
    qraw[...] = qkv[:, :nq]
    kraw[...] = qkv[:, nq : nq + nk]
    here = pl.ds(pl.multiple_of(i * 2 * ROWS, 2 * ROWS), 2 * ROWS)
    c, s = cos[...], sin[...]

    def turned(v, g):
        n = v * inverse_rms(v) * g
        return (n * c + pltpu.roll(n, HD // 2, 1) * s).astype(bf16)

    for h in range(nk // HD):
        k_low = turned(qkv[:, nq + h * HD : nq + (h + 1) * HD], kgain)
        v_low = qkv[:, nq + nk + h * HD : nq + nk + (h + 1) * HD].astype(bf16)
        low[:, nq + h * HD : nq + (h + 1) * HD] = k_low
        low[:, nq + nk + h * HD : nq + nk + (h + 1) * HD] = v_low
        keys[h, here, :] = k_low
        values[h, here, :HD] = v_low
        values[h, here, HD:] = jnp.ones((2 * ROWS, HD), bf16)
    for h in range(nq // HD):
        low[:, h * HD : (h + 1) * HD] = turned(qkv[:, h * HD : (h + 1) * HD], qgain)
    mask_q = lax.broadcasted_iota(jnp.int32, (GROUP * ROWS, ROWS), 0) % ROWS
    mask_k = lax.broadcasted_iota(jnp.int32, (GROUP * ROWS, ROWS), 1)

    def attend(block):
        half = block % 2 * ROWS
        n = block * ROWS
        sums = []
        for h in range(nk // HD):
            cols = [(h * GROUP + a) * HD for a in range(GROUP)]
            q2 = jnp.concatenate([low[half : half + ROWS, col : col + HD] for col in cols], axis=0)
            scores = matmul_t(q2, keys[h, : n + ROWS, :]) * log2_scale
            weights = jnp.exp2(scores[:, n:])
            weights = jnp.where(mask_k <= mask_q, weights, 0.0).astype(bf16)
            if n:
                weights = jnp.concatenate([jnp.exp2(scores[:, :n]).astype(bf16), weights], axis=1)
            acc = matmul(weights, values[h, : n + ROWS, :])
            total = acc[:, HD:]
            o = (acc[:, :HD] / total).astype(bf16)
            for a, col in enumerate(cols):
                att[half : half + ROWS, col : col + HD] = o[a * ROWS : (a + 1) * ROWS]
            sums.append(jnp.log2(total).T[:1, :])
        sums = jnp.concatenate(sums + [jnp.zeros((8 - len(sums), GROUP * ROWS), f32)], axis=0)
        totals[block % 2] = sums

    for k in range(2):

        @pl.when(i == k)
        def _(k=k):
            attend(2 * k)
            attend(2 * k + 1)

    put_pair(place[2 * i], matmul_t(att[...], wo[...]).astype(bf16), mine, other)

    @pl.when(i == pl.num_programs(0) - 1)
    def _():
        keep.wait()


def forward_attention(place, order, tokens, pieces, nq, nk, cos, sin):
    n, width = 4, tokens[0].shape[1]
    length = n * ROWS
    nqkv = nq + 2 * nk
    row = lambda cols: pl.BlockSpec((2 * ROWS, cols), lambda i, p, o: (i, 0))
    out = [
        ((length, width), bf16, row(width)),
        ((length, nq), f32, row(nq)),
        ((length, nk), f32, row(nk)),
        ((length, nqkv), bf16, row(nqkv)),
        ((length, nq), bf16, row(nq)),
        ((n, 8, GROUP * ROWS), f32, pl.BlockSpec((2, 8, GROUP * ROWS), lambda i, p, o: (i, 0, 0))),
        *[((2, ROWS, width), bf16, pl.BlockSpec((1, ROWS, width), lambda i, p, o: (p[2 * i] % 2, 0, 0)))] * 2,
        ((8, width), f32, whole_out((8, width))),
        ((8, HD), f32, whole_out((8, HD))),
        ((width, nqkv + nq + HD), bf16, pl.BlockSpec(memory_space=pltpu.HBM)),
    ]
    return pl.pallas_call(
        functools.partial(forward_attention_kernel, width // lax.axis_size(FSDP), len(pieces)),
        grid_spec=pltpu.PrefetchScalarGridSpec(
            num_scalar_prefetch=2,
            grid=(n // 2,),
            in_specs=[
                *[whole((ROWS, width))] * 4,
                *[pl.BlockSpec(memory_space=pl.ANY)] * len(pieces),
                row(HD),
                row(HD),
            ],
            out_specs=[o[2] for o in out],
            scratch_shapes=[
                pltpu.VMEM((2 * ROWS, width), bf16),
                pltpu.VMEM((nk // HD, length, HD), bf16),
                pltpu.VMEM((nk // HD, length, 2 * HD), bf16),
                pltpu.VMEM((width, nqkv + nq + HD), bf16),
                pltpu.SemaphoreType.DMA(order.shape),
                pltpu.SemaphoreType.DMA,
            ],
        ),
        out_shape=[(pltpu.HBM if k < 6 or k == 10 else jax.ShapeDtypeStruct)(o[0], o[1]) for k, o in enumerate(out)],
        compiler_params=params(24),
        cost_estimate=cost(7e9, 16e6, 3e6),
        name="forward_attention",
    )(place, order, far(tokens[0]), *tokens[1:], *map(far, pieces), far(cos), far(sin))


def middle_kernel(tokens, mine, from_core, from_z, gain, middle, second):
    total = mine[...].astype(f32) + from_core[...].astype(f32) + from_z[...].astype(f32)
    v = tokens[...].astype(f32) + total
    middle[...] = v
    second[...] = (v * inverse_rms(v) * gain[1:2, :]).astype(bf16)


def middle_step(tokens, part, from_core, from_z, gain):
    width = tokens.shape[1]
    half = ROWS // 2
    row = pl.BlockSpec((half, width), lambda i: (i, 0))
    first = pl.BlockSpec((None, half, width), lambda i: (0, i, 0))
    return pl.pallas_call(
        middle_kernel,
        grid=(2,),
        in_specs=[row, first, first, row, whole((8, width))],
        out_specs=[row, row],
        out_shape=[pltpu.HBM((ROWS, width), f32), jax.ShapeDtypeStruct((ROWS, width), bf16)],
        compiler_params=params(12),
        cost_estimate=cost(2e6, 4e6),
        name="middle_step",
    )(far(tokens), part, from_core, from_z, gain)


def feed_kernel(*refs):
    second, grads, weights = refs[:2], refs[2:4], refs[4]
    hidden, grad_units, mine, other = refs[5:9]
    rows_s, rows_g, matrices, row_sems, matrix_sems = refs[9:]
    units = hidden.shape[1]
    loads = []
    for k in range(2):
        at = slice(k * ROWS, (k + 1) * ROWS)
        loads.append(pltpu.make_async_copy(second[k], rows_s.at[at, :], row_sems.at[0, k]))
        loads.append(pltpu.make_async_copy(grads[k], rows_g.at[at, :], row_sems.at[1, k]))
    chunks = []
    for c in range(units // CHUNK):
        for m in range(3):
            some = slice(m * units + c * CHUNK, m * units + (c + 1) * CHUNK)
            chunks.append(
                pltpu.make_async_copy(weights.at[:, some], matrices.at[:, some], matrix_sems.at[m, c])
            )
    for copy in loads + chunks:
        copy.start()
    for copy in loads:
        copy.wait()
    s, g = rows_s[...], rows_g[...]
    for c, at in enumerate(range(0, units, CHUNK)):
        for copy in chunks[3 * c : 3 * c + 3]:
            copy.wait()
        gate = matmul(s, matrices[:, at : at + CHUNK])
        up = matmul(s, matrices[:, units + at : units + at + CHUNK])
        gh = matmul(g, matrices[:, 2 * units + at : 2 * units + at + CHUNK])
        sig = 0.5 * jnp.tanh(0.5 * gate) + 0.5
        swish = gate * sig
        hidden[:, at : at + CHUNK] = (swish * up).astype(bf16)
        grad_units[:, at : at + CHUNK] = (gh * up * (sig + swish * (1.0 - sig))).astype(bf16)
        grad_units[:, units + at : units + at + CHUNK] = (gh * swish).astype(bf16)
    part = matmul_t(grad_units[...], matrices[:, : 2 * units]).astype(bf16)
    mine[...] = part[:ROWS]
    other[...] = part[ROWS:]


def feed_step(second, grads, weights, units):
    width = second[0].shape[1]
    return pl.pallas_call(
        feed_kernel,
        in_specs=[pl.BlockSpec(memory_space=pl.ANY)] * 5,
        out_shape=[
            pltpu.HBM((2 * ROWS, units), bf16),
            pltpu.HBM((2 * ROWS, 2 * units), bf16),
            *[jax.ShapeDtypeStruct((ROWS, width), bf16)] * 2,
        ],
        scratch_shapes=[
            *[pltpu.VMEM((2 * ROWS, width), bf16)] * 2,
            pltpu.VMEM((width, 3 * units), bf16),
            pltpu.SemaphoreType.DMA((2, 2)),
            pltpu.SemaphoreType.DMA((3, units // CHUNK)),
        ],
        compiler_params=params(20),
        cost_estimate=cost(4e9, 8e6, 1e6),
        name="feed_step",
    )(*second, *map(far, grads), far(weights))


def feed_out_kernel(first, then, wd, mine, other):
    for k, hidden in enumerate((first, then)):

        @pl.when(pl.program_id(0) == k)
        def _(hidden=hidden):
            part = matmul_t(hidden[...], wd[...]).astype(bf16)
            mine[0] = part[:ROWS]
            other[0] = part[ROWS:]


def feed_out(hidden, weights):
    pair, units = hidden[0].shape
    width = weights.shape[0]
    block = pl.BlockSpec((1, ROWS, width), lambda i: (i, 0, 0))
    return pl.pallas_call(
        feed_out_kernel,
        grid=(2,),
        in_specs=[whole((pair, units)), whole((pair, units)), whole((width, units), (0, 2))],
        out_specs=[block, block],
        out_shape=[pltpu.HBM((2, ROWS, width), bf16)] * 2,
        compiler_params=params(20),
        cost_estimate=cost(1.6e9, 5e6),
        name="feed_out",
    )(*map(far, hidden), far(weights))


def feed_weights_kernel(*refs):
    second, grads, grad_units, hidden = refs[:4], refs[4:8], refs[8:10], refs[10:12]
    out, rows_s, rows_g = refs[12:]
    wide = grad_units[0].shape[1]
    pair = 2 * ROWS
    for k, block in enumerate(BLOCK_ORDER):
        rows_s[k * ROWS : (k + 1) * ROWS, :] = second[block][...]
        rows_g[k * ROWS : (k + 1) * ROWS, :] = grads[block][...]
    both = lambda rows, others: sum(
        t_matmul(rows[k * pair : (k + 1) * pair, :], other[...]) for k, other in enumerate(others)
    )
    out[:, :wide] = both(rows_s, grad_units).astype(bf16)
    out[:, wide:] = both(rows_g, hidden).astype(bf16)


def feed_weights(second, grads, grad_units, hidden):
    width = second[0].shape[1]
    pair, wide = grad_units[0].shape
    units = hidden[0].shape[1]
    return pl.pallas_call(
        feed_weights_kernel,
        grid=(width // 512,),
        in_specs=[
            *[pl.BlockSpec((ROWS, 512), lambda i: (0, i))] * 8,
            *[whole((pair, wide))] * 2,
            *[whole((pair, units))] * 2,
        ],
        out_specs=pl.BlockSpec((512, wide + units), lambda i: (i, 0)),
        out_shape=pltpu.HBM((width, wide + units), bf16),
        scratch_shapes=[pltpu.VMEM((2 * pair, 512), bf16)] * 2,
        compiler_params=params(24),
        cost_estimate=cost(4.8e9, 14e6),
        name="feed_weights",
    )(*map(far, second), *map(far, grads), *map(far, grad_units), *map(far, hidden))


def middle_back_kernel(middle, mine, from_core, from_z, cotangent, gain, grad_middle, branch, gain_part):
    u = mine[...].astype(f32) + from_core[...].astype(f32) + from_z[...].astype(f32)
    grad, part = norm_back(middle[...], gain[1:2, :], u)
    grad = cotangent[...].astype(f32) + grad
    grad_middle[...] = grad
    branch[...] = grad.astype(bf16)

    @pl.when(pl.program_id(0) == 0)
    def _():
        gain_part[...] = jnp.zeros_like(gain_part)

    gain_part[:1, :] += part


def middle_back(middle, part, from_core, from_z, cotangent, gain):
    width = middle.shape[1]
    half = ROWS // 2
    row = pl.BlockSpec((half, width), lambda i: (i, 0))
    return pl.pallas_call(
        middle_back_kernel,
        grid=(2,),
        in_specs=[row, row, row, row, row, whole((8, width))],
        out_specs=[row, row, whole_out((8, width))],
        out_shape=[
            pltpu.HBM((ROWS, width), f32),
            jax.ShapeDtypeStruct((ROWS, width), bf16),
            pltpu.HBM((8, width), f32),
        ],
        compiler_params=params(14),
        cost_estimate=cost(4e6, 5e6),
        name="middle_back",
    )(far(middle), part, from_core, from_z, far(cotangent), gain)


def backward_attention_kernel(per_device, place, *refs):
    branch = refs[:4]
    tokens = refs[4:8]
    weights, first, att_out, low, totals, qraw, kraw, cos, sin, head_gains, second_gain = refs[8:19]
    mine, other, out = refs[19:22]
    matrices, rows_all, xs_all, first_all, att, grads_all, block = refs[22:29]
    grad_att, dk, dv, dq, gain_part, head_part, row_sems, matrix_sems, out_sems = refs[29:]
    qgain, kgain = head_gains[:1, :], head_gains[1:2, :]
    step_id = pl.program_id(0)
    i = pl.num_programs(0) - 1 - step_id
    nq, nk = qraw.shape[1], kraw.shape[1]

    @pl.when(step_id == 0)
    def _():
        gain_part[...] = jnp.zeros_like(gain_part)
        head_part[...] = jnp.zeros_like(head_part)

    nqkv = nq + 2 * nk
    wqkv = matrices.at[:, :nqkv]
    wo = matrices.at[:, nqkv:]
    load_o = pltpu.make_async_copy(weights.at[:, nqkv : nqkv + nq], wo, matrix_sems.at[0])
    load_qkv = pltpu.make_async_copy(weights.at[:, :nqkv], wqkv, matrix_sems.at[1])
    load_att = pltpu.make_async_copy(att_out, att, matrix_sems.at[2])
    load_first = pltpu.make_async_copy(first, first_all, matrix_sems.at[3])
    loads = []
    for pieces, target, sem in ((branch, rows_all, row_sems.at[0]), (tokens, xs_all, row_sems.at[1])):
        for k, piece in enumerate(pieces):
            at = pl.ds(pl.multiple_of(place[4 + k] * ROWS, ROWS), ROWS)
            loads.append(pltpu.make_async_copy(piece, target.at[at, :], sem.at[k]))

    @pl.when(step_id == 0)
    def _():
        for copy in [load_o, *loads[:4], load_att, load_qkv, *loads[4:], load_first]:
            copy.start()
        for copy in [load_o, *loads[:4], load_att]:
            copy.wait()

    here = pl.ds(pl.multiple_of(i * 2 * ROWS, 2 * ROWS), 2 * ROWS)
    grad_att[...] = matmul(rows_all[here, :], wo[...]).astype(bf16)
    mask_k = lax.broadcasted_iota(jnp.int32, (ROWS, GROUP * ROWS), 0)
    mask_q = lax.broadcasted_iota(jnp.int32, (ROWS, GROUP * ROWS), 1) % ROWS

    def attend_back(block):
        half = block % 2 * ROWS
        n = block * ROWS
        end = n + ROWS
        for h in range(nk // HD):
            cols = [(h * GROUP + a) * HD for a in range(GROUP)]
            q2 = jnp.concatenate([low[n:end, col : col + HD] for col in cols], axis=0)
            g2 = jnp.concatenate([grad_att[half : half + ROWS, col : col + HD] for col in cols], axis=0)
            o2 = jnp.concatenate([att[n:end, col : col + HD] for col in cols], axis=0)
            total = totals[block % 2, h : h + 1, :]
            dot = jnp.sum((g2.astype(f32) * o2.astype(f32)).T, axis=0, keepdims=True)
            k = low[:end, nq + h * HD : nq + (h + 1) * HD]
            v = low[:end, nq + nk + h * HD : nq + nk + (h + 1) * HD]
            probs = jnp.exp2(matmul_t(k, q2) * log2_scale - total)
            last = jnp.where(mask_k <= mask_q, probs[n:], 0.0)
            probs = jnp.concatenate([probs[:n], last], axis=0) if n else last
            grad_scores = (probs * (matmul_t(v, g2) - dot)).astype(bf16)
            dv_part = matmul(probs.astype(bf16), g2)
            dk_part = matmul(grad_scores, q2)
            if end == keys:
                dv[h] = dv_part
                dk[h] = dk_part
            else:
                dv[h, :end, :] += dv_part
                dk[h, :end, :] += dk_part
            d = t_matmul(k, grad_scores).T * score_scale
            for a, col in enumerate(cols):
                dq[half : half + ROWS, col : col + HD] = d[a * ROWS : (a + 1) * ROWS]

    keys = low.shape[0]
    for k in range(keys // (2 * ROWS)):

        @pl.when(i == k)
        def _(k=k):
            attend_back(2 * k + 1)
            attend_back(2 * k)

    c, s = cos[...], sin[...]

    def unturned(w):
        return w * c - pltpu.roll(w, HD // 2, 1) * s

    for h in range(nq // HD):
        col = slice(h * HD, (h + 1) * HD)
        grad, gp = norm_back(qraw[:, col], qgain, unturned(dq[:, col]))
        grads_all[here, col] = grad.astype(bf16)
        head_part[:1, :] += gp
    for h in range(nk // HD):
        col = slice(h * HD, (h + 1) * HD)
        grad, gp = norm_back(kraw[:, col], kgain, unturned(dk[h, here, :] * score_scale))
        grads_all[here, nq + h * HD : nq + (h + 1) * HD] = grad.astype(bf16)
        head_part[1:2, :] += gp
        grads_all[here, nq + nk + h * HD : nq + nk + (h + 1) * HD] = dv[h, here, :].astype(bf16)
    @pl.when(step_id == 0)
    def _():
        for copy in [load_qkv, *loads[4:]]:
            copy.wait()

    upstream = matmul_t(grads_all[here, :], wqkv[...])
    put_pair(place[2 * i], upstream.astype(bf16), mine, other)
    x = xs_all[here, :].astype(f32)
    gain_part[:1, :] += jnp.sum(upstream * x * inverse_rms(x), axis=0, keepdims=True)

    @pl.when(step_id == pl.num_programs(0) - 1)
    def _():
        load_first.wait()
        more = nqkv + nq
        rows = 2 * ROWS
        stored = []
        for k in range(first_all.shape[1] // rows):
            at = slice(k * rows, (k + 1) * rows)
            block[at, :nqkv] = t_matmul(first_all[:, at], grads_all[...]).astype(bf16)
            block[at, nqkv:more] = t_matmul(rows_all[:, at], att[...]).astype(bf16)
            same = equal_iota(rows, rows, lambda r, c: r == c)
            stands = of_head(rows, per_device, k * rows)
            lane = lax.broadcasted_iota(jnp.int32, (rows, HD), 1)
            columns = jnp.zeros((rows, HD), f32)
            values = [
                (same, gain_part[:1, at]),
                (same, second_gain[:1, at]),
                (stands, head_part[:1, :]),
                (stands, head_part[1:2, :]),
            ]
            for m, (mask, line) in enumerate(values):
                column = jnp.sum(jnp.where(mask, line, 0.0), axis=1, keepdims=True)
                columns = jnp.where(lane == m, column, columns)
            block[at, more:] = columns.astype(bf16)
            stored.append(pltpu.make_async_copy(block.at[at, :], out.at[at, :], out_sems.at[k]))
            stored[-1].start()
        for copy in stored:
            copy.wait()


def backward_attention(
    place, branch, tokens, weights, first, low, att, totals, qraw, kraw, cos, sin, head_gains, second_gain
):
    n, width = 4, branch[0].shape[1]
    length, nqkv = low.shape
    nq, nk = qraw.shape[1], kraw.shape[1]
    total = nqkv + nq + HD
    row = lambda cols: pl.BlockSpec((2 * ROWS, cols), lambda i, p: (n // 2 - 1 - i, 0))
    half = pl.BlockSpec((1, ROWS, width), lambda i, p: (p[n - 2 - 2 * i] % 2, 0, 0))
    return pl.pallas_call(
        functools.partial(backward_attention_kernel, width // lax.axis_size(FSDP)),
        grid_spec=pltpu.PrefetchScalarGridSpec(
            num_scalar_prefetch=1,
            grid=(n // 2,),
            in_specs=[
                *[pl.BlockSpec(memory_space=pl.ANY)] * 11,
                whole((length, nqkv)),
                pl.BlockSpec((2, 8, GROUP * ROWS), lambda i, p: (n // 2 - 1 - i, 0, 0)),
                row(nq),
                row(nk),
                row(HD),
                row(HD),
                whole((8, HD)),
                whole((8, width)),
            ],
            out_specs=[half, half, pl.BlockSpec(memory_space=pltpu.HBM)],
            scratch_shapes=[
                pltpu.VMEM((width, nqkv + nq), bf16),
                pltpu.VMEM((length, width), bf16),
                pltpu.VMEM((length, width), bf16),
                pltpu.VMEM((length, width), bf16),
                pltpu.VMEM((length, nq), bf16),
                pltpu.VMEM((length, nqkv), bf16),
                pltpu.VMEM((width, total), bf16),
                pltpu.VMEM((2 * ROWS, nq), bf16),
                pltpu.VMEM((nk // HD, length, HD), f32),
                pltpu.VMEM((nk // HD, length, HD), f32),
                pltpu.VMEM((2 * ROWS, nq), f32),
                pltpu.VMEM((8, width), f32),
                pltpu.VMEM((8, HD), f32),
                pltpu.SemaphoreType.DMA((2, 4)),
                pltpu.SemaphoreType.DMA((4,)),
                pltpu.SemaphoreType.DMA((width // (2 * ROWS),)),
            ],
        ),
        out_shape=[
            pltpu.HBM((2, ROWS, width), bf16),
            pltpu.HBM((2, ROWS, width), bf16),
            pltpu.HBM((width, total), bf16),
        ],
        compiler_params=params(46),
        cost_estimate=cost(6e11, 18e6, 3e6),
        name="backward_attention",
    )(
        place, *branch, *map(far, tokens), far(weights), far(first), far(att), far(low), far(totals),
        far(qraw), far(kraw), far(cos), far(sin), far(head_gains), far(second_gain),
    )


def tokens_back_kernel(tokens, mine, from_core, from_z, grad_middle, gain, grad_tokens):
    u = mine[...].astype(f32) + from_core[...].astype(f32) + from_z[...].astype(f32)
    grad, _ = norm_back(tokens[...].astype(f32), gain[:1, :], u)
    grad_tokens[...] = grad_middle[...] + grad


def tokens_back(tokens, mine, from_core, from_z, grad_middle, gain):
    width = tokens.shape[1]
    half = ROWS // 2
    row = pl.BlockSpec((half, width), lambda i: (i, 0))
    first = pl.BlockSpec((None, half, width), lambda i: (0, i, 0))
    return pl.pallas_call(
        tokens_back_kernel,
        grid=(2,),
        in_specs=[row, first, first, row, row, whole((8, width))],
        out_specs=row,
        out_shape=pltpu.HBM((ROWS, width), f32),
        compiler_params=params(14),
        cost_estimate=cost(4e6, 4e6),
        name="tokens_back",
    )(far(tokens), mine, from_core, from_z, far(grad_middle), far(gain))


def close(zh, parts):
    senders, both, wide = parts.shape
    rows = both // 2

    def kernel(zh, parts, keep, give):
        for which, out in ((zh[0], keep), (1 - zh[0], give)):
            at = pl.ds(pl.multiple_of(which * rows, rows), rows)
            added = parts[0, at, :].astype(f32)
            for k in range(1, senders):
                added = added + parts[k, at, :].astype(f32)
            out[...] = added.astype(out.dtype)

    return pl.pallas_call(
        kernel,
        grid_spec=pltpu.PrefetchScalarGridSpec(
            num_scalar_prefetch=1,
            grid=(1,),
            in_specs=[whole(parts.shape)],
            out_specs=[whole_out((rows, wide))] * 2,
        ),
        out_shape=[
            jax.ShapeDtypeStruct((rows, wide), f32),
            jax.ShapeDtypeStruct((rows, wide), bf16),
        ],
        compiler_params=params(14),
        cost_estimate=cost(2e6, 4e6),
        name="close",
    )(zh, far(parts) if senders == 1 else parts)


def finish(keep, arrived, widths):
    rows = keep.shape[0]

    def kernel(keep, arrived, *outs):
        at = 0
        for out in outs:
            some = slice(at, at + out.shape[1])
            out[...] = keep[:, some] + arrived[:, some].astype(f32)
            at += out.shape[1]

    return pl.pallas_call(
        kernel,
        out_shape=[jax.ShapeDtypeStruct((rows, w), f32) for w in widths],
        compiler_params=params(8),
        cost_estimate=cost(1e5, 1e6),
        name="finish",
    )(keep, arrived)


def finish_gains(parts, rows, heads):
    def kernel(*refs):
        total = refs[0][...] + refs[1][...] + refs[2][...] + refs[3][...]
        same = equal_iota(rows, rows, lambda r, c: r == c)
        for k, out in enumerate(refs[4:]):
            line = jnp.sum(jnp.where(same, total[:, k : k + 1], 0.0), axis=0, keepdims=True)
            out[...] = line[:, : out.shape[1]]

    widths = (rows, rows, heads, heads)
    outs = pl.pallas_call(
        kernel,
        out_shape=[jax.ShapeDtypeStruct((1, w), f32) for w in widths],
        compiler_params=params(4),
        cost_estimate=cost(1e4, 1e5),
        name="finish_gains",
    )(*parts)
    return [out.reshape(-1) for out in outs]


def pack(first, second, gains, rows, heads):
    widths = [a.shape[1] for a in first], [a.shape[1] for a in second]
    split = sum(widths[0])

    def kernel(gains, *refs):
        out = refs[-1]
        at = 0
        for k, ref in enumerate(refs[:-1]):
            at += HD * (k == len(first))
            out[:, at : at + ref.shape[1]] = ref[...]
            at += ref.shape[1]
        g = gains[...].astype(f32)
        lane = lax.broadcasted_iota(jnp.int32, (rows, HD), 1)
        line = lax.broadcasted_iota(jnp.int32, (rows, HD), 0)
        columns = jnp.zeros((rows, HD), f32)
        places = [(0, rows), (rows, rows), (2 * rows, heads), (2 * rows + heads, heads)]
        for k, (start, count) in enumerate(places):
            mask = (lane == line + start) & (line < count)
            column = jnp.sum(jnp.where(mask, g, 0.0), axis=1, keepdims=True)
            columns = jnp.where(lane == k, column, columns)
        out[:, split : split + HD] = columns.astype(bf16)

    return pl.pallas_call(
        kernel,
        out_shape=jax.ShapeDtypeStruct((rows, split + HD + sum(widths[1])), bf16),
        compiler_params=params(8),
        cost_estimate=cost(1e3, 5e5),
        name="pack",
    )(gains, *map(far, first), *map(far, second))


def pair(zh, shard, other, cut, split):
    rows, wide = shard.shape

    def kernel(zh, shard, other, left, right, rest):
        for k, ref in enumerate((shard, other)):
            left[k] = ref[:, :cut]
            right[k] = ref[:, cut:split]
            rest[pl.ds(pl.multiple_of((zh[0] ^ k) * rows, rows), rows), :] = ref[:, split:]

    shapes = [(2, rows, cut), (2, rows, split - cut), (2 * rows, wide - split)]
    return pl.pallas_call(
        kernel,
        grid_spec=pltpu.PrefetchScalarGridSpec(
            num_scalar_prefetch=1,
            grid=(1,),
            in_specs=[whole((rows, wide))] * 2,
            out_specs=[whole_out(s) for s in shapes],
        ),
        out_shape=[
            *[jax.ShapeDtypeStruct(s, bf16) for s in shapes[:2]],
            pltpu.HBM(shapes[2], bf16),
        ],
        compiler_params=params(8),
        cost_estimate=cost(1e3, 1e6),
        name="pair",
    )(zh, shard, other)


def load_pieces(order, pieces, target, semaphores):
    copies = []
    half = len(pieces) // 2
    cut = pieces[0].shape[3]
    for side in range(2):
        n = 0
        for piece in pieces[side * half : (side + 1) * half]:
            rows, wide = piece.shape[2:]
            for j in range(piece.shape[0]):
                for k in range(2):
                    place = pl.multiple_of(order[side, n] * rows, rows)
                    copy = pltpu.make_async_copy(
                        piece.at[j, k],
                        target.at[pl.ds(place, rows), side * cut : side * cut + wide],
                        semaphores.at[side, n],
                    )
                    copy.start()
                    copies.append(copy)
                    n += 1
    return copies


def swapped(value, axis):
    return lax.ppermute(value, axis, [(0, 1), (1, 0)])


def tp_gather(own, over_z=None):
    over_z = swapped(own, "zl") if over_z is None else over_z
    return [own, over_z, swapped(own, "core"), swapped(over_z, "core")]


def tp_scatter(mine, other):
    from_core = swapped(other, "core")
    passed = (mine[1].astype(f32) + from_core[1].astype(f32)).astype(bf16)
    return mine, from_core, swapped(passed, "zl"), passed


def after(value, *others):
    return lax.optimization_barrier((value, *others))[0]


def sent_rows(part):
    planes = lax.axis_size(PLANE)
    blocks = part.reshape(planes, part.shape[0] // planes, part.shape[1])
    return lax.all_to_all(blocks, PLANE, 0, 0, tiled=True)


def by_distance(sides):
    done = [{0: own} for own, _ in sides]
    before = []
    for near in (True, False):
        arrived = []
        for kept, (own, axis) in zip(done, sides):
            n = lax.axis_size(axis)
            for j in range(1, n):
                if (j in (1, n - 1)) == near:
                    perm = [(s, (s - j) % n) for s in range(n)]
                    kept[j] = lax.ppermute(after(own, *before) if before else own, axis, perm)
                    arrived.append(kept[j])
        before = arrived
    return [[kept[j] for j in sorted(kept)] for kept in done]


def gathered_order():
    nx, ny = lax.axis_size("x"), lax.axis_size("y")
    x, y = (lax.axis_index("x") + jnp.arange(nx)) % nx, (lax.axis_index("y") + jnp.arange(ny)) % ny
    z = lax.axis_index("zh") ^ jnp.arange(2)
    block = lambda x, y: ((x * ny + y) * 2 + z).reshape(-1)
    left = block(x[None, :, None], y[:, None, None])
    right = block(x[:, None, None], y[None, :, None])
    return jnp.stack([left, right]).astype(jnp.int32)


def rotary_tables(length):
    midway = HD // 2
    frequency = 1.0 / rope_base ** (np.arange(midway) * 2.0 / HD)
    angles = np.arange(length)[:, None] * frequency[None, :]
    cos, sin = np.cos(angles), np.sin(angles)
    tables = np.concatenate([cos, cos], axis=1), np.concatenate([-sin, sin], axis=1)
    return [jnp.asarray(t.astype(np.float32)) for t in tables]


def local(
    tokens,
    attention_gain,
    query_weight,
    key_weight,
    value_weight,
    query_gain,
    key_gain,
    output_weight,
    feed_gain,
    gate_weight,
    up_weight,
    down_weight,
    cotangent,
):
    width = tokens.shape[2]
    nq, nk = query_weight.shape[1], key_weight.shape[1]
    units = gate_weight.shape[1]
    rows = query_weight.shape[0]
    x = tokens[0]
    dy = cotangent[0]
    zl, core = lax.axis_index("zl"), lax.axis_index("core")
    block = jnp.arange(4, dtype=jnp.int32)
    place = ((block % 2) ^ core) * 2 + ((block // 2) ^ zl)
    block_of = ((block // 2) ^ core) + ((block % 2) ^ zl) * 2
    place = jnp.concatenate([place, block_of]).astype(jnp.int32)
    cos, sin = rotary_tables(4 * ROWS)

    heads = query_gain.shape[0]
    gains = jnp.concatenate([attention_gain, feed_gain, query_gain, key_gain])
    gains = jnp.pad(gains, (0, HD - gains.shape[0]))[None]
    shard = pack(
        [query_weight, key_weight, value_weight, output_weight],
        [gate_weight, up_weight, down_weight],
        gains,
        rows,
        heads,
    )
    over_zh = swapped(shard, "zh")
    split = nq + 2 * nk + nq + HD
    left, right, feed = pair(lax.axis_index("zh").reshape(1), shard, over_zh, nq + nk, split)
    order = gathered_order()
    left, right = by_distance([(left, "x"), (right, "y")])
    token_blocks = tp_gather(after(x, over_zh))
    left, right = by_distance([(jnp.stack(left), "y"), (jnp.stack(right), "x")])
    feed = lax.all_gather(after(feed, left[1], left[-1], right[1], right[-1]), PLANE, axis=0, tiled=True)
    grads_over_z = swapped(after(dy, *left, *right), "zl")

    first, qraw, kraw, low, att, totals, mine, other, gains, head_gains, weights = forward_attention(
        place, order, token_blocks, left + right, nq, nk, cos, sin
    )
    grad_blocks = tp_gather(dy, after(grads_over_z, other))
    other = after(other, grads_over_z)
    mine, from_core, from_z, _ = tp_scatter(mine, other)
    middle, second = middle_step(x, mine, from_core, from_z, gains)
    over_z = swapped(second, "zl")
    near = feed_step([second, swapped(second, "core")], grad_blocks[::2], feed, units)
    second_blocks = tp_gather(second, after(over_z, near[1]))
    far_ones = feed_step(second_blocks[1::2], grad_blocks[1::2], feed, units)
    hidden, grad_units = [near[0], far_ones[0]], [near[1], far_ones[1]]
    from_core = swapped(near[3], "core")
    passed = (after(far_ones[2], from_core).astype(f32) + swapped(far_ones[3], "core").astype(f32)).astype(bf16)
    from_z = swapped(passed, "zl")
    grad_units[0] = after(grad_units[0], passed)
    feed_grads = feed_weights(second_blocks, grad_blocks, grad_units, hidden)
    from_z = after(from_z, feed_grads)
    grad_middle, branch, feed_gain_part = middle_back(middle, near[2], from_core, from_z, dy, gains)
    feed_sums = lax.psum_scatter(feed_grads, "x", scatter_dimension=0, tiled=True)
    feed_sums = lax.psum_scatter(feed_sums, "y", scatter_dimension=0, tiled=True)
    over_z = swapped(branch, "zl")
    mine, other = feed_out([after(hidden[0], branch), hidden[1]], feed)
    branch_blocks = tp_gather(branch, after(over_z, other))
    mine, from_core, from_z, _ = tp_scatter(mine, other)
    output = middle + mine[0].astype(f32) + from_core[0].astype(f32) + from_z.astype(f32)
    output = output.astype(bf16)

    mine, other, projection_grads = backward_attention(
        place, branch_blocks, token_blocks, weights, first, low, att, totals, qraw, kraw, cos, sin,
        head_gains, feed_gain_part,
    )
    mine, from_core, from_z, _ = tp_scatter(mine, other)
    tokens_grad = tokens_back(
        x, mine, from_core, after(from_z, projection_grads), grad_middle, gains
    )
    parts = after(sent_rows(projection_grads), tokens_grad, output)
    zh = lax.axis_index("zh").reshape(1)
    keep, give = close(zh, parts)
    arrived = swapped(give, "zh")
    query, key, value, out, columns = finish(keep, arrived, (nq, nk, nk, nq, HD))
    feed_keep, feed_give = close(zh, after(feed_sums, arrived)[None])
    gate, up, down = finish(feed_keep, swapped(feed_give, "zh"), (units, units, units))
    both = ("zl", "core")
    across = lax.ppermute(columns, both, [(s, 3 - s) for s in range(4)])
    parts = (columns, swapped(columns, "zl"), swapped(columns, "core"), across)
    first_sum, second_sum, query_sum, key_sum = finish_gains(parts, rows, heads)

    return (
        output[None],
        tokens_grad[None],
        first_sum,
        query,
        key,
        value,
        query_sum,
        key_sum,
        out,
        second_sum,
        gate,
        up,
        down,
    )


def solution(mesh):
    fsdp, tp = mesh.devices.shape
    cut = {32: (4, 4, 2), 2: (1, 1, 2), 1: (1, 1, 1)}[fsdp]
    fine = Mesh(mesh.devices.reshape(*cut, 2, tp // 2), EVERY)
    split = ("zl", "core")
    data = P(FSDP, split, None)
    matrix = P(FSDP, split)
    vector = P(FSDP)
    return jax.shard_map(
        local,
        mesh=fine,
        in_specs=(
            data, vector, matrix, matrix, matrix, vector, vector,
            matrix, vector, matrix, matrix, matrix, data,
        ),
        out_specs=(
            data, data, vector, matrix, matrix, matrix, vector, vector,
            matrix, vector, matrix, matrix, matrix,
        ),
        check_vma=False,
    )
```

```python
import functools
import math

import jax
import jax.numpy as jnp
import numpy as np
from jax import lax
from jax.experimental import pallas as pl
from jax.experimental.pallas import tpu as pltpu
from jax.sharding import Mesh, PartitionSpec as P

HD = 128
ROWS = 256
WIDTH = 1024
GROUP = 2
CHUNK = 256
BLOCK_ORDER = (0, 2, 1, 3)
epsilon = 1e-06
rope_base = 1000000.0
score_scale = 1.0 / math.sqrt(HD)
log2_scale = score_scale / math.log(2.0)
FSDP = ("x", "y", "zh")
PLANE = ("x", "y")
EVERY = ("x", "y", "zh", "zl", "core")
f32 = jnp.float32
bf16 = jnp.bfloat16


def matmul(a, b):
    return lax.dot_general(a, b, (((1,), (0,)), ((), ())), preferred_element_type=f32)


def matmul_t(a, b):
    return lax.dot_general(a, b, (((1,), (1,)), ((), ())), preferred_element_type=f32)


def t_matmul(a, b):
    return lax.dot_general(a, b, (((0,), (0,)), ((), ())), preferred_element_type=f32)


def inverse_rms(values):
    return lax.rsqrt(jnp.mean(values * values, axis=-1, keepdims=True) + epsilon)


def norm_back(values, gain, upstream):
    inverse = inverse_rms(values)
    scaled = gain * upstream
    moment = jnp.mean(scaled * values, axis=-1, keepdims=True)
    grad = inverse * scaled - values * (inverse * inverse * inverse) * moment
    return grad, jnp.sum(upstream * values * inverse, axis=0, keepdims=True)


def far(value):
    return pltpu.with_memory_space_constraint(value, pltpu.HBM)


def params(mib):
    return pltpu.CompilerParams(vmem_limit_bytes=mib * 1024 * 1024)


def cost(flops, nbytes, trans=0):
    return pl.CostEstimate(flops=int(flops / 8), bytes_accessed=int(nbytes / 8), transcendentals=int(trans / 8))


def whole(shape, index=None):
    index = index or (0,) * len(shape)
    return pl.BlockSpec(shape, lambda i, *_: index, pipeline_mode=pl.Buffered(1))


def halves(width):
    return [
        pl.BlockSpec((1, ROWS, width), lambda i: (jnp.minimum(i, 1), 0, 0)),
        pl.BlockSpec((1, ROWS, width), lambda i: (jnp.maximum(i - 2, 0), 0, 0)),
    ]


def whole_out(shape):
    return pl.BlockSpec(shape, lambda i, *_: (0,) * len(shape))


def pick(which, pieces, target):
    for k, piece in enumerate(pieces):

        @pl.when(which == k)
        def _(piece=piece):
            target[...] = piece[...]


def equal_iota(rows, cols, make):
    r = lax.broadcasted_iota(jnp.int32, (rows, cols), 0)
    c = lax.broadcasted_iota(jnp.int32, (rows, cols), 1)
    return make(r, c)


def row_of(columns, k):
    same = equal_iota(128, 128, lambda r, c: r == c)
    parts = []
    for m in range(columns.shape[0] // 128):
        col = columns[m * 128 : (m + 1) * 128, k : k + 1].astype(f32)
        parts.append(jnp.sum(jnp.where(same, col, 0.0), axis=0, keepdims=True))
    return jnp.concatenate(parts, axis=1)


def of_head(rows, per_device, first_row=0):
    held = HD * per_device // WIDTH
    return equal_iota(
        rows, HD, lambda r, c: ((r + first_row) // per_device * held + (r + first_row) % per_device == c)
        & ((r + first_row) % per_device < held)
    )


def heads_of(columns, k, per_device):
    col = columns[:, k : k + 1].astype(f32)
    return jnp.sum(jnp.where(of_head(columns.shape[0], per_device), col, 0.0), axis=0, keepdims=True)


def put_pair(which, value, mine, other):
    top, bottom = value[:ROWS], value[ROWS:]

    @pl.when(which < 2)
    def _():
        mine[0] = top
        other[0] = bottom

    @pl.when(which >= 2)
    def _():
        mine[0] = bottom
        other[0] = top


def put(which, value, mine, other):
    @pl.when(which < 2)
    def _():
        mine[0] = value

    @pl.when(which >= 2)
    def _():
        other[0] = value


def forward_attention_kernel(per_device, n_pieces, place, order, *refs):
    tokens = refs[:4]
    pieces, refs = refs[4 : 4 + n_pieces], refs[4 + n_pieces :]
    cos, sin = refs[:2]
    first, qraw, kraw, low, att, totals, mine, other, gains, head_gains, ordered = refs[2:13]
    rows, scaled, keys, values, weights, piece_sems, ordered_sem = refs[13:]
    i = pl.program_id(0)
    nq, nqkv = qraw.shape[1], low.shape[1]
    wqkv = weights.at[:, :nqkv]
    wo = weights.at[:, nqkv : nqkv + nq]
    columns = weights.at[:, nqkv + nq :]
    keep = pltpu.make_async_copy(weights, ordered, ordered_sem)
    loads = load_pieces(order, pieces, weights, piece_sems)

    @pl.when(i == 0)
    def _():
        for copy in loads:
            copy.start()

    for a in range(2):
        pick(place[2 * i + a], tokens, rows.at[a * ROWS : (a + 1) * ROWS, :])
    x = rows[...].astype(f32)
    scaled[...] = x * inverse_rms(x)

    @pl.when(i == 0)
    def _():
        for copy in loads:
            copy.wait()
        keep.start()
        gains[:2, :] = jnp.concatenate([row_of(columns, 0), row_of(columns, 1)], axis=0)
        gains[2:, :] = jnp.zeros_like(gains[2:, :])
        head_gains[:2, :] = jnp.concatenate([heads_of(columns, k, per_device) for k in (2, 3)], axis=0)
        head_gains[2:, :] = jnp.zeros_like(head_gains[2:, :])

    gain, qgain, kgain = gains[:1, :], head_gains[:1, :], head_gains[1:2, :]
    normed = (scaled[...] * gain).astype(bf16)
    first[...] = normed
    qkv = matmul(normed, wqkv[...])
    nq, nk = qraw.shape[1], kraw.shape[1]
    qraw[...] = qkv[:, :nq]
    kraw[...] = qkv[:, nq : nq + nk]
    here = pl.ds(pl.multiple_of(i * 2 * ROWS, 2 * ROWS), 2 * ROWS)
    c, s = cos[...], sin[...]

    def turned(v, g):
        n = v * inverse_rms(v) * g
        return (n * c + pltpu.roll(n, HD // 2, 1) * s).astype(bf16)

    for h in range(nk // HD):
        k_low = turned(qkv[:, nq + h * HD : nq + (h + 1) * HD], kgain)
        v_low = qkv[:, nq + nk + h * HD : nq + nk + (h + 1) * HD].astype(bf16)
        low[:, nq + h * HD : nq + (h + 1) * HD] = k_low
        low[:, nq + nk + h * HD : nq + nk + (h + 1) * HD] = v_low
        keys[h, here, :] = k_low
        values[h, here, :HD] = v_low
        values[h, here, HD:] = jnp.ones((2 * ROWS, HD), bf16)
    for h in range(nq // HD):
        low[:, h * HD : (h + 1) * HD] = turned(qkv[:, h * HD : (h + 1) * HD], qgain)
    mask_q = lax.broadcasted_iota(jnp.int32, (GROUP * ROWS, ROWS), 0) % ROWS
    mask_k = lax.broadcasted_iota(jnp.int32, (GROUP * ROWS, ROWS), 1)

    def attend(block):
        half = block % 2 * ROWS
        n = block * ROWS
        sums = []
        for h in range(nk // HD):
            cols = [(h * GROUP + a) * HD for a in range(GROUP)]
            q2 = jnp.concatenate([low[half : half + ROWS, col : col + HD] for col in cols], axis=0)
            scores = matmul_t(q2, keys[h, : n + ROWS, :]) * log2_scale
            weights = jnp.exp2(scores[:, n:])
            weights = jnp.where(mask_k <= mask_q, weights, 0.0).astype(bf16)
            if n:
                weights = jnp.concatenate([jnp.exp2(scores[:, :n]).astype(bf16), weights], axis=1)
            acc = matmul(weights, values[h, : n + ROWS, :])
            total = acc[:, HD:]
            o = (acc[:, :HD] / total).astype(bf16)
            for a, col in enumerate(cols):
                att[half : half + ROWS, col : col + HD] = o[a * ROWS : (a + 1) * ROWS]
            sums.append(jnp.log2(total).T[:1, :])
        sums = jnp.concatenate(sums + [jnp.zeros((8 - len(sums), GROUP * ROWS), f32)], axis=0)
        totals[block % 2] = sums

    for k in range(2):

        @pl.when(i == k)
        def _(k=k):
            attend(2 * k)
            attend(2 * k + 1)

    put_pair(place[2 * i], matmul_t(att[...], wo[...]).astype(bf16), mine, other)

    @pl.when(i == pl.num_programs(0) - 1)
    def _():
        keep.wait()


def forward_attention(place, order, tokens, pieces, nq, nk, cos, sin):
    n, width = 4, tokens[0].shape[1]
    length = n * ROWS
    nqkv = nq + 2 * nk
    row = lambda cols: pl.BlockSpec((2 * ROWS, cols), lambda i, p, o: (i, 0))
    out = [
        ((length, width), bf16, row(width)),
        ((length, nq), f32, row(nq)),
        ((length, nk), f32, row(nk)),
        ((length, nqkv), bf16, row(nqkv)),
        ((length, nq), bf16, row(nq)),
        ((n, 8, GROUP * ROWS), f32, pl.BlockSpec((2, 8, GROUP * ROWS), lambda i, p, o: (i, 0, 0))),
        *[((2, ROWS, width), bf16, pl.BlockSpec((1, ROWS, width), lambda i, p, o: (p[2 * i] % 2, 0, 0)))] * 2,
        ((8, width), f32, whole_out((8, width))),
        ((8, HD), f32, whole_out((8, HD))),
        ((width, nqkv + nq + HD), bf16, pl.BlockSpec(memory_space=pltpu.HBM)),
    ]
    return pl.pallas_call(
        functools.partial(forward_attention_kernel, width // lax.axis_size(FSDP), len(pieces)),
        grid_spec=pltpu.PrefetchScalarGridSpec(
            num_scalar_prefetch=2,
            grid=(n // 2,),
            in_specs=[
                *[whole((ROWS, width))] * 4,
                *[pl.BlockSpec(memory_space=pl.ANY)] * len(pieces),
                row(HD),
                row(HD),
            ],
            out_specs=[o[2] for o in out],
            scratch_shapes=[
                pltpu.VMEM((2 * ROWS, width), bf16),
                pltpu.VMEM((2 * ROWS, width), f32),
                pltpu.VMEM((nk // HD, length, HD), bf16),
                pltpu.VMEM((nk // HD, length, 2 * HD), bf16),
                pltpu.VMEM((width, nqkv + nq + HD), bf16),
                pltpu.SemaphoreType.DMA(order.shape),
                pltpu.SemaphoreType.DMA,
            ],
        ),
        out_shape=[(pltpu.HBM if k < 6 or k == 10 else jax.ShapeDtypeStruct)(o[0], o[1]) for k, o in enumerate(out)],
        compiler_params=params(24),
        cost_estimate=cost(7e9, 16e6, 3e6),
        name="forward_attention",
    )(place, order, far(tokens[0]), *tokens[1:], *map(far, pieces), far(cos), far(sin))


def middle_kernel(tokens, mine, from_core, from_z, gain, middle, second):
    total = mine[...].astype(f32) + from_core[...].astype(f32) + from_z[...].astype(f32)
    v = tokens[...].astype(f32) + total
    middle[...] = v
    second[...] = (v * inverse_rms(v) * gain[1:2, :]).astype(bf16)


def middle_step(tokens, part, from_core, from_z, gain):
    width = tokens.shape[1]
    half = ROWS // 2
    row = pl.BlockSpec((half, width), lambda i: (i, 0))
    first = pl.BlockSpec((None, half, width), lambda i: (0, i, 0))
    return pl.pallas_call(
        middle_kernel,
        grid=(2,),
        in_specs=[row, first, first, row, whole((8, width))],
        out_specs=[row, row],
        out_shape=[pltpu.HBM((ROWS, width), f32), jax.ShapeDtypeStruct((ROWS, width), bf16)],
        compiler_params=params(12),
        cost_estimate=cost(2e6, 4e6),
        name="middle_step",
    )(far(tokens), part, from_core, from_z, gain)


def feed_kernel(*refs):
    second, grads, weights = refs[:2], refs[2:4], refs[4]
    hidden, grad_units, mine, other = refs[5:9]
    rows_s, rows_g, matrices, row_sems, matrix_sems = refs[9:]
    units = hidden.shape[1]
    loads = []
    for k in range(2):
        at = slice(k * ROWS, (k + 1) * ROWS)
        loads.append(pltpu.make_async_copy(second[k], rows_s.at[at, :], row_sems.at[0, k]))
        loads.append(pltpu.make_async_copy(grads[k], rows_g.at[at, :], row_sems.at[1, k]))
    chunks = []
    for c in range(units // CHUNK):
        for m in range(3):
            some = slice(m * units + c * CHUNK, m * units + (c + 1) * CHUNK)
            chunks.append(
                pltpu.make_async_copy(weights.at[:, some], matrices.at[:, some], matrix_sems.at[m, c])
            )
    for copy in loads + chunks:
        copy.start()
    for copy in loads:
        copy.wait()
    s, g = rows_s[...], rows_g[...]
    for c, at in enumerate(range(0, units, CHUNK)):
        for copy in chunks[3 * c : 3 * c + 3]:
            copy.wait()
        gate = matmul(s, matrices[:, at : at + CHUNK])
        up = matmul(s, matrices[:, units + at : units + at + CHUNK])
        gh = matmul(g, matrices[:, 2 * units + at : 2 * units + at + CHUNK])
        sig = 0.5 * jnp.tanh(0.5 * gate) + 0.5
        swish = gate * sig
        hidden[:, at : at + CHUNK] = (swish * up).astype(bf16)
        grad_units[:, at : at + CHUNK] = (gh * up * (sig + swish * (1.0 - sig))).astype(bf16)
        grad_units[:, units + at : units + at + CHUNK] = (gh * swish).astype(bf16)
    part = matmul_t(grad_units[...], matrices[:, : 2 * units]).astype(bf16)
    mine[...] = part[:ROWS]
    other[...] = part[ROWS:]


def feed_step(second, grads, weights, units):
    width = second[0].shape[1]
    return pl.pallas_call(
        feed_kernel,
        in_specs=[pl.BlockSpec(memory_space=pl.ANY)] * 5,
        out_shape=[
            pltpu.HBM((2 * ROWS, units), bf16),
            pltpu.HBM((2 * ROWS, 2 * units), bf16),
            *[jax.ShapeDtypeStruct((ROWS, width), bf16)] * 2,
        ],
        scratch_shapes=[
            *[pltpu.VMEM((2 * ROWS, width), bf16)] * 2,
            pltpu.VMEM((width, 3 * units), bf16),
            pltpu.SemaphoreType.DMA((2, 2)),
            pltpu.SemaphoreType.DMA((3, units // CHUNK)),
        ],
        compiler_params=params(20),
        cost_estimate=cost(4e9, 8e6, 1e6),
        name="feed_step",
    )(*second, *map(far, grads), far(weights))


def feed_out_kernel(first, then, wd, mine, other):
    for k, hidden in enumerate((first, then)):

        @pl.when(pl.program_id(0) == k)
        def _(hidden=hidden):
            part = matmul_t(hidden[...], wd[...]).astype(bf16)
            mine[0] = part[:ROWS]
            other[0] = part[ROWS:]


def feed_out(hidden, weights):
    pair, units = hidden[0].shape
    width = weights.shape[0]
    block = pl.BlockSpec((1, ROWS, width), lambda i: (i, 0, 0))
    return pl.pallas_call(
        feed_out_kernel,
        grid=(2,),
        in_specs=[whole((pair, units)), whole((pair, units)), whole((width, units), (0, 2))],
        out_specs=[block, block],
        out_shape=[pltpu.HBM((2, ROWS, width), bf16)] * 2,
        compiler_params=params(20),
        cost_estimate=cost(1.6e9, 5e6),
        name="feed_out",
    )(*map(far, hidden), far(weights))


def feed_weights_kernel(*refs):
    second, grads, grad_units, hidden = refs[:4], refs[4:8], refs[8:10], refs[10:12]
    out, rows_s, rows_g = refs[12:]
    wide = grad_units[0].shape[1]
    pair = 2 * ROWS
    for k, block in enumerate(BLOCK_ORDER):
        rows_s[k * ROWS : (k + 1) * ROWS, :] = second[block][...]
        rows_g[k * ROWS : (k + 1) * ROWS, :] = grads[block][...]
    both = lambda rows, others: sum(
        t_matmul(rows[k * pair : (k + 1) * pair, :], other[...]) for k, other in enumerate(others)
    )
    out[:, :wide] = both(rows_s, grad_units).astype(bf16)
    out[:, wide:] = both(rows_g, hidden).astype(bf16)


def feed_weights(second, grads, grad_units, hidden):
    width = second[0].shape[1]
    pair, wide = grad_units[0].shape
    units = hidden[0].shape[1]
    return pl.pallas_call(
        feed_weights_kernel,
        grid=(width // 512,),
        in_specs=[
            *[pl.BlockSpec((ROWS, 512), lambda i: (0, i))] * 8,
            *[whole((pair, wide))] * 2,
            *[whole((pair, units))] * 2,
        ],
        out_specs=pl.BlockSpec((512, wide + units), lambda i: (i, 0)),
        out_shape=pltpu.HBM((width, wide + units), bf16),
        scratch_shapes=[pltpu.VMEM((2 * pair, 512), bf16)] * 2,
        compiler_params=params(24),
        cost_estimate=cost(4.8e9, 14e6),
        name="feed_weights",
    )(*map(far, second), *map(far, grads), *map(far, grad_units), *map(far, hidden))


def middle_back_kernel(middle, mine, from_core, from_z, cotangent, gain, grad_middle, branch, gain_part):
    u = mine[...].astype(f32) + from_core[...].astype(f32) + from_z[...].astype(f32)
    grad, part = norm_back(middle[...], gain[1:2, :], u)
    grad = cotangent[...].astype(f32) + grad
    grad_middle[...] = grad
    branch[...] = grad.astype(bf16)

    @pl.when(pl.program_id(0) == 0)
    def _():
        gain_part[...] = jnp.zeros_like(gain_part)

    gain_part[:1, :] += part


def middle_back(middle, part, from_core, from_z, cotangent, gain):
    width = middle.shape[1]
    half = ROWS // 2
    row = pl.BlockSpec((half, width), lambda i: (i, 0))
    return pl.pallas_call(
        middle_back_kernel,
        grid=(2,),
        in_specs=[row, row, row, row, row, whole((8, width))],
        out_specs=[row, row, whole_out((8, width))],
        out_shape=[
            pltpu.HBM((ROWS, width), f32),
            jax.ShapeDtypeStruct((ROWS, width), bf16),
            pltpu.HBM((8, width), f32),
        ],
        compiler_params=params(14),
        cost_estimate=cost(4e6, 5e6),
        name="middle_back",
    )(far(middle), part, from_core, from_z, far(cotangent), gain)


def backward_attention_kernel(per_device, place, *refs):
    branch = refs[:4]
    tokens = refs[4:8]
    weights, first, att_out, low, totals, qraw, kraw, cos, sin, head_gains, second_gain = refs[8:19]
    mine, other, out = refs[19:22]
    matrices, rows_all, xs_all, first_all, att, grads_all, block = refs[22:29]
    grad_att, dk, dv, dq, gain_part, head_part, row_sems, matrix_sems, out_sems = refs[29:]
    qgain, kgain = head_gains[:1, :], head_gains[1:2, :]
    step_id = pl.program_id(0)
    i = pl.num_programs(0) - 1 - step_id
    nq, nk = qraw.shape[1], kraw.shape[1]

    @pl.when(step_id == 0)
    def _():
        gain_part[...] = jnp.zeros_like(gain_part)
        head_part[...] = jnp.zeros_like(head_part)

    nqkv = nq + 2 * nk
    wqkv = matrices.at[:, :nqkv]
    wo = matrices.at[:, nqkv:]
    load_o = pltpu.make_async_copy(weights.at[:, nqkv : nqkv + nq], wo, matrix_sems.at[0])
    load_qkv = pltpu.make_async_copy(weights.at[:, :nqkv], wqkv, matrix_sems.at[1])
    load_att = pltpu.make_async_copy(att_out, att, matrix_sems.at[2])
    load_first = pltpu.make_async_copy(first, first_all, matrix_sems.at[3])
    loads = []
    for pieces, target, sem in ((branch, rows_all, row_sems.at[0]), (tokens, xs_all, row_sems.at[1])):
        for k, piece in enumerate(pieces):
            at = pl.ds(pl.multiple_of(place[4 + k] * ROWS, ROWS), ROWS)
            loads.append(pltpu.make_async_copy(piece, target.at[at, :], sem.at[k]))

    @pl.when(step_id == 0)
    def _():
        for copy in [load_o, *loads[:4], load_att, load_qkv, *loads[4:], load_first]:
            copy.start()
        for copy in [load_o, *loads[:4], load_att]:
            copy.wait()

    here = pl.ds(pl.multiple_of(i * 2 * ROWS, 2 * ROWS), 2 * ROWS)
    grad_att[...] = matmul(rows_all[here, :], wo[...]).astype(bf16)
    mask_k = lax.broadcasted_iota(jnp.int32, (ROWS, GROUP * ROWS), 0)
    mask_q = lax.broadcasted_iota(jnp.int32, (ROWS, GROUP * ROWS), 1) % ROWS

    def attend_back(block):
        half = block % 2 * ROWS
        n = block * ROWS
        end = n + ROWS
        for h in range(nk // HD):
            cols = [(h * GROUP + a) * HD for a in range(GROUP)]
            q2 = jnp.concatenate([low[n:end, col : col + HD] for col in cols], axis=0)
            g2 = jnp.concatenate([grad_att[half : half + ROWS, col : col + HD] for col in cols], axis=0)
            o2 = jnp.concatenate([att[n:end, col : col + HD] for col in cols], axis=0)
            total = totals[block % 2, h : h + 1, :]
            dot = jnp.sum((g2.astype(f32) * o2.astype(f32)).T, axis=0, keepdims=True)
            k = low[:end, nq + h * HD : nq + (h + 1) * HD]
            v = low[:end, nq + nk + h * HD : nq + nk + (h + 1) * HD]
            probs = jnp.exp2(matmul_t(k, q2) * log2_scale - total)
            last = jnp.where(mask_k <= mask_q, probs[n:], 0.0)
            probs = jnp.concatenate([probs[:n], last], axis=0) if n else last
            grad_scores = (probs * (matmul_t(v, g2) - dot)).astype(bf16)
            dv_part = matmul(probs.astype(bf16), g2)
            dk_part = matmul(grad_scores, q2)
            if end == keys:
                dv[h] = dv_part
                dk[h] = dk_part
            else:
                dv[h, :end, :] += dv_part
                dk[h, :end, :] += dk_part
            d = t_matmul(k, grad_scores).T * score_scale
            for a, col in enumerate(cols):
                dq[half : half + ROWS, col : col + HD] = d[a * ROWS : (a + 1) * ROWS]

    keys = low.shape[0]
    for k in range(keys // (2 * ROWS)):

        @pl.when(i == k)
        def _(k=k):
            attend_back(2 * k + 1)
            attend_back(2 * k)

    c, s = cos[...], sin[...]

    def unturned(w):
        return w * c - pltpu.roll(w, HD // 2, 1) * s

    for h in range(nq // HD):
        col = slice(h * HD, (h + 1) * HD)
        grad, gp = norm_back(qraw[:, col], qgain, unturned(dq[:, col]))
        grads_all[here, col] = grad.astype(bf16)
        head_part[:1, :] += gp
    for h in range(nk // HD):
        col = slice(h * HD, (h + 1) * HD)
        grad, gp = norm_back(kraw[:, col], kgain, unturned(dk[h, here, :] * score_scale))
        grads_all[here, nq + h * HD : nq + (h + 1) * HD] = grad.astype(bf16)
        head_part[1:2, :] += gp
        grads_all[here, nq + nk + h * HD : nq + nk + (h + 1) * HD] = dv[h, here, :].astype(bf16)
    @pl.when(step_id == 0)
    def _():
        for copy in [load_qkv, *loads[4:]]:
            copy.wait()

    upstream = matmul_t(grads_all[here, :], wqkv[...])
    put_pair(place[2 * i], upstream.astype(bf16), mine, other)
    x = xs_all[here, :].astype(f32)
    gain_part[:1, :] += jnp.sum(upstream * x * inverse_rms(x), axis=0, keepdims=True)

    @pl.when(step_id == pl.num_programs(0) - 1)
    def _():
        load_first.wait()
        more = nqkv + nq
        rows = 2 * ROWS
        stored = []
        for k in range(first_all.shape[1] // rows):
            at = slice(k * rows, (k + 1) * rows)
            block[at, :nqkv] = t_matmul(first_all[:, at], grads_all[...]).astype(bf16)
            block[at, nqkv:more] = t_matmul(rows_all[:, at], att[...]).astype(bf16)
            same = equal_iota(rows, rows, lambda r, c: r == c)
            stands = of_head(rows, per_device, k * rows)
            lane = lax.broadcasted_iota(jnp.int32, (rows, HD), 1)
            columns = jnp.zeros((rows, HD), f32)
            values = [
                (same, gain_part[:1, at]),
                (same, second_gain[:1, at]),
                (stands, head_part[:1, :]),
                (stands, head_part[1:2, :]),
            ]
            for m, (mask, line) in enumerate(values):
                column = jnp.sum(jnp.where(mask, line, 0.0), axis=1, keepdims=True)
                columns = jnp.where(lane == m, column, columns)
            block[at, more:] = columns.astype(bf16)
            stored.append(pltpu.make_async_copy(block.at[at, :], out.at[at, :], out_sems.at[k]))
            stored[-1].start()
        for copy in stored:
            copy.wait()


def backward_attention(
    place, branch, tokens, weights, first, low, att, totals, qraw, kraw, cos, sin, head_gains, second_gain
):
    n, width = 4, branch[0].shape[1]
    length, nqkv = low.shape
    nq, nk = qraw.shape[1], kraw.shape[1]
    total = nqkv + nq + HD
    row = lambda cols: pl.BlockSpec((2 * ROWS, cols), lambda i, p: (n // 2 - 1 - i, 0))
    half = pl.BlockSpec((1, ROWS, width), lambda i, p: (p[n - 2 - 2 * i] % 2, 0, 0))
    return pl.pallas_call(
        functools.partial(backward_attention_kernel, width // lax.axis_size(FSDP)),
        grid_spec=pltpu.PrefetchScalarGridSpec(
            num_scalar_prefetch=1,
            grid=(n // 2,),
            in_specs=[
                *[pl.BlockSpec(memory_space=pl.ANY)] * 11,
                whole((length, nqkv)),
                pl.BlockSpec((2, 8, GROUP * ROWS), lambda i, p: (n // 2 - 1 - i, 0, 0)),
                row(nq),
                row(nk),
                row(HD),
                row(HD),
                whole((8, HD)),
                whole((8, width)),
            ],
            out_specs=[half, half, pl.BlockSpec(memory_space=pltpu.HBM)],
            scratch_shapes=[
                pltpu.VMEM((width, nqkv + nq), bf16),
                pltpu.VMEM((length, width), bf16),
                pltpu.VMEM((length, width), bf16),
                pltpu.VMEM((length, width), bf16),
                pltpu.VMEM((length, nq), bf16),
                pltpu.VMEM((length, nqkv), bf16),
                pltpu.VMEM((width, total), bf16),
                pltpu.VMEM((2 * ROWS, nq), bf16),
                pltpu.VMEM((nk // HD, length, HD), f32),
                pltpu.VMEM((nk // HD, length, HD), f32),
                pltpu.VMEM((2 * ROWS, nq), f32),
                pltpu.VMEM((8, width), f32),
                pltpu.VMEM((8, HD), f32),
                pltpu.SemaphoreType.DMA((2, 4)),
                pltpu.SemaphoreType.DMA((4,)),
                pltpu.SemaphoreType.DMA((width // (2 * ROWS),)),
            ],
        ),
        out_shape=[
            pltpu.HBM((2, ROWS, width), bf16),
            pltpu.HBM((2, ROWS, width), bf16),
            pltpu.HBM((width, total), bf16),
        ],
        compiler_params=params(46),
        cost_estimate=cost(6e11, 18e6, 3e6),
        name="backward_attention",
    )(
        place, *branch, *map(far, tokens), far(weights), far(first), far(att), far(low), far(totals),
        far(qraw), far(kraw), far(cos), far(sin), far(head_gains), far(second_gain),
    )


def tokens_back_kernel(tokens, mine, from_core, from_z, grad_middle, gain, grad_tokens):
    u = mine[...].astype(f32) + from_core[...].astype(f32) + from_z[...].astype(f32)
    grad, _ = norm_back(tokens[...].astype(f32), gain[:1, :], u)
    grad_tokens[...] = grad_middle[...] + grad


def tokens_back(tokens, mine, from_core, from_z, grad_middle, gain):
    width = tokens.shape[1]
    half = ROWS // 2
    row = pl.BlockSpec((half, width), lambda i: (i, 0))
    first = pl.BlockSpec((None, half, width), lambda i: (0, i, 0))
    return pl.pallas_call(
        tokens_back_kernel,
        grid=(2,),
        in_specs=[row, first, first, row, row, whole((8, width))],
        out_specs=row,
        out_shape=pltpu.HBM((ROWS, width), f32),
        compiler_params=params(14),
        cost_estimate=cost(4e6, 4e6),
        name="tokens_back",
    )(far(tokens), mine, from_core, from_z, far(grad_middle), far(gain))


def close(zh, parts):
    senders, both, wide = parts.shape
    rows = both // 2

    def kernel(zh, parts, keep, give):
        for which, out in ((zh[0], keep), (1 - zh[0], give)):
            at = pl.ds(pl.multiple_of(which * rows, rows), rows)
            added = parts[0, at, :].astype(f32)
            for k in range(1, senders):
                added = added + parts[k, at, :].astype(f32)
            out[...] = added.astype(out.dtype)

    return pl.pallas_call(
        kernel,
        grid_spec=pltpu.PrefetchScalarGridSpec(
            num_scalar_prefetch=1,
            grid=(1,),
            in_specs=[whole(parts.shape)],
            out_specs=[whole_out((rows, wide))] * 2,
        ),
        out_shape=[
            jax.ShapeDtypeStruct((rows, wide), f32),
            jax.ShapeDtypeStruct((rows, wide), bf16),
        ],
        compiler_params=params(14),
        cost_estimate=cost(2e6, 4e6),
        name="close",
    )(zh, far(parts) if senders == 1 else parts)


def finish(keep, arrived, widths):
    rows = keep.shape[0]

    def kernel(keep, arrived, *outs):
        at = 0
        for out in outs:
            some = slice(at, at + out.shape[1])
            out[...] = keep[:, some] + arrived[:, some].astype(f32)
            at += out.shape[1]

    return pl.pallas_call(
        kernel,
        out_shape=[jax.ShapeDtypeStruct((rows, w), f32) for w in widths],
        compiler_params=params(8),
        cost_estimate=cost(1e5, 1e6),
        name="finish",
    )(keep, arrived)


def finish_gains(parts, rows, heads):
    def kernel(*refs):
        total = refs[0][...] + refs[1][...] + refs[2][...] + refs[3][...]
        same = equal_iota(rows, rows, lambda r, c: r == c)
        for k, out in enumerate(refs[4:]):
            line = jnp.sum(jnp.where(same, total[:, k : k + 1], 0.0), axis=0, keepdims=True)
            out[...] = line[:, : out.shape[1]]

    widths = (rows, rows, heads, heads)
    outs = pl.pallas_call(
        kernel,
        out_shape=[jax.ShapeDtypeStruct((1, w), f32) for w in widths],
        compiler_params=params(4),
        cost_estimate=cost(1e4, 1e5),
        name="finish_gains",
    )(*parts)
    return [out.reshape(-1) for out in outs]


def pack(first, second, gains, rows, heads):
    widths = [a.shape[1] for a in first], [a.shape[1] for a in second]
    split = sum(widths[0])

    def kernel(gains, *refs):
        out = refs[-1]
        at = 0
        for k, ref in enumerate(refs[:-1]):
            at += HD * (k == len(first))
            out[:, at : at + ref.shape[1]] = ref[...]
            at += ref.shape[1]
        g = gains[...].astype(f32)
        lane = lax.broadcasted_iota(jnp.int32, (rows, HD), 1)
        line = lax.broadcasted_iota(jnp.int32, (rows, HD), 0)
        columns = jnp.zeros((rows, HD), f32)
        places = [(0, rows), (rows, rows), (2 * rows, heads), (2 * rows + heads, heads)]
        for k, (start, count) in enumerate(places):
            mask = (lane == line + start) & (line < count)
            column = jnp.sum(jnp.where(mask, g, 0.0), axis=1, keepdims=True)
            columns = jnp.where(lane == k, column, columns)
        out[:, split : split + HD] = columns.astype(bf16)

    return pl.pallas_call(
        kernel,
        out_shape=jax.ShapeDtypeStruct((rows, split + HD + sum(widths[1])), bf16),
        compiler_params=params(8),
        cost_estimate=cost(1e3, 5e5),
        name="pack",
    )(gains, *map(far, first), *map(far, second))


def pair(zh, shard, other, cut, split):
    rows, wide = shard.shape

    def kernel(zh, shard, other, left, right, rest):
        for k, ref in enumerate((shard, other)):
            left[k] = ref[:, :cut]
            right[k] = ref[:, cut:split]
            rest[pl.ds(pl.multiple_of((zh[0] ^ k) * rows, rows), rows), :] = ref[:, split:]

    shapes = [(2, rows, cut), (2, rows, split - cut), (2 * rows, wide - split)]
    return pl.pallas_call(
        kernel,
        grid_spec=pltpu.PrefetchScalarGridSpec(
            num_scalar_prefetch=1,
            grid=(1,),
            in_specs=[whole((rows, wide))] * 2,
            out_specs=[whole_out(s) for s in shapes],
        ),
        out_shape=[
            *[jax.ShapeDtypeStruct(s, bf16) for s in shapes[:2]],
            pltpu.HBM(shapes[2], bf16),
        ],
        compiler_params=params(8),
        cost_estimate=cost(1e3, 1e6),
        name="pair",
    )(zh, shard, other)


def load_pieces(order, pieces, target, semaphores):
    copies = []
    half = len(pieces) // 2
    cut = pieces[0].shape[3]
    for side in range(2):
        n = 0
        for piece in pieces[side * half : (side + 1) * half]:
            rows, wide = piece.shape[2:]
            for j in range(piece.shape[0]):
                for k in range(2):
                    place = pl.multiple_of(order[side, n] * rows, rows)
                    copy = pltpu.make_async_copy(
                        piece.at[j, k],
                        target.at[pl.ds(place, rows), side * cut : side * cut + wide],
                        semaphores.at[side, n],
                    )
                    copies.append(copy)
                    n += 1
    return copies


def swapped(value, axis):
    return lax.ppermute(value, axis, [(0, 1), (1, 0)])


def tp_gather(own, over_z=None):
    over_z = swapped(own, "zl") if over_z is None else over_z
    return [own, over_z, swapped(own, "core"), swapped(over_z, "core")]


def tp_scatter(mine, other):
    from_core = swapped(other, "core")
    passed = (mine[1].astype(f32) + from_core[1].astype(f32)).astype(bf16)
    return mine, from_core, swapped(passed, "zl"), passed


def after(value, *others):
    return lax.optimization_barrier((value, *others))[0]


def sent_rows(part):
    planes = lax.axis_size(PLANE)
    blocks = part.reshape(planes, part.shape[0] // planes, part.shape[1])
    return lax.all_to_all(blocks, PLANE, 0, 0, tiled=True)


def by_distance(sides, staged):
    done = [{0: own} for own, _ in sides]
    before = []
    for near in (True, False):
        arrived = []
        for kept, (own, axis) in zip(done, sides):
            n = lax.axis_size(axis)
            for j in range(1, n):
                if (j in (1, n - 1)) == near:
                    perm = [(s, (s - j) % n) for s in range(n)]
                    kept[j] = lax.ppermute(after(own, *before) if before else own, axis, perm)
                    arrived.append(kept[j])
        before = arrived if staged else []
    return [[kept[j] for j in sorted(kept)] for kept in done]


def gathered_order():
    nx, ny = lax.axis_size("x"), lax.axis_size("y")
    x, y = (lax.axis_index("x") + jnp.arange(nx)) % nx, (lax.axis_index("y") + jnp.arange(ny)) % ny
    z = lax.axis_index("zh") ^ jnp.arange(2)
    block = lambda x, y: ((x * ny + y) * 2 + z).reshape(-1)
    left = block(x[None, :, None], y[:, None, None])
    right = block(x[:, None, None], y[None, :, None])
    return jnp.stack([left, right]).astype(jnp.int32)


def rotary_tables(length):
    midway = HD // 2
    frequency = 1.0 / rope_base ** (np.arange(midway) * 2.0 / HD)
    angles = np.arange(length)[:, None] * frequency[None, :]
    cos, sin = np.cos(angles), np.sin(angles)
    tables = np.concatenate([cos, cos], axis=1), np.concatenate([-sin, sin], axis=1)
    return [jnp.asarray(t.astype(np.float32)) for t in tables]


def local(
    tokens,
    attention_gain,
    query_weight,
    key_weight,
    value_weight,
    query_gain,
    key_gain,
    output_weight,
    feed_gain,
    gate_weight,
    up_weight,
    down_weight,
    cotangent,
):
    width = tokens.shape[2]
    nq, nk = query_weight.shape[1], key_weight.shape[1]
    units = gate_weight.shape[1]
    rows = query_weight.shape[0]
    x = tokens[0]
    dy = cotangent[0]
    zl, core = lax.axis_index("zl"), lax.axis_index("core")
    block = jnp.arange(4, dtype=jnp.int32)
    place = ((block % 2) ^ core) * 2 + ((block // 2) ^ zl)
    block_of = ((block // 2) ^ core) + ((block % 2) ^ zl) * 2
    place = jnp.concatenate([place, block_of]).astype(jnp.int32)
    cos, sin = rotary_tables(4 * ROWS)

    heads = query_gain.shape[0]
    gains = jnp.concatenate([attention_gain, feed_gain, query_gain, key_gain])
    gains = jnp.pad(gains, (0, HD - gains.shape[0]))[None]
    shard = pack(
        [query_weight, key_weight, value_weight, output_weight],
        [gate_weight, up_weight, down_weight],
        gains,
        rows,
        heads,
    )
    over_zh = swapped(shard, "zh")
    split = nq + 2 * nk + nq + HD
    left, right, feed = pair(lax.axis_index("zh").reshape(1), shard, over_zh, nq + nk, split)
    order = gathered_order()
    left, right = by_distance([(left, "x"), (right, "y")], False)
    token_blocks = tp_gather(after(x, over_zh))
    left, right = by_distance([(jnp.stack(left), "y"), (jnp.stack(right), "x")], True)
    feed = lax.all_gather(after(feed, left[1], left[-1], right[1], right[-1]), PLANE, axis=0, tiled=True)
    grads_over_z = swapped(after(dy, *left, *right), "zl")

    first, qraw, kraw, low, att, totals, mine, other, gains, head_gains, weights = forward_attention(
        place, order, token_blocks, left + right, nq, nk, cos, sin
    )
    grad_blocks = tp_gather(dy, after(grads_over_z, other))
    other = after(other, grads_over_z)
    mine, from_core, from_z, _ = tp_scatter(mine, other)
    middle, second = middle_step(x, mine, from_core, from_z, gains)
    over_z = swapped(second, "zl")
    near = feed_step([second, swapped(second, "core")], grad_blocks[::2], feed, units)
    second_blocks = tp_gather(second, after(over_z, near[1]))
    far_ones = feed_step(second_blocks[1::2], grad_blocks[1::2], feed, units)
    hidden, grad_units = [near[0], far_ones[0]], [near[1], far_ones[1]]
    from_core = swapped(near[3], "core")
    passed = (after(far_ones[2], from_core).astype(f32) + swapped(far_ones[3], "core").astype(f32)).astype(bf16)
    from_z = swapped(passed, "zl")
    grad_units[0] = after(grad_units[0], passed)
    feed_grads = feed_weights(second_blocks, grad_blocks, grad_units, hidden)
    from_z = after(from_z, feed_grads)
    grad_middle, branch, feed_gain_part = middle_back(middle, near[2], from_core, from_z, dy, gains)
    feed_sums = lax.psum_scatter(feed_grads, "x", scatter_dimension=0, tiled=True)
    feed_sums = lax.psum_scatter(feed_sums, "y", scatter_dimension=0, tiled=True)
    over_z = swapped(branch, "zl")
    mine, other = feed_out([after(hidden[0], branch), hidden[1]], feed)
    branch_blocks = tp_gather(branch, after(over_z, other))
    mine, from_core, from_z, _ = tp_scatter(mine, other)
    output = middle + mine[0].astype(f32) + from_core[0].astype(f32) + from_z.astype(f32)
    output = output.astype(bf16)

    mine, other, projection_grads = backward_attention(
        place, branch_blocks, token_blocks, weights, first, low, att, totals, qraw, kraw, cos, sin,
        head_gains, feed_gain_part,
    )
    mine, from_core, from_z, _ = tp_scatter(mine, other)
    tokens_grad = tokens_back(
        x, mine, from_core, after(from_z, projection_grads), grad_middle, gains
    )
    parts = after(sent_rows(projection_grads), tokens_grad, output)
    zh = lax.axis_index("zh").reshape(1)
    keep, give = close(zh, parts)
    arrived = swapped(give, "zh")
    query, key, value, out, columns = finish(keep, arrived, (nq, nk, nk, nq, HD))
    feed_keep, feed_give = close(zh, after(feed_sums, arrived)[None])
    gate, up, down = finish(feed_keep, swapped(feed_give, "zh"), (units, units, units))
    both = ("zl", "core")
    across = lax.ppermute(columns, both, [(s, 3 - s) for s in range(4)])
    parts = (columns, swapped(columns, "zl"), swapped(columns, "core"), across)
    first_sum, second_sum, query_sum, key_sum = finish_gains(parts, rows, heads)

    return (
        output[None],
        tokens_grad[None],
        first_sum,
        query,
        key,
        value,
        query_sum,
        key_sum,
        out,
        second_sum,
        gate,
        up,
        down,
    )


def solution(mesh):
    fsdp, tp = mesh.devices.shape
    cut = {32: (4, 4, 2), 2: (1, 1, 2), 1: (1, 1, 1)}[fsdp]
    fine = Mesh(mesh.devices.reshape(*cut, 2, tp // 2), EVERY)
    split = ("zl", "core")
    data = P(FSDP, split, None)
    matrix = P(FSDP, split)
    vector = P(FSDP)
    return jax.shard_map(
        local,
        mesh=fine,
        in_specs=(
            data, vector, matrix, matrix, matrix, vector, vector,
            matrix, vector, matrix, matrix, matrix, data,
        ),
        out_specs=(
            data, data, vector, matrix, matrix, matrix, vector, vector,
            matrix, vector, matrix, matrix, matrix,
        ),
        check_vma=False,
    )
```

```python
import functools
import math

import jax
import jax.numpy as jnp
import numpy as np
from jax import lax
from jax.experimental import pallas as pl
from jax.experimental.pallas import tpu as pltpu
from jax.sharding import Mesh, PartitionSpec as P

HD = 128
ROWS = 256
WIDTH = 1024
GROUP = 2
CHUNK = 256
BLOCK_ORDER = (0, 2, 1, 3)
epsilon = 1e-06
rope_base = 1000000.0
score_scale = 1.0 / math.sqrt(HD)
log2_scale = score_scale / math.log(2.0)
FSDP = ("x", "y", "zh")
PLANE = ("x", "y")
EVERY = ("x", "y", "zh", "zl", "core")
f32 = jnp.float32
bf16 = jnp.bfloat16


def matmul(a, b):
    return lax.dot_general(a, b, (((1,), (0,)), ((), ())), preferred_element_type=f32)


def matmul_t(a, b):
    return lax.dot_general(a, b, (((1,), (1,)), ((), ())), preferred_element_type=f32)


def t_matmul(a, b):
    return lax.dot_general(a, b, (((0,), (0,)), ((), ())), preferred_element_type=f32)


def inverse_rms(values):
    return lax.rsqrt(jnp.mean(values * values, axis=-1, keepdims=True) + epsilon)


def norm_back(values, gain, upstream):
    inverse = inverse_rms(values)
    scaled = gain * upstream
    moment = jnp.mean(scaled * values, axis=-1, keepdims=True)
    grad = inverse * scaled - values * (inverse * inverse * inverse) * moment
    return grad, jnp.sum(upstream * values * inverse, axis=0, keepdims=True)


def far(value):
    return pltpu.with_memory_space_constraint(value, pltpu.HBM)


def params(mib):
    return pltpu.CompilerParams(vmem_limit_bytes=mib * 1024 * 1024)


def cost(flops, nbytes, trans=0):
    return pl.CostEstimate(flops=int(flops / 8), bytes_accessed=int(nbytes / 8), transcendentals=int(trans / 8))


def whole(shape, index=None):
    index = index or (0,) * len(shape)
    return pl.BlockSpec(shape, lambda i, *_: index, pipeline_mode=pl.Buffered(1))


def halves(width):
    return [
        pl.BlockSpec((1, ROWS, width), lambda i: (jnp.minimum(i, 1), 0, 0)),
        pl.BlockSpec((1, ROWS, width), lambda i: (jnp.maximum(i - 2, 0), 0, 0)),
    ]


def whole_out(shape):
    return pl.BlockSpec(shape, lambda i, *_: (0,) * len(shape))


def pick(which, pieces, target):
    for k, piece in enumerate(pieces):

        @pl.when(which == k)
        def _(piece=piece):
            target[...] = piece[...]


def equal_iota(rows, cols, make):
    r = lax.broadcasted_iota(jnp.int32, (rows, cols), 0)
    c = lax.broadcasted_iota(jnp.int32, (rows, cols), 1)
    return make(r, c)


def row_of(columns, k):
    same = equal_iota(128, 128, lambda r, c: r == c)
    parts = []
    for m in range(columns.shape[0] // 128):
        col = columns[m * 128 : (m + 1) * 128, k : k + 1].astype(f32)
        parts.append(jnp.sum(jnp.where(same, col, 0.0), axis=0, keepdims=True))
    return jnp.concatenate(parts, axis=1)


def of_head(rows, per_device, first_row=0):
    held = HD * per_device // WIDTH
    return equal_iota(
        rows, HD, lambda r, c: ((r + first_row) // per_device * held + (r + first_row) % per_device == c)
        & ((r + first_row) % per_device < held)
    )


def heads_of(columns, k, per_device):
    col = columns[:, k : k + 1].astype(f32)
    return jnp.sum(jnp.where(of_head(columns.shape[0], per_device), col, 0.0), axis=0, keepdims=True)


def put_pair(which, value, mine, other):
    top, bottom = value[:ROWS], value[ROWS:]

    @pl.when(which < 2)
    def _():
        mine[0] = top
        other[0] = bottom

    @pl.when(which >= 2)
    def _():
        mine[0] = bottom
        other[0] = top


def put(which, value, mine, other):
    @pl.when(which < 2)
    def _():
        mine[0] = value

    @pl.when(which >= 2)
    def _():
        other[0] = value


def forward_attention_kernel(per_device, n_pieces, place, order, *refs):
    tokens = refs[:4]
    pieces, refs = refs[4 : 4 + n_pieces], refs[4 + n_pieces :]
    cos, sin = refs[:2]
    first, qraw, kraw, low, att, totals, mine, other, gains, head_gains, ordered = refs[2:13]
    rows, scaled, keys, values, weights, piece_sems, ordered_sem = refs[13:]
    i = pl.program_id(0)
    nq, nqkv = qraw.shape[1], low.shape[1]
    wqkv = weights.at[:, :nqkv]
    wo = weights.at[:, nqkv : nqkv + nq]
    columns = weights.at[:, nqkv + nq :]
    keep = pltpu.make_async_copy(weights, ordered, ordered_sem)
    loads = load_pieces(order, pieces, weights, piece_sems)

    @pl.when(i == 0)
    def _():
        for copy in loads:
            copy.start()

    for a in range(2):
        pick(place[2 * i + a], tokens, rows.at[a * ROWS : (a + 1) * ROWS, :])
    x = rows[...].astype(f32)
    scaled[...] = x * inverse_rms(x)

    @pl.when(i == 0)
    def _():
        for copy in loads:
            copy.wait()
        keep.start()
        gains[:2, :] = jnp.concatenate([row_of(columns, 0), row_of(columns, 1)], axis=0)
        gains[2:, :] = jnp.zeros_like(gains[2:, :])
        head_gains[:2, :] = jnp.concatenate([heads_of(columns, k, per_device) for k in (2, 3)], axis=0)
        head_gains[2:, :] = jnp.zeros_like(head_gains[2:, :])

    gain, qgain, kgain = gains[:1, :], head_gains[:1, :], head_gains[1:2, :]
    normed = (scaled[...] * gain).astype(bf16)
    first[...] = normed
    qkv = matmul(normed, wqkv[...])
    nq, nk = qraw.shape[1], kraw.shape[1]
    qraw[...] = qkv[:, :nq]
    kraw[...] = qkv[:, nq : nq + nk]
    here = pl.ds(pl.multiple_of(i * 2 * ROWS, 2 * ROWS), 2 * ROWS)
    c, s = cos[...], sin[...]

    def turned(v, g):
        n = v * inverse_rms(v) * g
        return (n * c + pltpu.roll(n, HD // 2, 1) * s).astype(bf16)

    for h in range(nk // HD):
        k_low = turned(qkv[:, nq + h * HD : nq + (h + 1) * HD], kgain)
        v_low = qkv[:, nq + nk + h * HD : nq + nk + (h + 1) * HD].astype(bf16)
        low[:, nq + h * HD : nq + (h + 1) * HD] = k_low
        low[:, nq + nk + h * HD : nq + nk + (h + 1) * HD] = v_low
        keys[h, here, :] = k_low
        values[h, here, :HD] = v_low
        values[h, here, HD:] = jnp.ones((2 * ROWS, HD), bf16)
    for h in range(nq // HD):
        low[:, h * HD : (h + 1) * HD] = turned(qkv[:, h * HD : (h + 1) * HD], qgain)
    mask_q = lax.broadcasted_iota(jnp.int32, (GROUP * ROWS, ROWS), 0) % ROWS
    mask_k = lax.broadcasted_iota(jnp.int32, (GROUP * ROWS, ROWS), 1)

    def attend(block):
        half = block % 2 * ROWS
        n = block * ROWS
        sums = []
        for h in range(nk // HD):
            cols = [(h * GROUP + a) * HD for a in range(GROUP)]
            q2 = jnp.concatenate([low[half : half + ROWS, col : col + HD] for col in cols], axis=0)
            scores = matmul_t(q2, keys[h, : n + ROWS, :]) * log2_scale
            weights = jnp.exp2(scores[:, n:])
            weights = jnp.where(mask_k <= mask_q, weights, 0.0).astype(bf16)
            if n:
                weights = jnp.concatenate([jnp.exp2(scores[:, :n]).astype(bf16), weights], axis=1)
            acc = matmul(weights, values[h, : n + ROWS, :])
            total = acc[:, HD:]
            o = (acc[:, :HD] / total).astype(bf16)
            for a, col in enumerate(cols):
                att[half : half + ROWS, col : col + HD] = o[a * ROWS : (a + 1) * ROWS]
            sums.append(jnp.log2(total).T[:1, :])
        sums = jnp.concatenate(sums + [jnp.zeros((8 - len(sums), GROUP * ROWS), f32)], axis=0)
        totals[block % 2] = sums

    for k in range(2):

        @pl.when(i == k)
        def _(k=k):
            attend(2 * k)
            attend(2 * k + 1)

    put_pair(place[2 * i], matmul_t(att[...], wo[...]).astype(bf16), mine, other)

    @pl.when(i == pl.num_programs(0) - 1)
    def _():
        keep.wait()


def forward_attention(place, order, tokens, pieces, nq, nk, cos, sin):
    n, width = 4, tokens[0].shape[1]
    length = n * ROWS
    nqkv = nq + 2 * nk
    row = lambda cols: pl.BlockSpec((2 * ROWS, cols), lambda i, p, o: (i, 0))
    out = [
        ((length, width), bf16, row(width)),
        ((length, nq), f32, row(nq)),
        ((length, nk), f32, row(nk)),
        ((length, nqkv), bf16, row(nqkv)),
        ((length, nq), bf16, row(nq)),
        ((n, 8, GROUP * ROWS), f32, pl.BlockSpec((2, 8, GROUP * ROWS), lambda i, p, o: (i, 0, 0))),
        *[((2, ROWS, width), bf16, pl.BlockSpec((1, ROWS, width), lambda i, p, o: (p[2 * i] % 2, 0, 0)))] * 2,
        ((8, width), f32, whole_out((8, width))),
        ((8, HD), f32, whole_out((8, HD))),
        ((width, nqkv + nq + HD), bf16, pl.BlockSpec(memory_space=pltpu.HBM)),
    ]
    return pl.pallas_call(
        functools.partial(forward_attention_kernel, width // lax.axis_size(FSDP), len(pieces)),
        grid_spec=pltpu.PrefetchScalarGridSpec(
            num_scalar_prefetch=2,
            grid=(n // 2,),
            in_specs=[
                *[whole((ROWS, width))] * 4,
                *[pl.BlockSpec(memory_space=pl.ANY)] * len(pieces),
                row(HD),
                row(HD),
            ],
            out_specs=[o[2] for o in out],
            scratch_shapes=[
                pltpu.VMEM((2 * ROWS, width), bf16),
                pltpu.VMEM((2 * ROWS, width), f32),
                pltpu.VMEM((nk // HD, length, HD), bf16),
                pltpu.VMEM((nk // HD, length, 2 * HD), bf16),
                pltpu.VMEM((width, nqkv + nq + HD), bf16),
                pltpu.SemaphoreType.DMA(order.shape),
                pltpu.SemaphoreType.DMA,
            ],
        ),
        out_shape=[(pltpu.HBM if k < 6 or k == 10 else jax.ShapeDtypeStruct)(o[0], o[1]) for k, o in enumerate(out)],
        compiler_params=params(24),
        cost_estimate=cost(7e9, 16e6, 3e6),
        name="forward_attention",
    )(place, order, far(tokens[0]), *tokens[1:], *map(far, pieces), far(cos), far(sin))


def middle_kernel(tokens, mine, from_core, from_z, gain, middle, second):
    total = mine[...].astype(f32) + from_core[...].astype(f32) + from_z[...].astype(f32)
    v = tokens[...].astype(f32) + total
    middle[...] = v
    second[...] = (v * inverse_rms(v) * gain[1:2, :]).astype(bf16)


def middle_step(tokens, part, from_core, from_z, gain):
    width = tokens.shape[1]
    half = ROWS // 2
    row = pl.BlockSpec((half, width), lambda i: (i, 0))
    first = pl.BlockSpec((None, half, width), lambda i: (0, i, 0))
    return pl.pallas_call(
        middle_kernel,
        grid=(2,),
        in_specs=[row, first, first, row, whole((8, width))],
        out_specs=[row, row],
        out_shape=[pltpu.HBM((ROWS, width), f32), jax.ShapeDtypeStruct((ROWS, width), bf16)],
        compiler_params=params(12),
        cost_estimate=cost(2e6, 4e6),
        name="middle_step",
    )(far(tokens), part, from_core, from_z, gain)


def feed_kernel(*refs):
    second, grads, weights = refs[:2], refs[2:4], refs[4]
    hidden, grad_units, mine, other = refs[5:9]
    rows_s, rows_g, matrices, row_sems, matrix_sems = refs[9:]
    units = hidden.shape[1]
    loads = []
    for k in range(2):
        at = slice(k * ROWS, (k + 1) * ROWS)
        loads.append(pltpu.make_async_copy(second[k], rows_s.at[at, :], row_sems.at[0, k]))
        loads.append(pltpu.make_async_copy(grads[k], rows_g.at[at, :], row_sems.at[1, k]))
    chunks = []
    for c in range(units // CHUNK):
        for m in range(3):
            some = slice(m * units + c * CHUNK, m * units + (c + 1) * CHUNK)
            chunks.append(
                pltpu.make_async_copy(weights.at[:, some], matrices.at[:, some], matrix_sems.at[m, c])
            )
    for copy in loads + chunks:
        copy.start()
    for copy in loads:
        copy.wait()
    s, g = rows_s[...], rows_g[...]
    for c, at in enumerate(range(0, units, CHUNK)):
        for copy in chunks[3 * c : 3 * c + 3]:
            copy.wait()
        gate = matmul(s, matrices[:, at : at + CHUNK])
        up = matmul(s, matrices[:, units + at : units + at + CHUNK])
        gh = matmul(g, matrices[:, 2 * units + at : 2 * units + at + CHUNK])
        sig = 0.5 * jnp.tanh(0.5 * gate) + 0.5
        swish = gate * sig
        hidden[:, at : at + CHUNK] = (swish * up).astype(bf16)
        grad_units[:, at : at + CHUNK] = (gh * up * (sig + swish * (1.0 - sig))).astype(bf16)
        grad_units[:, units + at : units + at + CHUNK] = (gh * swish).astype(bf16)
    part = matmul_t(grad_units[...], matrices[:, : 2 * units]).astype(bf16)
    mine[...] = part[:ROWS]
    other[...] = part[ROWS:]


def feed_step(second, grads, weights, units):
    width = second[0].shape[1]
    return pl.pallas_call(
        feed_kernel,
        in_specs=[pl.BlockSpec(memory_space=pl.ANY)] * 5,
        out_shape=[
            pltpu.HBM((2 * ROWS, units), bf16),
            pltpu.HBM((2 * ROWS, 2 * units), bf16),
            *[jax.ShapeDtypeStruct((ROWS, width), bf16)] * 2,
        ],
        scratch_shapes=[
            *[pltpu.VMEM((2 * ROWS, width), bf16)] * 2,
            pltpu.VMEM((width, 3 * units), bf16),
            pltpu.SemaphoreType.DMA((2, 2)),
            pltpu.SemaphoreType.DMA((3, units // CHUNK)),
        ],
        compiler_params=params(20),
        cost_estimate=cost(4e9, 8e6, 1e6),
        name="feed_step",
    )(*second, *map(far, grads), far(weights))


def feed_out_kernel(first, then, wd, mine, other):
    for k, hidden in enumerate((first, then)):

        @pl.when(pl.program_id(0) == k)
        def _(hidden=hidden):
            part = matmul_t(hidden[...], wd[...]).astype(bf16)
            mine[0] = part[:ROWS]
            other[0] = part[ROWS:]


def feed_out(hidden, weights):
    pair, units = hidden[0].shape
    width = weights.shape[0]
    block = pl.BlockSpec((1, ROWS, width), lambda i: (i, 0, 0))
    return pl.pallas_call(
        feed_out_kernel,
        grid=(2,),
        in_specs=[whole((pair, units)), whole((pair, units)), whole((width, units), (0, 2))],
        out_specs=[block, block],
        out_shape=[pltpu.HBM((2, ROWS, width), bf16)] * 2,
        compiler_params=params(20),
        cost_estimate=cost(1.6e9, 5e6),
        name="feed_out",
    )(*map(far, hidden), far(weights))


def feed_weights_kernel(*refs):
    second, grads, grad_units, hidden = refs[:4], refs[4:8], refs[8:10], refs[10:12]
    out, rows_s, rows_g = refs[12:]
    wide = grad_units[0].shape[1]
    pair = 2 * ROWS
    for k, block in enumerate(BLOCK_ORDER):
        rows_s[k * ROWS : (k + 1) * ROWS, :] = second[block][...]
        rows_g[k * ROWS : (k + 1) * ROWS, :] = grads[block][...]
    both = lambda rows, others: sum(
        t_matmul(rows[k * pair : (k + 1) * pair, :], other[...]) for k, other in enumerate(others)
    )
    out[:, :wide] = both(rows_s, grad_units).astype(bf16)
    out[:, wide:] = both(rows_g, hidden).astype(bf16)


def feed_weights(second, grads, grad_units, hidden):
    width = second[0].shape[1]
    pair, wide = grad_units[0].shape
    units = hidden[0].shape[1]
    return pl.pallas_call(
        feed_weights_kernel,
        grid=(width // 512,),
        in_specs=[
            *[pl.BlockSpec((ROWS, 512), lambda i: (0, i))] * 8,
            *[whole((pair, wide))] * 2,
            *[whole((pair, units))] * 2,
        ],
        out_specs=pl.BlockSpec((512, wide + units), lambda i: (i, 0)),
        out_shape=pltpu.HBM((width, wide + units), bf16),
        scratch_shapes=[pltpu.VMEM((2 * pair, 512), bf16)] * 2,
        compiler_params=params(24),
        cost_estimate=cost(4.8e9, 14e6),
        name="feed_weights",
    )(*map(far, second), *map(far, grads), *map(far, grad_units), *map(far, hidden))


def middle_back_kernel(middle, mine, from_core, from_z, cotangent, gain, grad_middle, branch, gain_part):
    u = mine[...].astype(f32) + from_core[...].astype(f32) + from_z[...].astype(f32)
    grad, part = norm_back(middle[...], gain[1:2, :], u)
    grad = cotangent[...].astype(f32) + grad
    grad_middle[...] = grad
    branch[...] = grad.astype(bf16)

    @pl.when(pl.program_id(0) == 0)
    def _():
        gain_part[...] = jnp.zeros_like(gain_part)

    gain_part[:1, :] += part


def middle_back(middle, part, from_core, from_z, cotangent, gain):
    width = middle.shape[1]
    half = ROWS // 2
    row = pl.BlockSpec((half, width), lambda i: (i, 0))
    return pl.pallas_call(
        middle_back_kernel,
        grid=(2,),
        in_specs=[row, row, row, row, row, whole((8, width))],
        out_specs=[row, row, whole_out((8, width))],
        out_shape=[
            pltpu.HBM((ROWS, width), f32),
            jax.ShapeDtypeStruct((ROWS, width), bf16),
            pltpu.HBM((8, width), f32),
        ],
        compiler_params=params(14),
        cost_estimate=cost(4e6, 5e6),
        name="middle_back",
    )(far(middle), part, from_core, from_z, far(cotangent), gain)


def backward_attention_kernel(per_device, place, *refs):
    branch = refs[:4]
    tokens = refs[4:8]
    weights, first, att_out, low, totals, qraw, kraw, cos, sin, head_gains, second_gain = refs[8:19]
    mine, other, out = refs[19:22]
    matrices, rows_all, xs_all, first_all, att, grads_all, block = refs[22:29]
    grad_att, dk, dv, dq, gain_part, head_part, row_sems, matrix_sems, out_sems = refs[29:]
    qgain, kgain = head_gains[:1, :], head_gains[1:2, :]
    step_id = pl.program_id(0)
    i = pl.num_programs(0) - 1 - step_id
    nq, nk = qraw.shape[1], kraw.shape[1]

    @pl.when(step_id == 0)
    def _():
        gain_part[...] = jnp.zeros_like(gain_part)
        head_part[...] = jnp.zeros_like(head_part)

    nqkv = nq + 2 * nk
    wqkv = matrices.at[:, :nqkv]
    wo = matrices.at[:, nqkv:]
    load_o = pltpu.make_async_copy(weights.at[:, nqkv : nqkv + nq], wo, matrix_sems.at[0])
    load_qkv = pltpu.make_async_copy(weights.at[:, :nqkv], wqkv, matrix_sems.at[1])
    load_att = pltpu.make_async_copy(att_out, att, matrix_sems.at[2])
    load_first = pltpu.make_async_copy(first, first_all, matrix_sems.at[3])
    loads = []
    for pieces, target, sem in ((branch, rows_all, row_sems.at[0]), (tokens, xs_all, row_sems.at[1])):
        for k, piece in enumerate(pieces):
            at = pl.ds(pl.multiple_of(place[4 + k] * ROWS, ROWS), ROWS)
            loads.append(pltpu.make_async_copy(piece, target.at[at, :], sem.at[k]))

    @pl.when(step_id == 0)
    def _():
        for copy in [load_o, *loads[:4], load_att, load_qkv, *loads[4:], load_first]:
            copy.start()
        for copy in [load_o, *loads[:4], load_att]:
            copy.wait()

    here = pl.ds(pl.multiple_of(i * 2 * ROWS, 2 * ROWS), 2 * ROWS)
    grad_att[...] = matmul(rows_all[here, :], wo[...]).astype(bf16)
    mask_k = lax.broadcasted_iota(jnp.int32, (ROWS, GROUP * ROWS), 0)
    mask_q = lax.broadcasted_iota(jnp.int32, (ROWS, GROUP * ROWS), 1) % ROWS

    def attend_back(block):
        half = block % 2 * ROWS
        n = block * ROWS
        end = n + ROWS
        for h in range(nk // HD):
            cols = [(h * GROUP + a) * HD for a in range(GROUP)]
            q2 = jnp.concatenate([low[n:end, col : col + HD] for col in cols], axis=0)
            g2 = jnp.concatenate([grad_att[half : half + ROWS, col : col + HD] for col in cols], axis=0)
            o2 = jnp.concatenate([att[n:end, col : col + HD] for col in cols], axis=0)
            total = totals[block % 2, h : h + 1, :]
            dot = jnp.sum((g2.astype(f32) * o2.astype(f32)).T, axis=0, keepdims=True)
            k = low[:end, nq + h * HD : nq + (h + 1) * HD]
            v = low[:end, nq + nk + h * HD : nq + nk + (h + 1) * HD]
            probs = jnp.exp2(matmul_t(k, q2) * log2_scale - total)
            last = jnp.where(mask_k <= mask_q, probs[n:], 0.0)
            probs = jnp.concatenate([probs[:n], last], axis=0) if n else last
            grad_scores = (probs * (matmul_t(v, g2) - dot)).astype(bf16)
            dv_part = matmul(probs.astype(bf16), g2)
            dk_part = matmul(grad_scores, q2)
            if end == keys:
                dv[h] = dv_part
                dk[h] = dk_part
            else:
                dv[h, :end, :] += dv_part
                dk[h, :end, :] += dk_part
            d = t_matmul(k, grad_scores).T * score_scale
            for a, col in enumerate(cols):
                dq[half : half + ROWS, col : col + HD] = d[a * ROWS : (a + 1) * ROWS]

    keys = low.shape[0]
    for k in range(keys // (2 * ROWS)):

        @pl.when(i == k)
        def _(k=k):
            attend_back(2 * k + 1)
            attend_back(2 * k)

    c, s = cos[...], sin[...]

    def unturned(w):
        return w * c - pltpu.roll(w, HD // 2, 1) * s

    for h in range(nq // HD):
        col = slice(h * HD, (h + 1) * HD)
        grad, gp = norm_back(qraw[:, col], qgain, unturned(dq[:, col]))
        grads_all[here, col] = grad.astype(bf16)
        head_part[:1, :] += gp
    for h in range(nk // HD):
        col = slice(h * HD, (h + 1) * HD)
        grad, gp = norm_back(kraw[:, col], kgain, unturned(dk[h, here, :] * score_scale))
        grads_all[here, nq + h * HD : nq + (h + 1) * HD] = grad.astype(bf16)
        head_part[1:2, :] += gp
        grads_all[here, nq + nk + h * HD : nq + nk + (h + 1) * HD] = dv[h, here, :].astype(bf16)
    @pl.when(step_id == 0)
    def _():
        for copy in [load_qkv, *loads[4:]]:
            copy.wait()

    upstream = matmul_t(grads_all[here, :], wqkv[...])
    put_pair(place[2 * i], upstream.astype(bf16), mine, other)
    x = xs_all[here, :].astype(f32)
    gain_part[:1, :] += jnp.sum(upstream * x * inverse_rms(x), axis=0, keepdims=True)

    @pl.when(step_id == pl.num_programs(0) - 1)
    def _():
        load_first.wait()
        more = nqkv + nq
        rows = 2 * ROWS
        stored = []
        for k in range(first_all.shape[1] // rows):
            at = slice(k * rows, (k + 1) * rows)
            block[at, :nqkv] = t_matmul(first_all[:, at], grads_all[...]).astype(bf16)
            block[at, nqkv:more] = t_matmul(rows_all[:, at], att[...]).astype(bf16)
            same = equal_iota(rows, rows, lambda r, c: r == c)
            stands = of_head(rows, per_device, k * rows)
            lane = lax.broadcasted_iota(jnp.int32, (rows, HD), 1)
            columns = jnp.zeros((rows, HD), f32)
            values = [
                (same, gain_part[:1, at]),
                (same, second_gain[:1, at]),
                (stands, head_part[:1, :]),
                (stands, head_part[1:2, :]),
            ]
            for m, (mask, line) in enumerate(values):
                column = jnp.sum(jnp.where(mask, line, 0.0), axis=1, keepdims=True)
                columns = jnp.where(lane == m, column, columns)
            block[at, more:] = columns.astype(bf16)
            stored.append(pltpu.make_async_copy(block.at[at, :], out.at[at, :], out_sems.at[k]))
            stored[-1].start()
        for copy in stored:
            copy.wait()


def backward_attention(
    place, branch, tokens, weights, first, low, att, totals, qraw, kraw, cos, sin, head_gains, second_gain
):
    n, width = 4, branch[0].shape[1]
    length, nqkv = low.shape
    nq, nk = qraw.shape[1], kraw.shape[1]
    total = nqkv + nq + HD
    row = lambda cols: pl.BlockSpec((2 * ROWS, cols), lambda i, p: (n // 2 - 1 - i, 0))
    half = pl.BlockSpec((1, ROWS, width), lambda i, p: (p[n - 2 - 2 * i] % 2, 0, 0))
    return pl.pallas_call(
        functools.partial(backward_attention_kernel, width // lax.axis_size(FSDP)),
        grid_spec=pltpu.PrefetchScalarGridSpec(
            num_scalar_prefetch=1,
            grid=(n // 2,),
            in_specs=[
                *[pl.BlockSpec(memory_space=pl.ANY)] * 11,
                whole((length, nqkv)),
                pl.BlockSpec((2, 8, GROUP * ROWS), lambda i, p: (n // 2 - 1 - i, 0, 0)),
                row(nq),
                row(nk),
                row(HD),
                row(HD),
                whole((8, HD)),
                whole((8, width)),
            ],
            out_specs=[half, half, pl.BlockSpec(memory_space=pltpu.HBM)],
            scratch_shapes=[
                pltpu.VMEM((width, nqkv + nq), bf16),
                pltpu.VMEM((length, width), bf16),
                pltpu.VMEM((length, width), bf16),
                pltpu.VMEM((length, width), bf16),
                pltpu.VMEM((length, nq), bf16),
                pltpu.VMEM((length, nqkv), bf16),
                pltpu.VMEM((width, total), bf16),
                pltpu.VMEM((2 * ROWS, nq), bf16),
                pltpu.VMEM((nk // HD, length, HD), f32),
                pltpu.VMEM((nk // HD, length, HD), f32),
                pltpu.VMEM((2 * ROWS, nq), f32),
                pltpu.VMEM((8, width), f32),
                pltpu.VMEM((8, HD), f32),
                pltpu.SemaphoreType.DMA((2, 4)),
                pltpu.SemaphoreType.DMA((4,)),
                pltpu.SemaphoreType.DMA((width // (2 * ROWS),)),
            ],
        ),
        out_shape=[
            pltpu.HBM((2, ROWS, width), bf16),
            pltpu.HBM((2, ROWS, width), bf16),
            pltpu.HBM((width, total), bf16),
        ],
        compiler_params=params(46),
        cost_estimate=cost(6e11, 18e6, 3e6),
        name="backward_attention",
    )(
        place, *branch, *map(far, tokens), far(weights), far(first), far(att), far(low), far(totals),
        far(qraw), far(kraw), far(cos), far(sin), far(head_gains), far(second_gain),
    )


def tokens_back_kernel(tokens, mine, from_core, from_z, grad_middle, gain, grad_tokens):
    u = mine[...].astype(f32) + from_core[...].astype(f32) + from_z[...].astype(f32)
    grad, _ = norm_back(tokens[...].astype(f32), gain[:1, :], u)
    grad_tokens[...] = grad_middle[...] + grad


def tokens_back(tokens, mine, from_core, from_z, grad_middle, gain):
    width = tokens.shape[1]
    half = ROWS // 2
    row = pl.BlockSpec((half, width), lambda i: (i, 0))
    first = pl.BlockSpec((None, half, width), lambda i: (0, i, 0))
    return pl.pallas_call(
        tokens_back_kernel,
        grid=(2,),
        in_specs=[row, first, first, row, row, whole((8, width))],
        out_specs=row,
        out_shape=pltpu.HBM((ROWS, width), f32),
        compiler_params=params(14),
        cost_estimate=cost(4e6, 4e6),
        name="tokens_back",
    )(far(tokens), mine, from_core, from_z, far(grad_middle), far(gain))


def close(zh, parts):
    senders, both, wide = parts.shape
    rows = both // 2

    def kernel(zh, parts, keep, give):
        for which, out in ((zh[0], keep), (1 - zh[0], give)):
            at = pl.ds(pl.multiple_of(which * rows, rows), rows)
            added = parts[0, at, :].astype(f32)
            for k in range(1, senders):
                added = added + parts[k, at, :].astype(f32)
            out[...] = added.astype(out.dtype)

    return pl.pallas_call(
        kernel,
        grid_spec=pltpu.PrefetchScalarGridSpec(
            num_scalar_prefetch=1,
            grid=(1,),
            in_specs=[whole(parts.shape)],
            out_specs=[whole_out((rows, wide))] * 2,
        ),
        out_shape=[
            jax.ShapeDtypeStruct((rows, wide), f32),
            jax.ShapeDtypeStruct((rows, wide), bf16),
        ],
        compiler_params=params(14),
        cost_estimate=cost(2e6, 4e6),
        name="close",
    )(zh, far(parts) if senders == 1 else parts)


def finish(keep, arrived, widths):
    rows = keep.shape[0]

    def kernel(keep, arrived, *outs):
        at = 0
        for out in outs:
            some = slice(at, at + out.shape[1])
            out[...] = keep[:, some] + arrived[:, some].astype(f32)
            at += out.shape[1]

    return pl.pallas_call(
        kernel,
        out_shape=[jax.ShapeDtypeStruct((rows, w), f32) for w in widths],
        compiler_params=params(8),
        cost_estimate=cost(1e5, 1e6),
        name="finish",
    )(keep, arrived)


def finish_gains(parts, rows, heads):
    def kernel(*refs):
        total = refs[0][...] + refs[1][...] + refs[2][...] + refs[3][...]
        same = equal_iota(rows, rows, lambda r, c: r == c)
        for k, out in enumerate(refs[4:]):
            line = jnp.sum(jnp.where(same, total[:, k : k + 1], 0.0), axis=0, keepdims=True)
            out[...] = line[:, : out.shape[1]]

    widths = (rows, rows, heads, heads)
    outs = pl.pallas_call(
        kernel,
        out_shape=[jax.ShapeDtypeStruct((1, w), f32) for w in widths],
        compiler_params=params(4),
        cost_estimate=cost(1e4, 1e5),
        name="finish_gains",
    )(*parts)
    return [out.reshape(-1) for out in outs]


def pack(first, second, gains, rows, heads):
    widths = [a.shape[1] for a in first], [a.shape[1] for a in second]
    split = sum(widths[0])

    def kernel(gains, *refs):
        out = refs[-1]
        at = 0
        for k, ref in enumerate(refs[:-1]):
            at += HD * (k == len(first))
            out[:, at : at + ref.shape[1]] = ref[...]
            at += ref.shape[1]
        g = gains[...].astype(f32)
        lane = lax.broadcasted_iota(jnp.int32, (rows, HD), 1)
        line = lax.broadcasted_iota(jnp.int32, (rows, HD), 0)
        columns = jnp.zeros((rows, HD), f32)
        places = [(0, rows), (rows, rows), (2 * rows, heads), (2 * rows + heads, heads)]
        for k, (start, count) in enumerate(places):
            mask = (lane == line + start) & (line < count)
            column = jnp.sum(jnp.where(mask, g, 0.0), axis=1, keepdims=True)
            columns = jnp.where(lane == k, column, columns)
        out[:, split : split + HD] = columns.astype(bf16)

    return pl.pallas_call(
        kernel,
        out_shape=jax.ShapeDtypeStruct((rows, split + HD + sum(widths[1])), bf16),
        compiler_params=params(8),
        cost_estimate=cost(1e3, 5e5),
        name="pack",
    )(gains, *map(far, first), *map(far, second))


def pair(zh, shard, other, cut, split):
    rows, wide = shard.shape

    def kernel(zh, shard, other, left, right, rest):
        for k, ref in enumerate((shard, other)):
            left[k] = ref[:, :cut]
            right[k] = ref[:, cut:split]
            rest[pl.ds(pl.multiple_of((zh[0] ^ k) * rows, rows), rows), :] = ref[:, split:]

    shapes = [(2, rows, cut), (2, rows, split - cut), (2 * rows, wide - split)]
    return pl.pallas_call(
        kernel,
        grid_spec=pltpu.PrefetchScalarGridSpec(
            num_scalar_prefetch=1,
            grid=(1,),
            in_specs=[whole((rows, wide))] * 2,
            out_specs=[whole_out(s) for s in shapes],
        ),
        out_shape=[
            *[jax.ShapeDtypeStruct(s, bf16) for s in shapes[:2]],
            pltpu.HBM(shapes[2], bf16),
        ],
        compiler_params=params(8),
        cost_estimate=cost(1e3, 1e6),
        name="pair",
    )(zh, shard, other)


def load_pieces(order, pieces, target, semaphores):
    copies = []
    half = len(pieces) // 2
    cut = pieces[0].shape[3]
    for side in range(2):
        n = 0
        for piece in pieces[side * half : (side + 1) * half]:
            rows, wide = piece.shape[2:]
            for j in range(piece.shape[0]):
                for k in range(2):
                    place = pl.multiple_of(order[side, n] * rows, rows)
                    copy = pltpu.make_async_copy(
                        piece.at[j, k],
                        target.at[pl.ds(place, rows), side * cut : side * cut + wide],
                        semaphores.at[side, n],
                    )
                    copies.append(copy)
                    n += 1
    return copies


def swapped(value, axis):
    return lax.ppermute(value, axis, [(0, 1), (1, 0)])


def tp_gather(own, over_z=None):
    over_z = swapped(own, "zl") if over_z is None else over_z
    return [own, over_z, swapped(own, "core"), swapped(over_z, "core")]


def tp_scatter(mine, other):
    from_core = swapped(other, "core")
    passed = (mine[1].astype(f32) + from_core[1].astype(f32)).astype(bf16)
    return mine, from_core, swapped(passed, "zl"), passed


def after(value, *others):
    return lax.optimization_barrier((value, *others))[0]


def sent_rows(part):
    planes = lax.axis_size(PLANE)
    blocks = part.reshape(planes, part.shape[0] // planes, part.shape[1])
    return lax.all_to_all(blocks, PLANE, 0, 0, tiled=True)


def by_distance(sides, staged):
    done = [{0: own} for own, _ in sides]
    before = []
    for near in (True, False):
        arrived = []
        for kept, (own, axis) in zip(done, sides):
            n = lax.axis_size(axis)
            for j in range(1, n):
                if (j in (1, n - 1)) == near:
                    perm = [(s, (s - j) % n) for s in range(n)]
                    kept[j] = lax.ppermute(after(own, *before) if before else own, axis, perm)
                    arrived.append(kept[j])
        before = arrived if staged else []
    return [[kept[j] for j in sorted(kept)] for kept in done]


def gathered_order():
    nx, ny = lax.axis_size("x"), lax.axis_size("y")
    x, y = (lax.axis_index("x") + jnp.arange(nx)) % nx, (lax.axis_index("y") + jnp.arange(ny)) % ny
    z = lax.axis_index("zh") ^ jnp.arange(2)
    block = lambda x, y: ((x * ny + y) * 2 + z).reshape(-1)
    left = block(x[None, :, None], y[:, None, None])
    right = block(x[:, None, None], y[None, :, None])
    return jnp.stack([left, right]).astype(jnp.int32)


def rotary_tables(length):
    midway = HD // 2
    frequency = 1.0 / rope_base ** (np.arange(midway) * 2.0 / HD)
    angles = np.arange(length)[:, None] * frequency[None, :]
    cos, sin = np.cos(angles), np.sin(angles)
    tables = np.concatenate([cos, cos], axis=1), np.concatenate([-sin, sin], axis=1)
    return [jnp.asarray(t.astype(np.float32)) for t in tables]


def local(
    tokens,
    attention_gain,
    query_weight,
    key_weight,
    value_weight,
    query_gain,
    key_gain,
    output_weight,
    feed_gain,
    gate_weight,
    up_weight,
    down_weight,
    cotangent,
):
    width = tokens.shape[2]
    nq, nk = query_weight.shape[1], key_weight.shape[1]
    units = gate_weight.shape[1]
    rows = query_weight.shape[0]
    x = tokens[0]
    dy = cotangent[0]
    zl, core = lax.axis_index("zl"), lax.axis_index("core")
    block = jnp.arange(4, dtype=jnp.int32)
    place = ((block % 2) ^ core) * 2 + ((block // 2) ^ zl)
    block_of = ((block // 2) ^ core) + ((block % 2) ^ zl) * 2
    place = jnp.concatenate([place, block_of]).astype(jnp.int32)
    cos, sin = rotary_tables(4 * ROWS)

    heads = query_gain.shape[0]
    gains = jnp.concatenate([attention_gain, feed_gain, query_gain, key_gain])
    gains = jnp.pad(gains, (0, HD - gains.shape[0]))[None]
    shard = pack(
        [query_weight, key_weight, value_weight, output_weight],
        [gate_weight, up_weight, down_weight],
        gains,
        rows,
        heads,
    )
    over_zh = swapped(shard, "zh")
    split = nq + 2 * nk + nq + HD
    left, right, feed = pair(lax.axis_index("zh").reshape(1), shard, over_zh, nq + nk, split)
    order = gathered_order()
    left, right = by_distance([(left, "x"), (right, "y")], False)
    token_blocks = tp_gather(after(x, over_zh))
    left, right = by_distance([(jnp.stack(left), "y"), (jnp.stack(right), "x")], True)
    feed = lax.all_gather(after(feed, left[1], left[-1], right[1], right[-1]), PLANE, axis=0, tiled=True)
    grads_over_z = swapped(after(dy, *left, *right), "zl")

    first, qraw, kraw, low, att, totals, mine, other, gains, head_gains, weights = forward_attention(
        place, order, token_blocks, left + right, nq, nk, cos, sin
    )
    grad_blocks = tp_gather(dy, after(grads_over_z, other))
    other = after(other, grads_over_z)
    mine, from_core, from_z, _ = tp_scatter(mine, other)
    middle, second = middle_step(x, mine, from_core, from_z, gains)
    over_z = swapped(second, "zl")
    near = feed_step([second, swapped(second, "core")], grad_blocks[::2], feed, units)
    second_blocks = tp_gather(second, after(over_z, near[1]))
    far_ones = feed_step(second_blocks[1::2], grad_blocks[1::2], feed, units)
    hidden, grad_units = [near[0], far_ones[0]], [near[1], far_ones[1]]
    from_core = swapped(near[3], "core")
    passed = (after(far_ones[2], from_core).astype(f32) + swapped(far_ones[3], "core").astype(f32)).astype(bf16)
    from_z = swapped(passed, "zl")
    grad_units[0] = after(grad_units[0], passed)
    feed_grads = feed_weights(second_blocks, grad_blocks, grad_units, hidden)
    from_z = after(from_z, feed_grads)
    grad_middle, branch, feed_gain_part = middle_back(middle, near[2], from_core, from_z, dy, gains)
    feed_sums = lax.psum_scatter(feed_grads, "x", scatter_dimension=0, tiled=True)
    feed_sums = lax.psum_scatter(feed_sums, "y", scatter_dimension=0, tiled=True)
    over_z = swapped(branch, "zl")
    mine, other = feed_out([after(hidden[0], branch), hidden[1]], feed)
    branch_blocks = tp_gather(branch, after(over_z, other))
    mine, from_core, from_z, _ = tp_scatter(mine, other)
    output = middle + mine[0].astype(f32) + from_core[0].astype(f32) + from_z.astype(f32)
    output = output.astype(bf16)

    mine, other, projection_grads = backward_attention(
        place, branch_blocks, token_blocks, weights, first, low, att, totals, qraw, kraw, cos, sin,
        head_gains, feed_gain_part,
    )
    mine, from_core, from_z, _ = tp_scatter(mine, other)
    tokens_grad = tokens_back(
        x, mine, from_core, after(from_z, projection_grads), grad_middle, gains
    )
    parts = after(sent_rows(projection_grads), tokens_grad, output)
    zh = lax.axis_index("zh").reshape(1)
    keep, give = close(zh, parts)
    arrived = swapped(give, "zh")
    query, key, value, out, columns = finish(keep, arrived, (nq, nk, nk, nq, HD))
    feed_keep, feed_give = close(zh, after(feed_sums, columns)[None])
    gate, up, down = finish(feed_keep, swapped(feed_give, "zh"), (units, units, units))
    both = ("zl", "core")
    across = lax.ppermute(columns, both, [(s, 3 - s) for s in range(4)])
    parts = (columns, swapped(columns, "zl"), swapped(columns, "core"), across)
    first_sum, second_sum, query_sum, key_sum = finish_gains(parts, rows, heads)

    return (
        output[None],
        tokens_grad[None],
        first_sum,
        query,
        key,
        value,
        query_sum,
        key_sum,
        out,
        second_sum,
        gate,
        up,
        down,
    )


def solution(mesh):
    fsdp, tp = mesh.devices.shape
    cut = {32: (4, 4, 2), 2: (1, 1, 2), 1: (1, 1, 1)}[fsdp]
    fine = Mesh(mesh.devices.reshape(*cut, 2, tp // 2), EVERY)
    split = ("zl", "core")
    data = P(FSDP, split, None)
    matrix = P(FSDP, split)
    vector = P(FSDP)
    return jax.shard_map(
        local,
        mesh=fine,
        in_specs=(
            data, vector, matrix, matrix, matrix, vector, vector,
            matrix, vector, matrix, matrix, matrix, data,
        ),
        out_specs=(
            data, data, vector, matrix, matrix, matrix, vector, vector,
            matrix, vector, matrix, matrix, matrix,
        ),
        check_vma=False,
    )
```
